32 devices in a mesh: section: 4 (over y, x), dp: 8 (over z, core).
Axes of the slice: x: 2, y: 2, z: 4, core: 2. Of those that a mesh axis runs over, the one named last changes fastest.
Arguments:
- history: bfloat16 [12288, 3600], P('dp'), may hold values from -6 to 6
- targets: bfloat16 [12288, 720], P('dp'), may hold values from -6 to 6
- horizon: int32 [12288], P('dp'), may hold values from 96 to 720, as said below
- residual_cotangent: bfloat16 [12288, 3600], P('dp'), may hold values from -6 to 6
- coarse_entry: float32 [450, 512], P(None, 'dp'), may hold values from -0.25 to 0.25
- coarse_entry_bias: float32 [512], P('dp'), may hold values from -3 to 3
- coarse_middle: float32 [512, 512], P('dp'), may hold values from -0.25 to 0.25
- coarse_middle_bias: float32 [512], P('dp'), may hold values from -3 to 3
- coarse_upper: float32 [512, 512], P('dp'), may hold values from -0.25 to 0.25
- coarse_upper_bias: float32 [512], P('dp'), may hold values from -3 to 3
- coarse_head: float32 [512, 180], P('dp'), may hold values from -0.25 to 0.25
- coarse_head_bias: float32 [180], replicated, may hold values from -3 to 3
- fine_entry: float32 [3600, 512], P(None, 'dp'), may hold values from -0.09375 to 0.09375
- fine_entry_bias: float32 [512], P('dp'), may hold values from -3 to 3
- fine_middle: float32 [512, 512], P('dp'), may hold values from -0.25 to 0.25
- fine_middle_bias: float32 [512], P('dp'), may hold values from -3 to 3
- fine_upper: float32 [512, 512], P('dp'), may hold values from -0.25 to 0.25
- fine_upper_bias: float32 [512], P('dp'), may hold values from -3 to 3
- fine_head: float32 [512, 4320], P('dp'), may hold values from -0.25 to 0.25
- fine_head_bias: float32 [4320], replicated, may hold values from -3 to 3
Outputs:
- summed_prediction: float32 [12288, 720], P('dp')
- residual: bfloat16 [12288, 3600], P('dp')
- history_grad: bfloat16 [12288, 3600], P('dp')
- coarse_entry_grad: float32 [450, 512], P(None, 'dp')
- coarse_entry_bias_grad: float32 [512], P('dp')
- coarse_middle_grad: float32 [512, 512], P('dp')
- coarse_middle_bias_grad: float32 [512], P('dp')
- coarse_upper_grad: float32 [512, 512], P('dp')
- coarse_upper_bias_grad: float32 [512], P('dp')
- coarse_head_grad: float32 [512, 180], P('dp')
- coarse_head_bias_grad: float32 [180], replicated
- fine_entry_grad: float32 [3600, 512], P(None, 'dp')
- fine_entry_bias_grad: float32 [512], P('dp')
- fine_middle_grad: float32 [512, 512], P('dp')
- fine_middle_bias_grad: float32 [512], P('dp')
- fine_upper_grad: float32 [512, 512], P('dp')
- fine_upper_bias_grad: float32 [512], P('dp')
- fine_head_grad: float32 [512, 4320], P('dp')
- fine_head_bias_grad: float32 [4320], replicated
The draws below stay inside these ranges and needn't reach their ends.
Inputs may be any that keep to these rules, and one draw needn't show every extreme that they name: Each window's horizon is one of 96, 336 and 720.
All inputs are finite; a program needn't handle non-finite values.
Results may differ from the reference program's by a relative error of at most 0.0093.
Values may be sent and summed in bfloat16 or wider, within the bound.
A program may use at most 320 MiB of HBM per device.

```python
import jax
import jax.numpy as jnp
from jax import lax

HISTORY_SPAN = 3600
HORIZON_STEPS = 720
WID = 512
KERNEL_EXTENT = 8
DETAIL_SHARE = 24
MICRO = 6
MB_ROWS = 128
PIN = 450
OUT1 = 180
OUT2 = 4320
SAMPLE_COUNT = 12288


def draw_horizon(key, part):
    key = jax.random.fold_in(key, 11)
    chosen = jax.random.randint(key, (SAMPLE_COUNT,), 0, 3)
    return jnp.where(chosen == 0, HORIZON_STEPS * 2 // 15, jnp.where(chosen == 1, HORIZON_STEPS * 7 // 15, HORIZON_STEPS)).astype(jnp.int32)


def block_scale(stream_key, dims, shards, low, high):
    factor_of, own = 1.0, jax.random.fold_in(stream_key, 6)
    for axis_at, parts in shards:
        draws = jnp.exp(jax.random.uniform(jax.random.fold_in(own, axis_at), (parts,), jnp.float32, low / len(shards), high / len(shards)))
        factor_of = factor_of * jnp.repeat(draws, dims[axis_at] // parts).reshape([-1 if axis == axis_at else 1 for axis in range(len(dims))])
    return factor_of


def bell_draw(stream_key, dims, scale, most, cuts=(), kind=jnp.bfloat16):
    drawn = scale * jax.random.normal(stream_key, dims, jnp.float32)
    if cuts:
        drawn = drawn * block_scale(stream_key, dims, cuts, -0.22, 0.18)
    return jnp.clip(drawn, -most, most).astype(kind)


def setup_inputs(seed: int = 0) -> dict:
    splits = jax.random.split(jax.random.key(seed), 21)
    history = bell_draw(splits[0], (SAMPLE_COUNT, HISTORY_SPAN), 1.0, 6.0, ((0, 8),))
    targets = bell_draw(splits[1], (SAMPLE_COUNT, HORIZON_STEPS), 1.0, 6.0, ((0, 8),))
    horizon = draw_horizon(jax.random.fold_in(splits[20], 71), 0)
    residual_cotangent = bell_draw(splits[3], (SAMPLE_COUNT, HISTORY_SPAN), 1.0, 6.0, ((0, 8),))
    coarse_entry = bell_draw(splits[4], (PIN, WID), PIN ** -0.5, 0.25, ((1, 8),), jnp.float32)
    coarse_entry_bias = bell_draw(splits[5], (WID,), 0.5, 3.0, ((0, 8),), jnp.float32)
    coarse_middle = bell_draw(splits[6], (WID, WID), WID ** -0.5, 0.25, ((0, 8),), jnp.float32)
    coarse_middle_bias = bell_draw(splits[7], (WID,), 0.5, 3.0, ((0, 8),), jnp.float32)
    coarse_upper = bell_draw(splits[8], (WID, WID), WID ** -0.5, 0.25, ((0, 8),), jnp.float32)
    coarse_upper_bias = bell_draw(splits[9], (WID,), 0.5, 3.0, ((0, 8),), jnp.float32)
    coarse_head = bell_draw(splits[10], (WID, OUT1), WID ** -0.5, 0.25, ((0, 8),), jnp.float32)
    coarse_head_bias = bell_draw(splits[11], (OUT1,), 0.5, 3.0, (), jnp.float32)
    fine_entry = bell_draw(splits[12], (HISTORY_SPAN, WID), HISTORY_SPAN ** -0.5, 0.09375, ((1, 8),), jnp.float32)
    fine_entry_bias = bell_draw(splits[13], (WID,), 0.5, 3.0, ((0, 8),), jnp.float32)
    fine_middle = bell_draw(splits[14], (WID, WID), WID ** -0.5, 0.25, ((0, 8),), jnp.float32)
    fine_middle_bias = bell_draw(splits[15], (WID,), 0.5, 3.0, ((0, 8),), jnp.float32)
    fine_upper = bell_draw(splits[16], (WID, WID), WID ** -0.5, 0.25, ((0, 8),), jnp.float32)
    fine_upper_bias = bell_draw(splits[17], (WID,), 0.5, 3.0, ((0, 8),), jnp.float32)
    fine_head = bell_draw(splits[18], (WID, OUT2), WID ** -0.5, 0.25, ((0, 8),), jnp.float32)
    fine_head_bias = bell_draw(splits[19], (OUT2,), 0.5, 3.0, (), jnp.float32)
    return {"history": history, "targets": targets, "horizon": horizon, "residual_cotangent": residual_cotangent, "coarse_entry": coarse_entry, "coarse_entry_bias": coarse_entry_bias, "coarse_middle": coarse_middle, "coarse_middle_bias": coarse_middle_bias, "coarse_upper": coarse_upper, "coarse_upper_bias": coarse_upper_bias, "coarse_head": coarse_head, "coarse_head_bias": coarse_head_bias, "fine_entry": fine_entry, "fine_entry_bias": fine_entry_bias, "fine_middle": fine_middle, "fine_middle_bias": fine_middle_bias, "fine_upper": fine_upper, "fine_upper_bias": fine_upper_bias, "fine_head": fine_head, "fine_head_bias": fine_head_bias}


@jax.custom_vjp
def downsampled_history(v):
    return lax.optimization_barrier(v.astype(jnp.bfloat16)).astype(jnp.float32)

@jax.custom_vjp
def low_back(v):
    return v

def low_keep(v):
    return (downsampled_history(v), None)

def low_pass(kept, grad):
    return (grad,)

def back_keep(v):
    return (v, None)

def back_low(kept, grad):
    return (downsampled_history(grad),)
downsampled_history.defvjp(low_keep, low_pass)
low_back.defvjp(back_keep, back_low)

def highest(left_side, right_side):
    return jnp.dot(left_side, right_side, precision=lax.Precision.HIGHEST)

def interpolate_knots(theta_values, knot_divisor):
    later_part = jnp.concatenate([theta_values[:, 1:], theta_values[:, -1:]], axis=1)
    fraction = jnp.arange(knot_divisor, dtype=jnp.float32) / knot_divisor
    spread = theta_values[:, :, None] * (1.0 - fraction) + later_part[:, :, None] * fraction
    return spread.reshape(theta_values.shape[0], theta_values.shape[1] * knot_divisor)

def apply_module(module_arguments, weights, pool_size, knot_divisor, history_extent):
    entry_weight, entry_offset, middle_weight, middle_offset, upper_weight, upper_offset, head_weight, head_offset = weights
    pooled = module_arguments
    if pool_size > 1:
        pooled = lax.optimization_barrier(jnp.mean(module_arguments.reshape(module_arguments.shape[0], -1, pool_size), axis=2))
    hidden = downsampled_history(pooled)
    for weight, offset in ((entry_weight, entry_offset), (middle_weight, middle_offset), (upper_weight, upper_offset)):
        hidden = downsampled_history(jax.nn.gelu(low_back(highest(hidden, weight) + offset)))
    theta_values = low_back(highest(hidden, head_weight) + head_offset)
    history_reconstruction = theta_values[:, :history_extent]
    summed_prediction = theta_values[:, history_extent:]
    if knot_divisor > 1:
        history_reconstruction = interpolate_knots(history_reconstruction, knot_divisor)
        summed_prediction = interpolate_knots(summed_prediction, knot_divisor)
    return (module_arguments - history_reconstruction, summed_prediction)

def reference(history, targets, horizon, residual_cotangent, coarse_entry, coarse_entry_bias, coarse_middle, coarse_middle_bias, coarse_upper, coarse_upper_bias, coarse_head, coarse_head_bias, fine_entry, fine_entry_bias, fine_middle, fine_middle_bias, fine_upper, fine_upper_bias, fine_head, fine_head_bias):
    broad_params = (coarse_entry, coarse_entry_bias, coarse_middle, coarse_middle_bias, coarse_upper, coarse_upper_bias, coarse_head, coarse_head_bias)
    detailed_params = (fine_entry, fine_entry_bias, fine_middle, fine_middle_bias, fine_upper, fine_upper_bias, fine_head, fine_head_bias)
    signal_samples = history.astype(jnp.float32)
    target_rows = targets.astype(jnp.float32)
    horizon_mask = (jnp.arange(HORIZON_STEPS, dtype=jnp.int32)[None, :] < horizon[:, None]).astype(jnp.float32)
    group_rows = MICRO * MB_ROWS
    groups = SAMPLE_COUNT // group_rows

    def one_group(history_samples, target_samples, validity_flags, leading_params, trailing_params):
        leading_remainder, leading_prediction = apply_module(history_samples, leading_params, KERNEL_EXTENT, DETAIL_SHARE, HISTORY_SPAN // DETAIL_SHARE)
        trailing_remainder, trailing_prediction = apply_module(leading_remainder, trailing_params, 1, 1, HISTORY_SPAN)
        prediction_error = leading_prediction + trailing_prediction - target_samples
        return (0.5 * jnp.sum(validity_flags * prediction_error * prediction_error), trailing_remainder, leading_prediction, trailing_prediction)
    verified_result = jax.checkpoint(one_group)

    def evaluate_network(series_in, coarse_in, fine_in):
        broad_knots = tuple((downsampled_history(weight) for weight in coarse_in[:7])) + (coarse_in[7],)
        detailed_knots = tuple((downsampled_history(weight) for weight in fine_in[:7])) + (fine_in[7],)
        joined_arrays = (series_in.reshape(groups, group_rows, HISTORY_SPAN), target_rows.reshape(groups, group_rows, HORIZON_STEPS), horizon_mask.reshape(groups, group_rows, HORIZON_STEPS))
        penalty_values, leftover_signal, leading_prediction, trailing_prediction = lax.map(lambda cluster_members: verified_result(cluster_members[0], cluster_members[1], cluster_members[2], broad_knots, detailed_knots), joined_arrays)
        return ((jnp.sum(penalty_values), leftover_signal.reshape(SAMPLE_COUNT, HISTORY_SPAN)), (leading_prediction.reshape(SAMPLE_COUNT, HORIZON_STEPS), trailing_prediction.reshape(SAMPLE_COUNT, HORIZON_STEPS)))
    (overall_penalty, leftover_signal), cotangent_map, (leading_prediction, trailing_prediction) = jax.vjp(evaluate_network, signal_samples, broad_params, detailed_params, has_aux=True)
    signal_derivative, broad_derivative, detailed_derivative = cotangent_map((jnp.ones_like(overall_penalty), residual_cotangent.astype(jnp.float32)))
    summed_prediction = downsampled_history(leading_prediction) + downsampled_history(trailing_prediction)
    return (summed_prediction, leftover_signal.astype(jnp.bfloat16), signal_derivative.astype(jnp.bfloat16), broad_derivative[0], broad_derivative[1], broad_derivative[2], broad_derivative[3], broad_derivative[4], broad_derivative[5], broad_derivative[6], broad_derivative[7], detailed_derivative[0], detailed_derivative[1], detailed_derivative[2], detailed_derivative[3], detailed_derivative[4], detailed_derivative[5], detailed_derivative[6], detailed_derivative[7])
```

```python
import functools

import jax
import jax.numpy as jnp
from jax import lax
from jax.experimental import pallas as pl
from jax.experimental.pallas import tpu as pltpu
from jax.sharding import PartitionSpec as P

POOL = 8
KNOT = 24
LANES = 128
ONES = 16
GELU_A = 0.7978845608028654
GELU_B = GELU_A * 0.044715
F32 = jnp.float32
BF16 = jnp.bfloat16
MIB = 1 << 20


def up(size, unit):
    return -(-size // unit) * unit


class Plan:
    def __init__(self, length, horizon, hidden, pooled, coarse_out, sections, windows):
        self.length, self.horizon, self.hidden = length, horizon, hidden
        self.pooled, self.coarse_out = pooled, coarse_out
        self.fine_out = length + horizon
        self.sections, self.windows = sections, windows
        self.back, self.fore = length // KNOT, horizon // KNOT
        self.wide_in, self.wide_out = up(length + 1, LANES), up(self.fine_out + 1, LANES)
        self.pool_wide, self.theta_wide = up(pooled + 1, LANES), up(coarse_out + 1, LANES)
        widths = [
            ("coarse_entry", self.pool_wide),
            ("coarse_middle", hidden),
            ("coarse_upper", hidden),
            ("coarse_head", self.theta_wide),
            ("bias", LANES),
            ("fine_entry", self.wide_in),
            ("fine_middle", hidden),
            ("fine_upper", hidden),
            ("fine_head", self.wide_out),
        ]
        self.at, place = {}, 0
        for name, width in widths:
            self.at[name] = place
            place += width
        self.columns = place
        self.knots_wide = up(self.back, ONES)
        self.low = length // LANES * LANES
        self.skip = length - self.low
        self.square = hidden // sections
        self.slice_at, self.part, place = {}, {}, 0
        for name, width in (
            ("fine_head", self.wide_out),
            ("fine_entry", self.wide_in),
            ("fine_middle", hidden),
            ("fine_upper", hidden),
            ("coarse_middle", hidden),
            ("coarse_upper", hidden),
            ("coarse_head", self.theta_wide),
            ("coarse_entry", self.pool_wide),
        ):
            self.slice_at[name] = place
            total = width // LANES
            share = -(-total // sections)
            self.part[name] = share, total
            place += share * LANES
        self.slice_columns = place
        self.bias_at, place = {}, 0
        for name in ("fine_head", "coarse_head", "coarse_middle", "coarse_upper", "fine_middle", "fine_upper"):
            self.bias_at[name] = place
            place += self.part[name][0]
        self.bias_rows = up(place, 8)
        self.knot_rows = up(coarse_out, ONES)
        self.pair = 2 * KNOT
        self.r1_pairs = -(-(self.rows("fine_entry") + self.pair - ONES) // self.pair)

    def rows(self, name):
        return self.part[name][0] * LANES

    def start(self, name, section):
        low = min if isinstance(section, int) else jnp.minimum
        share, total = self.part[name]
        return low(section * share, total - share) * LANES


def gelu_both(a):
    square = a * a
    t = jnp.tanh(a * (GELU_A + GELU_B * square))
    half = 0.5 * a
    slope = 0.5 + 0.5 * t + half * (1.0 - t * t) * (GELU_A + (3.0 * GELU_B) * square)
    return half + half * t, slope


def dot(a, b):
    return jnp.dot(a, b, preferred_element_type=F32)


def dot_rows(a, b):
    return lax.dot_general(a, b, (((1,), (1,)), ((), ())), preferred_element_type=F32)


def aligned(start, size, unit):
    return pl.ds(pl.multiple_of(start, unit), size)


def column_of(row_ref, first, count):
    size = row_ref.shape[1]
    columns = []
    for at in range(first, first + count, LANES):
        width = max(0, min(LANES, size - at))
        row = jnp.zeros((1, LANES), F32) if width == 0 else row_ref[:, at : at + width]
        if 0 < width < LANES:
            row = jnp.concatenate([row, jnp.zeros((1, LANES - width), F32)], axis=1)
        columns.append(jnp.broadcast_to(row, (LANES, LANES)).T[:, :1])
    return jnp.concatenate(columns, axis=0)


def hat_weights(first, count, plan, turned=False):
    shape = (plan.knots_wide, count) if turned else (count, plan.theta_wide)
    row = lax.broadcasted_iota(jnp.int32, shape, 1 if turned else 0) + first
    knot = lax.broadcasted_iota(jnp.int32, shape, 0 if turned else 1)
    away = row - KNOT * knot
    weight = jnp.maximum(KNOT - jnp.abs(away), 0)
    weight = jnp.where((knot == plan.back - 1) & (away > 0), KNOT, weight)
    return jnp.where((knot < plan.back) & (row < plan.length), weight, 0).astype(F32).astype(BF16)


def fractions(width):
    later = lax.broadcasted_iota(jnp.int32, (KNOT, width), 0).astype(F32) * (1.0 / KNOT)
    return 1.0 - later, later


NAMES = (
    "coarse_entry",
    "coarse_middle",
    "coarse_upper",
    "coarse_head",
    "fine_entry",
    "fine_middle",
    "fine_upper",
    "fine_head",
)
KEPT = ("fine_entry", "fine_head")


def remote(source, target, send_sem, recv_sem, place):
    return pltpu.make_async_remote_copy(
        src_ref=source,
        dst_ref=target,
        send_sem=send_sem,
        recv_sem=recv_sem,
        device_id=place,
        device_id_type=pl.DeviceIdType.MESH,
    )


def signal(semaphore, places):
    for place in places:
        pl.semaphore_signal(semaphore, inc=1, device_id=place, device_id_type=pl.DeviceIdType.MESH)


class Ways:
    def __init__(self, groups):
        self.section, self.dp = lax.axis_index("section"), lax.axis_index("dp")
        self.group, self.core = self.dp // 2, self.dp % 2
        self.groups = groups
        self.partner = (self.section, self.group * 2 + 1 - self.core)
        s = self.section
        self.side = [s + 1 - 2 * (s % 2), (s + 2) % 4]
        self.sides = [(t, self.dp) for t in self.side]
        self.across = 3 - s

    def far(self, j):
        group = (self.group + j) % self.groups
        return group, (self.section, group * 2 + self.core)

    def from_far(self, j):
        return (self.group + self.groups - j) % self.groups

    def all(self):
        return [self.partner] + self.sides + [self.far(j)[1] for j in range(1, self.groups)]


class Gather:
    def __init__(self, plan, way, per, cuts, w_ref, shards, biases, send, recv, partner_recv):
        self.p, self.way, self.per, self.cuts, self.w_ref = plan, way, per, cuts, w_ref
        self.shards, self.biases = shards, biases
        self.send, self.recv, self.partner_recv = send, recv, partner_recv
        self.near = range(1, way.groups)
        self.chunks, self.ahead = len(cuts) - 1, 3

    def at(self, k, owner, s=None):
        quarter = self.per // 4
        rows = aligned(owner * self.per, self.per, self.per)
        if s is not None:
            rows = aligned(owner * self.per + s * quarter, quarter, quarter)
        return self.w_ref.at[rows, self.cuts[k] : self.cuts[k + 1]]

    def source(self, j):
        return self.way.from_far(j) * 2 + self.way.core

    def copy(self, here, k, j, kind, place):
        return remote(here, here, self.send.at[k, j - 1, kind], self.recv.at[k, j - 1, kind], place)

    def to_far(self, k, j):
        return self.copy(self.at(k, self.way.dp, self.way.section), k, j, 0, self.way.far(j)[1])

    def to_side(self, k, j, i):
        return self.copy(self.at(k, self.source(j), self.way.section), k, j, 1 + i, self.way.sides[i])

    def to_across(self, k, j):
        i = (k + j) % 2
        return self.copy(self.at(k, self.source(j), self.way.side[i]), k, j, 3, self.way.sides[1 - i])

    def to_partner(self, k, j):
        here = self.at(k, self.source(j) if j else self.way.dp)
        return remote(here, here, self.send.at[k, max(j - 1, 0), 4 if j else 5], self.partner_recv.at[k, j], self.way.partner)

    def arrived(self, k, j, kind):
        s = [self.way.section, self.way.side[0], self.way.side[1], self.way.across][kind]
        self.copy(self.at(k, self.source(j), s), k, j, kind, self.way.partner).wait_recv()

    def cast(self, k):
        p, own = self.p, aligned(self.way.dp * self.per, self.per, self.per)
        low, high = self.cuts[k], self.cuts[k + 1]
        for ref, name in zip(self.shards, NAMES):
            at, size = p.at[name], ref.shape[1]
            wide = up(size + 1, LANES) if name.endswith(("entry", "head")) else size
            first, last = max(at, low), min(at + wide, high)
            full = min(last, at + size // LANES * LANES)
            if first < full:
                self.w_ref[own, first:full] = ref[:, first - at : full - at].astype(BF16)
            if first < last and last > full:
                rest = ref[:, full - at : size].astype(BF16)
                pad = jnp.zeros((self.per, last - at - size), BF16)
                self.w_ref[own, full:last] = jnp.concatenate([rest, pad], axis=1)
        at = p.at["bias"]
        if low <= at < high:
            count = len(self.biases)
            rows = jnp.concatenate([ref[...] for ref in self.biases] + [jnp.zeros((8 - count, self.per), F32)], axis=0)
            wide = jnp.concatenate([rows, jnp.zeros((8, LANES - self.per), F32)], axis=1)
            wide = jnp.concatenate([wide, jnp.zeros((LANES - 8, LANES), F32)], axis=0)
            self.w_ref[own, at : at + LANES] = wide.T[: self.per].astype(BF16)

    def first(self, k):
        self.cast(k)
        for j in self.near:
            self.to_far(k, j).start()
        self.to_partner(k, 0).start()

    def second(self, k):
        for j in self.near:
            self.arrived(k, j, 0)
            for i in range(2):
                self.to_side(k, j, i).start()

    def third(self, k):
        for j in self.near:
            self.arrived(k, j, 1)
            self.arrived(k, j, 2)
            self.to_across(k, j).start()

    def fourth(self, k):
        for j in self.near:
            self.arrived(k, j, 3)
            self.to_partner(k, j).start()

    def turn(self, t):
        for depth, stage in enumerate((self.second, self.third, self.fourth)):
            if 0 <= t - depth < self.chunks:
                stage(t - depth)
            if depth == 0 and t + self.ahead < self.chunks:
                self.first(t + self.ahead)

    def complete(self, k):
        for j in range(self.way.groups):
            there = (self.way.from_far(j) * 2 + 1 - self.way.core) if j else self.way.partner[1]
            here = self.at(k, there)
            remote(here, here, self.send.at[k, 0, 5], self.partner_recv.at[k, j], self.way.partner).wait_recv()

    def sent(self):
        for k in range(self.chunks):
            for j in self.near:
                for copy in (self.to_far(k, j), self.to_side(k, j, 0), self.to_side(k, j, 1), self.to_across(k, j)):
                    copy.wait_send()
                self.to_partner(k, j).wait_send()
            self.to_partner(k, 0).wait_send()


class Reduce:
    def __init__(self, plan, way, per, cuts, part_ref, core_in, far_in, far_out, out_ref, send, recv):
        self.p, self.way, self.per, self.cuts = plan, way, per, cuts
        self.part_ref, self.core_in, self.far_in, self.far_out = part_ref, core_in, far_in, far_out
        self.out_ref, self.send, self.recv = out_ref, send, recv
        self.near = range(1, way.groups)
        self.chunks = len(cuts) - 1

    def columns(self, k):
        return slice(self.cuts[k], self.cuts[k + 1])

    def to_partner(self, k, g):
        return remote(
            self.part_ref(g * 2 + 1 - self.way.core, k),
            self.core_in(g, k),
            self.send.at[k, g, 0],
            self.recv.at[k, g, 0],
            self.way.partner,
        )

    def to_far(self, k, j):
        here, there = self.far_out(j - 1, k), self.far_in(j - 1, k)
        return remote(here, there, self.send.at[k, j - 1, 1], self.recv.at[k, j - 1, 1], self.way.far(j)[1])

    def side(self, k, source, i, to):
        here = self.out_ref.at[source, :, self.columns(k)]
        return remote(here, here, self.send.at[k, i, 2], self.recv.at[k, i, 2], to)

    def to_side(self, k, i):
        return self.side(k, self.way.section, i, self.way.sides[i])

    def to_across(self, k):
        i = k % 2
        return self.side(k, self.way.side[i], 2, self.way.sides[1 - i])

    def summed(self, k, group):
        own = self.part_ref(group * 2 + self.way.core, k)[...].astype(F32)
        return own + self.core_in(group, k)[...].astype(F32)

    def first(self, k):
        for g in range(self.way.groups):
            self.to_partner(k, g).start()

    def second(self, k):
        for g in range(self.way.groups):
            self.to_partner(k, g).wait_recv()
        for j in self.near:
            self.far_out(j - 1, k)[...] = self.summed(k, self.way.far(j)[0]).astype(BF16)
            self.to_far(k, j).start()

    def third(self, k):
        total = self.summed(k, self.way.group)
        for j in self.near:
            self.to_far(k, j).wait_recv()
            total += self.far_in(j - 1, k)[...].astype(F32)
        self.out_ref[self.way.section, :, self.columns(k)] = total.astype(BF16)
        for i in range(2):
            self.to_side(k, i).start()

    def fourth(self, k):
        i = k % 2
        for turn in (i, 1 - i):
            self.side(k, self.way.side[turn], turn, self.way.sides[turn]).wait_recv()
            if turn == i:
                self.to_across(k).start()

    def complete(self, k):
        self.side(k, self.way.across, 2, self.way.partner).wait_recv()

    def sent(self, k):
        for g in range(self.way.groups):
            self.to_partner(k, g).wait_send()
        for j in self.near:
            self.to_far(k, j).wait_send()
        for i in range(2):
            self.to_side(k, i).wait_send()
        self.to_across(k).wait_send()


class ReduceBias:
    def __init__(self, way, own_ref, core_in, far_ref, out_ref, send, recv):
        self.way, self.own_ref, self.core_in, self.far_ref, self.out_ref = way, own_ref, core_in, far_ref, out_ref
        self.send, self.recv = send, recv
        self.near = range(1, way.groups)

    def copy(self, here, there, n, place):
        return remote(here, there, self.send.at[n], self.recv.at[n], place)

    def to_partner(self):
        return self.copy(self.own_ref, self.core_in, 0, self.way.partner)

    def to_far(self, j):
        here = self.far_ref.at[self.way.group]
        return self.copy(here, here, j, self.way.far(j)[1])

    def side(self, source, n, to):
        here = self.out_ref.at[source]
        return self.copy(here, here, self.way.groups + n, to)

    def to_across(self):
        return self.side(self.way.side[0], 2, self.way.sides[1])

    def second(self):
        self.to_partner().wait_recv()
        self.far_ref[self.way.group] = self.own_ref[...] + self.core_in[...]
        for j in self.near:
            self.to_far(j).start()

    def third(self):
        for j in self.near:
            here = self.far_ref.at[self.way.from_far(j)]
            self.copy(here, here, j, self.way.partner).wait_recv()
        total = self.far_ref[0]
        for g in range(1, self.way.groups):
            total += self.far_ref[g]
        self.out_ref[self.way.section] = total
        for i in range(2):
            self.side(self.way.section, i, self.way.sides[i]).start()

    def fourth(self):
        self.side(self.way.side[0], 0, self.way.partner).wait_recv()
        self.to_across().start()
        self.side(self.way.side[1], 1, self.way.partner).wait_recv()

    def complete(self):
        self.side(self.way.across, 2, self.way.partner).wait_recv()
        self.to_partner().wait_send()
        for j in self.near:
            self.to_far(j).wait_send()
        for i in range(2):
            self.side(self.way.section, i, self.way.sides[i]).wait_send()
        self.to_across().wait_send()


def core_kernel(plan, per, groups, *refs):
    p = plan
    refs = list(refs)
    take = lambda count: [refs.pop(0) for _ in range(count)]
    history_ref, cotangent_ref, target_ref, horizon_ref, coarse_bias_ref, fine_bias_ref = take(6)
    if groups:
        shards_in = take(14)
    else:
        (packed_ref,) = take(1)
    theta_out, h3_out, gfine_out, pool_out = take(4)
    if groups:
        kept_out, slices_out, bias_out = take(3)
    else:
        slice_out, bias_out = take(2)
    w_ref, big_ref, h_ref, g_ref, r1_ref, pooled_ref, split_ref, theta_ref, gtheta_ref, gknot_ref = take(10)
    pw_ref, pwt_ref, f32_ref, product_ref, bias_ref = take(5)
    fore_bias_ref, horizon_buf, coarse_bias_buf, fine_bias_buf, sems = take(5)
    if groups:
        shards = take(14)
        shard_sems, send, recv, partner_recv = take(4)
        head_bias_ref, bias_in, bias_far, far_first, ready, reduce_send, reduce_recv, bias_send, bias_recv = take(9)
    else:
        head_bias_ref = bias_out
    hid, windows = p.hidden, p.windows
    section = lax.axis_index("section")
    chunk = min(512, windows)
    chunks = windows // chunk
    H = slice(0, hid)
    lanes_of = lambda n: aligned(n * chunk, chunk, chunk)
    place = p.at["fine_entry"]
    head_at = p.at["fine_head"]

    load = lambda source, out, sem: pltpu.make_async_copy(source, out, sems.at[sem])
    history_in = load(history_ref, big_ref.at[: p.length], 1)
    cotangent_in = load(cotangent_ref, big_ref.at[: p.length], 2)
    target_in = load(target_ref, big_ref.at[p.length : p.fine_out], 0)
    rows_in = [
        load(horizon_ref, horizon_buf, 3),
        load(coarse_bias_ref, coarse_bias_buf, 4),
        load(fine_bias_ref, fine_bias_buf, 5),
    ]
    theta_copy = load(theta_ref, theta_out, 6)
    h3_copy = load(h_ref.at[5, H], h3_out, 7)
    gfine_copy = load(g_ref.at[3], gfine_out, 8)
    pool_copy = load(pooled_ref, pool_out, 9)

    if groups:
        shards_load = [
            pltpu.make_async_copy(source, out, shard_sems.at[n]) for n, (source, out) in enumerate(zip(shards_in, shards))
        ]
        order = [0, 1, 2, 3, 8, 9, 10, 11, 12, 13, 4, 5, 6, 7]
        for n in order:
            shards_load[n].start()
        way = Ways(groups)
        middle = p.at["fine_middle"]
        third = (p.columns - middle) // 3 // LANES * LANES
        entry_cut = place + up((middle - place) // 2, LANES)
        cuts = (0, 2 * hid, place, entry_cut, middle, middle + third, middle + 2 * third, p.columns)
        gather = Gather(p, way, per, cuts, w_ref, shards[:8], shards[8:], send, recv, partner_recv)
        history_in.start()
        for copy in rows_in:
            copy.start()
        barrier = pltpu.get_barrier_semaphore()
        signal(barrier, way.all())
        for n in order[:10]:
            shards_load[n].wait()
        pl.semaphore_wait(barrier, len(way.all()))
        gather.first(0)
        for n in order[10:]:
            shards_load[n].wait()
        for k in range(1, gather.ahead):
            gather.first(k)
    else:
        weights_in = load(packed_ref, w_ref, 10)
        weights_in.start()
        history_in.start()
        for copy in rows_in:
            copy.start()

    def turn(t):
        if groups:
            gather.turn(t)

    def complete(*ks):
        if groups:
            for k in ks:
                gather.complete(k)

    tail = p.wide_out - p.length
    mark = lax.broadcasted_iota(jnp.int32, (tail, windows), 0) < POOL
    big_ref[p.length :, :] = mark.astype(F32).astype(BF16)
    pooled_ref[...] = jnp.zeros_like(pooled_ref)
    for index in range(6):
        h_ref[index, hid:, :] = jnp.ones((ONES, windows), BF16)
    for copy in rows_in:
        copy.wait()
    fore_bias_ref[...] = column_of(fine_bias_buf, p.low, p.wide_out - p.low)
    history_in.wait()
    turn(0)

    pool_unit = LANES
    pool_count = p.wide_in // pool_unit

    def pool(i):
        rows = aligned(i * pool_unit, pool_unit, pool_unit)
        for c in range(windows // LANES):
            lanes = slice(c * LANES, (c + 1) * LANES)
            f32_ref[c] = big_ref[rows, lanes].astype(F32)
            total = f32_ref[c, pl.ds(0, pool_unit // POOL, stride=POOL), :]
            for j in range(1, POOL):
                total += f32_ref[c, pl.ds(j, pool_unit // POOL, stride=POOL), :]
            pooled_ref[aligned(i * (pool_unit // POOL), pool_unit // POOL, ONES), lanes] = (total * (1.0 / POOL)).astype(BF16)

    pieces = 4
    for piece in range(pieces):
        pl.loop(pool_count * piece // pieces, pool_count * (piece + 1) // pieces)(pool)
        if piece + 1 < pieces:
            turn(piece + 1)
    complete(0, 1)
    if not groups:
        weights_in.wait()
    bias_ref[...] = w_ref[:, p.at["bias"] : p.at["bias"] + LANES].astype(F32)

    strip = ONES

    def strips():
        for r in range(0, hid, strip):
            rows = slice(r, r + strip)
            yield product_ref[rows, :], rows

    def activate(a, index, lanes):
        product_ref[H, :] = a
        for value, rows in strips():
            h, slope = gelu_both(value + bias_ref[rows, index : index + 1])
            h_ref[index, rows, lanes] = h.astype(BF16)
            g_ref[index, rows, lanes] = slope.astype(BF16)

    def tiles(body):
        @pl.loop(0, chunks)
        def _(n):
            body(lanes_of(n))

    def hidden_layer(name, index):
        at = p.at[name]
        turned = w_ref[:, at : at + hid].T
        tiles(lambda lanes: activate(dot(turned, h_ref[index - 1, H, lanes]), index, lanes))

    at_entry = p.at["coarse_entry"]
    tiles(
        lambda lanes: activate(dot(w_ref[:, at_entry : at_entry + p.pool_wide], pooled_ref[:, lanes]), 0, lanes)
    )
    turn(4)
    hidden_layer("coarse_middle", 1)
    turn(5)
    hidden_layer("coarse_upper", 2)
    at_head = p.at["coarse_head"]
    turned_head = w_ref[:, at_head : at_head + p.theta_wide].T
    theta_bias = column_of(coarse_bias_buf, 0, p.theta_wide)
    used = lax.broadcasted_iota(jnp.int32, (p.theta_wide, chunk), 0) < p.back

    @pl.loop(0, chunks)
    def _(n):
        lanes = lanes_of(n)
        theta = dot(turned_head, h_ref[2, H, lanes]) + theta_bias
        theta_ref[:, lanes] = theta
        knots = jnp.where(used, theta, 0.0)
        high = knots.astype(BF16)
        split_ref[: p.theta_wide, lanes] = high
        split_ref[p.theta_wide :, lanes] = (knots - high.astype(F32)).astype(BF16)

    theta_copy.start()
    turn(6)
    complete(2, 3)

    total = jnp.zeros((hid, p.theta_wide), F32)
    step = 6 * LANES
    for first in range(0, p.wide_in, step):
        count = min(step, p.wide_in - first)
        total += dot(w_ref[:, place + first : place + first + count], hat_weights(first, count, p))
    product = (total * (1.0 / KNOT)).astype(BF16)
    pwt_ref[:, : p.theta_wide] = product
    pwt_ref[:, p.theta_wide :] = product
    pw_ref[...] = product.T

    def fine_entry(lanes):
        a = dot(w_ref[:, place : place + p.wide_in], big_ref[: p.wide_in, lanes])
        activate(a - dot(pwt_ref[...], split_ref[:, lanes]), 3, lanes)

    for n in range(chunks):
        fine_entry(slice(n * chunk, (n + 1) * chunk))
        if n < 2:
            turn(7 + n)
    if chunks < 2:
        turn(8)

    first_pair = p.start("fine_entry", section) // p.pair

    def interpolate(base, count, k, rest, later, lanes):
        own = theta_ref[pl.ds(base + jnp.minimum(k, count - 1), 1), lanes]
        after = theta_ref[pl.ds(base + jnp.minimum(k + 1, count - 1), 1), lanes]
        return own * rest + after * later

    everything = slice(0, windows)
    rest, later = fractions(windows)

    @pl.loop(0, p.r1_pairs)
    def _(i):
        pair = first_pair + i
        source = aligned(pair * p.pair, p.pair, ONES)
        made = jnp.concatenate(
            [interpolate(0, p.back, 2 * pair + j, rest, later, everything) for j in range(2)], axis=0
        )
        made = made * (pair < p.back // 2).astype(F32)
        r1_ref[aligned(i * p.pair, p.pair, ONES), :] = (big_ref[source, :].astype(F32) - made).astype(BF16)

    cotangent_in.start()
    target_in.start()
    big_ref[p.fine_out :, :] = jnp.zeros((p.wide_out - p.fine_out, windows), BF16)
    if groups:
        signal(ready.at[0], way.all())
    complete(4)
    hidden_layer("fine_middle", 4)
    hidden_layer("fine_upper", 5)
    h3_copy.start()
    complete(5, 6)
    if groups:
        kept = [
            load(w_ref.at[:, p.at[name] : p.at[name] + wide], kept_out.at[:, p.at[name] : p.at[name] + wide], 10 + n)
            for n, (name, wide) in enumerate(zip(KEPT, (p.wide_in, p.wide_out)))
        ]
        for copy in kept:
            copy.start()

    rest_c, later_c = fractions(chunk)
    turned_fore = w_ref[:, head_at + p.low : head_at + p.wide_out].T
    target_in.wait()

    @pl.loop(0, chunks)
    def _(n):
        lanes = lanes_of(n)
        before = jnp.zeros((1, chunk), F32)
        product_ref[: p.horizon, :] = dot(turned_fore[p.skip : p.skip + p.horizon], h_ref[5, H, lanes])
        for k in range(0, p.fore, 2):
            here = slice(k * KNOT, (k + 2) * KNOT)
            second = product_ref[here, :] + fore_bias_ref[p.skip + k * KNOT : p.skip + (k + 2) * KNOT, :]
            first = jnp.concatenate(
                [interpolate(p.back, p.fore, k + j, rest_c, later_c, lanes) for j in range(2)], axis=0
            )
            counts = (lax.broadcasted_iota(jnp.int32, (2 * KNOT, chunk), 0) + k * KNOT) < horizon_buf[:, lanes]
            there = slice(p.length + k * KNOT, p.length + (k + 2) * KNOT)
            error = first + second - big_ref[there, lanes].astype(F32)
            gradient = jnp.where(counts, error, 0.0)
            big_ref[there, lanes] = (-gradient).astype(BF16)
            for j in range(2):
                part = gradient[j * KNOT : (j + 1) * KNOT]
                own = jnp.sum(part * rest_c, axis=0, keepdims=True)
                after = jnp.sum(part * later_c, axis=0, keepdims=True)
                last = after if k + j == p.fore - 1 else 0.0
                gtheta_ref[p.back + k + j : p.back + k + j + 1, lanes] = own + before + last
                before = after

    cotangent_in.wait()

    def gradient_slice(name, left, right_ref, first, step=LANES, sign=1.0):
        left_side = left if name.endswith("entry") else h_ref[left]
        for b in range(0, p.rows(name), step):
            width = min(step, p.rows(name) - b)
            value = sign * dot_rows(left_side, right_ref[aligned(first + b, width, ONES), :])
            to = place + p.slice_at[name] + b
            w_ref[:, to : to + width] = value[:hid].astype(BF16)
            if name in p.bias_at:
                for c in range(0, width, LANES):
                    row = p.bias_at[name] + (b + c) // LANES
                    head_bias_ref[row : row + 1, :] = value[hid : hid + 1, c : c + LANES]

    def square_slice(name, index):
        gradient_slice(name, index - 1, g_ref.at[index], p.start(name, section))

    def back_layer(product, index):
        def body(lanes):
            product_ref[H, :] = product(lanes)
            for value, rows in strips():
                g_ref[index, rows, lanes] = (value * g_ref[index, rows, lanes].astype(F32)).astype(BF16)

        tiles(body)

    def times(name, index):
        at = p.at[name]
        return lambda lanes: dot(w_ref[:, at : at + hid], g_ref[index, :, lanes])

    if groups:
        for copy in kept:
            copy.wait()
        gather.sent()
        cuts = (0, p.slice_at["fine_entry"], p.slice_at["coarse_middle"], p.slice_columns)
        width = lambda k: cuts[k + 1] - cuts[k]

        def arrivals(row, k):
            rows = slice(row * per, (row + 1) * per) if isinstance(row, int) else aligned(row * per, per, per)
            if k == 0:
                return split_ref.at[rows, : width(0)]
            first = head_at + cuts[k] - cuts[1]
            return w_ref.at[rows, first : first + width(k)]

        def departures(j, k):
            if k == 0:
                return far_first.at[j * per : (j + 1) * per, :]
            first = (k * groups + j) * per
            return big_ref.at[first : first + per, : width(k)]

        reduce = Reduce(
            p,
            way,
            per,
            cuts,
            lambda owner, k: w_ref.at[aligned(owner * per, per, per), place + cuts[k] : place + cuts[k + 1]],
            arrivals,
            lambda j, k: arrivals(groups + j, k),
            departures,
            slices_out,
            reduce_send,
            reduce_recv,
        )
        reduce_bias = ReduceBias(way, head_bias_ref, bias_in, bias_far, bias_out, bias_send, bias_recv)

    gradient_slice("fine_head", 5, big_ref, p.start("fine_head", section), 3 * LANES, -1.0)
    if groups:
        pl.semaphore_wait(ready.at[0], len(way.all()))
        reduce.first(0)

    back_layer(lambda lanes: -dot(w_ref[:, head_at : head_at + p.wide_out], big_ref[:, lanes]), 5)
    if groups:
        signal(ready.at[1], way.all())
        reduce.second(0)

    for first in range(0, p.wide_in, step):
        count = min(step, p.wide_in - first)
        hats = hat_weights(first, count, p, True)

        @pl.loop(0, chunks)
        def _(n):
            lanes = lanes_of(n)
            part = dot(hats, big_ref[first : first + count, lanes])[: p.back] * (-1.0 / KNOT)
            if first == 0:
                gtheta_ref[: p.back, lanes] = part
            else:
                gtheta_ref[: p.back, lanes] += part

    back_layer(times("fine_upper", 5), 4)
    back_layer(times("fine_middle", 4), 3)
    gfine_copy.start()
    gradient_slice("fine_entry", g_ref[3], r1_ref, p.start("fine_entry", section) - first_pair * p.pair, 2 * LANES)
    square_slice("fine_middle", 4)
    square_slice("fine_upper", 5)
    if groups:
        pl.semaphore_wait(ready.at[1], len(way.all()))
        reduce.first(1)
        reduce.third(0)
    row = lax.broadcasted_iota(jnp.int32, (p.knot_rows, chunk), 0)
    gknot_ref[p.knot_rows :, :] = jnp.zeros((p.theta_wide - p.knot_rows, windows), BF16)

    @pl.loop(0, chunks)
    def _(n):
        lanes = lanes_of(n)
        knots = jnp.where(row < p.coarse_out, gtheta_ref[:, lanes], 0.0)
        gknot_ref[: p.knot_rows, lanes] = (knots - dot(pw_ref[: p.knot_rows, :], g_ref[3, :, lanes])).astype(BF16)

    back_layer(lambda lanes: dot(w_ref[:, at_head : at_head + p.theta_wide], gknot_ref[:, lanes]), 2)
    if groups:
        reduce.second(1)
    back_layer(times("coarse_upper", 2), 1)
    if groups:
        reduce.fourth(0)
    back_layer(times("coarse_middle", 1), 0)
    gradient_slice("coarse_head", 2, gknot_ref, p.start("coarse_head", section))
    gradient_slice("coarse_entry", g_ref[0], pooled_ref, p.start("coarse_entry", section))
    square_slice("coarse_middle", 1)
    square_slice("coarse_upper", 2)
    if groups:
        reduce.first(2)
        reduce_bias.to_partner().start()
        reduce.third(1)
        reduce.second(2)
        reduce_bias.second()

    turned_entry = w_ref[:, at_entry : at_entry + p.pool_wide].T

    def pool_gradient(lanes):
        product_ref[: p.pool_wide, :] = dot(turned_entry, g_ref[0, :, lanes])
        for r in range(0, p.pool_wide, strip):
            pooled_ref[r : r + strip, lanes] = (product_ref[r : r + strip, :] * (1.0 / POOL)).astype(BF16)

    tiles(pool_gradient)
    pool_copy.start()
    if groups:
        reduce.fourth(1)
        reduce_bias.third()
        reduce.third(2)
        reduce_bias.fourth()
        reduce.fourth(2)
        for k in range(reduce.chunks):
            reduce.complete(k)
            reduce.sent(k)
        reduce_bias.complete()
    else:
        out = load(w_ref.at[:, place : place + p.slice_columns], slice_out, 10)
        out.start()
        out.wait()
    theta_copy.wait()
    h3_copy.wait()
    gfine_copy.wait()
    pool_copy.wait()


ANY = pl.BlockSpec(memory_space=pl.ANY)
VMEM = pl.BlockSpec(memory_space=pltpu.VMEM)


def core(plan, per, groups, history, cotangent, targets, horizon, coarse_bias, fine_bias, weights):
    p = plan
    hid, windows = p.hidden, p.windows
    flops = 2 * windows * hid * (2 * p.length + 2 * p.wide_out // 3 + 12 * hid + p.slice_columns)
    out_shape = [
        jax.ShapeDtypeStruct((p.theta_wide, windows), F32),
        jax.ShapeDtypeStruct((hid, windows), BF16),
        jax.ShapeDtypeStruct((hid, windows), BF16),
        jax.ShapeDtypeStruct((p.pool_wide, windows), BF16),
    ]
    out_specs = [ANY] * 4
    scratch = [
        pltpu.VMEM((hid, p.columns), BF16),
        pltpu.VMEM((p.wide_out, windows), BF16),
        pltpu.VMEM((6, hid + ONES, windows), BF16),
        pltpu.VMEM((6, hid, windows), BF16),
        pltpu.VMEM((p.r1_pairs * p.pair, windows), BF16),
        pltpu.VMEM((p.pool_wide, windows), BF16),
        pltpu.VMEM((2 * p.theta_wide, windows), BF16),
        pltpu.VMEM((p.theta_wide, windows), F32),
        pltpu.VMEM((p.knot_rows, windows), F32),
        pltpu.VMEM((p.theta_wide, windows), BF16),
        pltpu.VMEM((p.theta_wide, hid), BF16),
        pltpu.VMEM((hid, 2 * p.theta_wide), BF16),
        pltpu.VMEM((windows // LANES, LANES, LANES), F32),
        pltpu.VMEM((max(hid, p.horizon), min(512, windows)), F32),
        pltpu.VMEM((hid, LANES), F32),
        pltpu.VMEM((p.wide_out - p.low, 1), F32),
        pltpu.VMEM(horizon.shape, jnp.int32),
        pltpu.VMEM(coarse_bias.shape, F32),
        pltpu.VMEM(fine_bias.shape, F32),
        pltpu.SemaphoreType.DMA((13,)),
    ]
    params = {}
    if groups:
        bias = (p.bias_rows, LANES)
        out_shape += [
            jax.ShapeDtypeStruct((hid, p.columns), BF16),
            jax.ShapeDtypeStruct((4, per, p.slice_columns), BF16),
            jax.ShapeDtypeStruct((4,) + bias, F32),
        ]
        out_specs += [ANY, VMEM, VMEM]
        chunks, reduce_chunks = 7, 3
        scratch += [pltpu.VMEM(piece.shape, F32) for piece in weights]
        scratch += [
            pltpu.SemaphoreType.DMA((len(weights),)),
            pltpu.SemaphoreType.DMA((chunks, groups - 1, 6)),
            pltpu.SemaphoreType.DMA((chunks, groups - 1, 4)),
            pltpu.SemaphoreType.DMA((chunks, groups)),
            pltpu.VMEM(bias, F32),
            pltpu.VMEM(bias, F32),
            pltpu.VMEM((groups,) + bias, F32),
            pltpu.VMEM(((groups - 1) * per, p.rows("fine_head")), BF16),
            pltpu.SemaphoreType.REGULAR((2,)),
            pltpu.SemaphoreType.DMA((reduce_chunks, max(groups, 3), 3)),
            pltpu.SemaphoreType.DMA((reduce_chunks, max(groups, 3), 3)),
            pltpu.SemaphoreType.DMA((groups + 3,)),
            pltpu.SemaphoreType.DMA((groups + 3,)),
        ]
        params = {"collective_id": 0, "has_side_effects": True}
    else:
        out_shape += [jax.ShapeDtypeStruct((hid, p.slice_columns), BF16), jax.ShapeDtypeStruct((p.bias_rows, LANES), F32)]
        out_specs += [ANY, VMEM]
    return pl.pallas_call(
        functools.partial(core_kernel, p, per, groups),
        out_shape=tuple(out_shape),
        in_specs=[ANY] * (6 + len(weights)),
        out_specs=tuple(out_specs),
        scratch_shapes=scratch,
        compiler_params=pltpu.CompilerParams(vmem_limit_bytes=63 * MIB, **params),
        cost_estimate=pl.CostEstimate(flops=flops, bytes_accessed=windows * p.length * 4, transcendentals=0),
    )(history, cotangent, targets, horizon, coarse_bias, fine_bias, *weights)


def outputs_kernel(
    plan,
    block,
    steps,
    packed_ref,
    history_ref,
    cotangent_ref,
    theta_ref,
    h3_ref,
    gfine_ref,
    pool_ref,
    fine_bias_ref,
    slices_ref,
    bias_rows_ref,
    residual_ref,
    history_grad_ref,
    prediction_ref,
    *refs,
):
    grads = refs[:16]
    head_ref, entry_ref, side_ref, pool_grad, fore_ref, back_ref, fine_ref, bias_ref, sems = refs[16:]
    p = plan
    step = pl.program_id(0)
    windows = p.windows
    chunk = min(512, p.windows)
    chunks = windows // chunk
    lanes_of = lambda n: aligned(n * chunk, chunk, chunk)
    knots = block // KNOT
    pooled = block // POOL
    rest, later = fractions(chunk)

    def fetch(name, out, at, slot, sem):
        first = aligned(p.at[name] + at * block, block, LANES)
        return pltpu.make_async_copy(packed_ref.at[:, first], out.at[slot], sems.at[sem, slot])

    def interpolate(k, count, base, lanes):
        low = jnp.minimum if not isinstance(k, int) else min
        own = theta_ref[pl.ds(base + low(k, count - 1), 1), lanes]
        after = theta_ref[pl.ds(base + low(k + 1, count - 1), 1), lanes]
        return own * rest + after * later

    fore_out = pltpu.make_async_copy(fore_ref, prediction_ref, sems.at[3, 0])
    wide = p.wide_out - p.low
    first_fore = p.at["fine_head"] + p.low
    side = pltpu.make_async_copy(packed_ref.at[:, first_fore : first_fore + wide], side_ref, sems.at[2, 0])

    @pl.when(step == 0)
    def _():
        fetch("fine_head", head_ref, 0, 0, 0).start()
        fetch("fine_entry", entry_ref, 0, 0, 1).start()
        side.start()
        pool_grad[...] = pool_ref[...].astype(F32)

    @pl.when(step == 2)
    def _():
        side.wait()
        turned_fore = side_ref[...].T
        fore_bias = column_of(fine_bias_ref, p.low, wide)

        @pl.loop(0, chunks)
        def _(n):
            lanes = lanes_of(n)
            back_ref[: p.horizon, :] = dot(turned_fore[p.skip : p.skip + p.horizon], h3_ref[:, lanes])
            for k in range(0, p.fore, 2):
                rows = slice(k * KNOT, (k + 2) * KNOT)
                second = back_ref[rows, :] + fore_bias[p.skip + k * KNOT : p.skip + (k + 2) * KNOT]
                first = jnp.concatenate([interpolate(k + j, p.fore, p.back, lanes) for j in range(2)], axis=0)
                fore_ref[rows, lanes] = first.astype(BF16).astype(F32) + second.astype(BF16).astype(F32)

        fore_out.start()

    @pl.when(step == 1)
    def _():
        unpack(p, slices_ref, bias_rows_ref, grads)

    slot = step % 2

    @pl.when(step + 1 < steps)
    def _():
        fetch("fine_head", head_ref, step + 1, 1 - slot, 0).start()
        fetch("fine_entry", entry_ref, step + 1, 1 - slot, 1).start()

    fetch("fine_head", head_ref, step, slot, 0).wait()
    fetch("fine_entry", entry_ref, step, slot, 1).wait()
    turned_head = head_ref[slot].T
    turned_entry = entry_ref[slot].T
    row = jnp.broadcast_to(fine_bias_ref[:, aligned(step * block, block, LANES)], (8, block))
    bias_ref[...] = row.T[:, :1]
    pair = 2 * KNOT

    @pl.loop(0, chunks)
    def _(n):
        lanes = lanes_of(n)
        back_ref[...] = dot(turned_head, h3_ref[:, lanes])
        fine_ref[...] = dot(turned_entry, gfine_ref[:, lanes])
        for at in range(0, block, pair):
            rows = slice(at, at + pair)
            k = step * knots + at // KNOT
            made = jnp.concatenate([interpolate(k + j, p.back, 0, lanes) for j in range(2)], axis=0)
            back = back_ref[rows, :] + bias_ref[rows, :]
            residual_ref[rows, lanes] = (history_ref[rows, lanes].astype(F32) - made - back).astype(BF16)
        for at in range(0, block, pair):
            rows = slice(at, at + pair)
            first = step * pooled + at // POOL
            spread = jnp.concatenate(
                [jnp.broadcast_to(pool_grad[pl.ds(first + j, 1), lanes], (POOL, chunk)) for j in range(pair // POOL)],
                axis=0,
            )
            history_grad_ref[rows, lanes] = (cotangent_ref[rows, lanes].astype(F32) + fine_ref[rows, :] + spread).astype(BF16)

    @pl.when(step == steps - 1)
    def _():
        fore_out.wait()


def outputs(plan, packed, history, cotangent, theta, h3, gfine, pool, fine_bias, slices, bias_rows):
    p = plan
    hid, windows = p.hidden, p.windows
    block = 6 * LANES
    steps = -(-p.length // block)
    rows = pl.BlockSpec((block, windows), lambda i: (i, 0))
    wide = p.wide_out - p.low
    per = slices.shape[1]
    square, vector = (per, hid), (1, per)
    grads = []
    for entry, out in ((p.pooled, p.coarse_out), (p.length, p.fine_out)):
        grads += [(per, entry), vector, square, vector, square, vector, (per, out), (1, out)]
    return pl.pallas_call(
        functools.partial(outputs_kernel, p, block, steps),
        grid=(steps,),
        out_shape=(
            jax.ShapeDtypeStruct((p.length, windows), BF16),
            jax.ShapeDtypeStruct((p.length, windows), BF16),
            jax.ShapeDtypeStruct((p.horizon, windows), F32),
        )
        + tuple(jax.ShapeDtypeStruct(shape, F32) for shape in grads),
        in_specs=[ANY, rows, rows, VMEM, VMEM, VMEM, VMEM, VMEM, VMEM, VMEM],
        out_specs=(rows, rows, ANY) + (VMEM,) * len(grads),
        scratch_shapes=[
            pltpu.VMEM((2, hid, block), BF16),
            pltpu.VMEM((2, hid, block), BF16),
            pltpu.VMEM((hid, wide), BF16),
            pltpu.VMEM((p.pool_wide, windows), F32),
            pltpu.VMEM((p.horizon, windows), F32),
            pltpu.VMEM((block, min(512, windows)), F32),
            pltpu.VMEM((block, min(512, windows)), F32),
            pltpu.VMEM((block, 1), F32),
            pltpu.SemaphoreType.DMA((4, 2)),
        ],
        compiler_params=pltpu.CompilerParams(vmem_limit_bytes=56 * MIB),
        cost_estimate=pl.CostEstimate(
            flops=2 * windows * hid * (2 * p.length + p.horizon), bytes_accessed=windows * p.length * 8, transcendentals=0
        ),
    )(packed, history, cotangent, theta, h3, gfine, pool, fine_bias, slices, bias_rows)


def pack(plan, arrays, biases):
    p = plan
    names = sorted(p.at, key=p.at.get)
    ends = [p.at[name] for name in names[1:]] + [p.columns]
    columns = []
    for name, end in zip(names, ends):
        piece = arrays[name] if name != "bias" else biases
        columns.append(jnp.pad(piece.astype(BF16), ((0, 0), (0, end - p.at[name] - piece.shape[1]))))
    return jnp.concatenate(columns, axis=1)


def unpack(plan, slices_ref, bias_rows_ref, grads):
    p = plan
    hid = p.hidden

    def joined(name, out, source, row=None):
        size, done = out.shape[1], 0
        for section in range(p.sections):
            first = p.start(name, section)
            last = min(first + p.rows(name), size)
            if row is not None:
                for at in range(done, last, LANES):
                    width = min(LANES, last - at)
                    out[:, at : at + width] = source[section, pl.ds(row + (at - first) // LANES, 1), :][:, :width]
            elif done < last:
                at = p.slice_at[name] + done - first
                out[:, done:last] = source[section, :, at : at + last - done].astype(F32)
            done = max(done, last)

    def ones_column(name, row):
        section = p.sections - 1
        at = p.slice_at[name] + row - p.start(name, section)
        block = slices_ref[section, :, at // LANES * LANES : at // LANES * LANES + LANES].astype(F32)
        return block.T[at % LANES : at % LANES + 1]

    def own_part(name, out):
        per = out.shape[1]
        width = min(per, LANES)
        share = p.part[name][0]
        for at in range(0, per, width):
            first = lax.axis_index("dp") * per + at
            block = first // LANES
            row = bias_rows_ref[block // share, pl.ds(p.bias_at[name] + block % share, 1), :]
            wide = jnp.broadcast_to(row, (8, LANES))
            out[:, at : at + width] = pltpu.roll(wide, (LANES - first % LANES) % LANES, 1)[:1, :width]

    for base, block in ((0, "coarse_"), (8, "fine_")):
        entry, head = block + "entry", block + "head"
        joined(entry, grads[base], slices_ref)
        grads[base + 1][...] = ones_column(entry, grads[base].shape[1])
        for i, name in enumerate((block + "middle", block + "upper")):
            joined(name, grads[base + 2 + 2 * i], slices_ref)
            own_part(name, grads[base + 3 + 2 * i])
        joined(head, grads[base + 6], slices_ref)
        joined(head, grads[base + 7], bias_rows_ref, p.bias_at[head])


def body(mesh_shape, history, targets, horizon, cotangent, *params):
    (c_entry, c_entry_b, c_middle, c_middle_b, c_upper, c_upper_b, c_head, c_head_b) = params[:8]
    (f_entry, f_entry_b, f_middle, f_middle_b, f_upper, f_upper_b, f_head, f_head_b) = params[8:]
    sections = mesh_shape["section"]
    length, hidden = f_entry.shape[0], c_middle.shape[1]
    p = Plan(
        length, f_head.shape[1] - length, hidden, c_entry.shape[0], c_head.shape[1], sections, history.shape[0]
    )
    pieces = (c_entry.T, c_middle, c_upper, c_head, f_entry.T, f_middle, f_upper, f_head)
    bias_pieces = (c_entry_b, c_middle_b, c_upper_b, f_entry_b, f_middle_b, f_upper_b)
    dp_count, per = mesh_shape["dp"], c_middle.shape[0]
    rows = (history.T, cotangent.T)
    fine_bias = f_head_b[None, :]
    rest = (targets.T, horizon[None, :], c_head_b[None, :], fine_bias)
    groups = dp_count // 2
    if sections == 4 and dp_count % 2 == 0 and per % 64 == 0 and groups > 1:
        theta, h3, gfine, pool, packed, slices, bias_rows = core(
            p, per, groups, *rows, *rest, pieces + tuple(b[None, :] for b in bias_pieces)
        )
    else:
        packed = pack(p, dict(zip(NAMES, pieces)), jnp.stack(bias_pieces, axis=1))
        packed = lax.all_gather(packed, "dp", axis=0, tiled=True)
        theta, h3, gfine, pool, part, head_bias = core(p, per, 0, *rows, *rest, (packed,))
        own = lax.psum_scatter(part.astype(F32), "dp", scatter_dimension=0, tiled=True)
        slices = lax.all_gather(own, "section", axis=0)
        bias_rows = lax.all_gather(lax.psum(head_bias, "dp"), "section", axis=0)
    residual, history_grad, prediction, *grads = outputs(
        p, packed, *rows, theta, h3, gfine, pool, fine_bias, slices, bias_rows
    )
    grads = [g.T if i in (0, 8) else g if g.shape[0] > 1 else g[0] for i, g in enumerate(grads)]
    return (prediction.T, residual.T, history_grad.T) + tuple(grads)


def solution(mesh):
    by_row, by_column, by_entry, copied = P("dp", None), P(None, "dp"), P("dp"), P()
    block = (by_column, by_entry, by_row, by_entry, by_row, by_entry, by_row, copied)
    in_specs = (by_row, by_row, by_entry, by_row) + block + block
    out_specs = (by_row, by_row, by_row) + block + block
    return jax.shard_map(
        functools.partial(body, dict(mesh.shape)), mesh=mesh, in_specs=in_specs, out_specs=out_specs, check_vma=False
    )
```

```python
import functools

import jax
import jax.numpy as jnp
from jax import lax
from jax.experimental import pallas as pl
from jax.experimental.pallas import tpu as pltpu
from jax.sharding import PartitionSpec as P

POOL = 8
KNOT = 24
LANES = 128
ONES = 16
GELU_A = 0.7978845608028654
GELU_B = GELU_A * 0.044715
F32 = jnp.float32
BF16 = jnp.bfloat16
MIB = 1 << 20


def up(size, unit):
    return -(-size // unit) * unit


class Plan:
    def __init__(self, length, horizon, hidden, pooled, coarse_out, sections, windows):
        self.length, self.horizon, self.hidden = length, horizon, hidden
        self.pooled, self.coarse_out = pooled, coarse_out
        self.fine_out = length + horizon
        self.sections, self.windows = sections, windows
        self.back, self.fore = length // KNOT, horizon // KNOT
        self.wide_in, self.wide_out = up(length + 1, LANES), up(self.fine_out + 1, LANES)
        self.pool_wide, self.theta_wide = up(pooled + 1, LANES), up(coarse_out + 1, LANES)
        widths = [
            ("coarse_entry", self.pool_wide),
            ("coarse_middle", hidden),
            ("coarse_upper", hidden),
            ("coarse_head", self.theta_wide),
            ("bias", LANES),
            ("fine_entry", self.wide_in),
            ("fine_middle", hidden),
            ("fine_upper", hidden),
            ("fine_head", self.wide_out),
        ]
        self.at, place = {}, 0
        for name, width in widths:
            self.at[name] = place
            place += width
        self.columns = place
        self.low = length // LANES * LANES
        self.skip = length - self.low
        self.square = hidden // sections
        self.slice_at, self.part, place = {}, {}, 0
        for name, width in (
            ("fine_head", self.wide_out),
            ("fine_entry", self.wide_in),
            ("fine_middle", hidden),
            ("fine_upper", hidden),
            ("coarse_middle", hidden),
            ("coarse_upper", hidden),
            ("coarse_head", self.theta_wide),
            ("coarse_entry", self.pool_wide),
        ):
            self.slice_at[name] = place
            total = width // LANES
            share = -(-total // sections)
            self.part[name] = share, total
            place += share * LANES
        self.slice_columns = place
        self.bias_at, place = {}, 0
        for name in ("fine_head", "coarse_head", "coarse_middle", "coarse_upper", "fine_middle", "fine_upper"):
            self.bias_at[name] = place
            place += self.part[name][0]
        self.bias_rows = up(place, 8)
        self.knot_rows = up(coarse_out, ONES)
        self.pair = 2 * KNOT
        self.r1_pairs = -(-(self.rows("fine_entry") + self.pair - ONES) // self.pair)

    def rows(self, name):
        return self.part[name][0] * LANES

    def start(self, name, section):
        low = min if isinstance(section, int) else jnp.minimum
        share, total = self.part[name]
        return low(section * share, total - share) * LANES


def gelu_both(a):
    square = a * a
    v = 0.5 + 0.5 * jnp.tanh(a * (GELU_A + GELU_B * square))
    h = a * v
    return h, v + h * (1.0 - v) * (2.0 * GELU_A + (6.0 * GELU_B) * square)


def dot(a, b):
    return jnp.dot(a, b, preferred_element_type=F32)


def dot_rows(a, b):
    return lax.dot_general(a, b, (((1,), (1,)), ((), ())), preferred_element_type=F32)


def aligned(start, size, unit):
    return pl.ds(pl.multiple_of(start, unit), size)


def column_of(row_ref, first, count):
    size = row_ref.shape[1]
    columns = []
    for at in range(first, first + count, LANES):
        width = max(0, min(LANES, size - at))
        row = jnp.zeros((1, LANES), F32) if width == 0 else row_ref[:, at : at + width]
        if 0 < width < LANES:
            row = jnp.concatenate([row, jnp.zeros((1, LANES - width), F32)], axis=1)
        columns.append(jnp.broadcast_to(row, (LANES, LANES)).T[:, :1])
    return jnp.concatenate(columns, axis=0)


def hat_weights(first, count, plan, turned=False, fore=False):
    p = plan
    shape = (p.knot_rows, count) if turned else (count, p.theta_wide)
    row = lax.broadcasted_iota(jnp.int32, shape, 1 if turned else 0) + first
    knot = lax.broadcasted_iota(jnp.int32, shape, 0 if turned else 1)
    away = row - KNOT * knot
    weight = jnp.maximum(KNOT - jnp.abs(away), 0)
    last = (knot == p.back - 1) | (knot == p.back + p.fore - 1)
    weight = jnp.where(last & (away > 0) & (away < KNOT), KNOT, weight)
    own = (knot >= p.back) & (row >= p.length) if fore else (knot < p.back) & (row < p.length)
    inside = own & (row < p.fine_out) & (knot < p.back + p.fore)
    return jnp.where(inside, weight, 0).astype(F32).astype(BF16)


def fractions(width):
    later = lax.broadcasted_iota(jnp.int32, (KNOT, width), 0).astype(F32) * (1.0 / KNOT)
    return 1.0 - later, later


NAMES = (
    "coarse_entry",
    "coarse_middle",
    "coarse_upper",
    "coarse_head",
    "fine_entry",
    "fine_middle",
    "fine_upper",
    "fine_head",
)
KEPT = ("fine_entry", "fine_head")


def remote(source, target, send_sem, recv_sem, place):
    return pltpu.make_async_remote_copy(
        src_ref=source,
        dst_ref=target,
        send_sem=send_sem,
        recv_sem=recv_sem,
        device_id=place,
        device_id_type=pl.DeviceIdType.MESH,
    )


def signal(semaphore, places):
    for place in places:
        pl.semaphore_signal(semaphore, inc=1, device_id=place, device_id_type=pl.DeviceIdType.MESH)


class Ways:
    def __init__(self, groups):
        self.section, self.dp = lax.axis_index("section"), lax.axis_index("dp")
        self.group, self.core = self.dp // 2, self.dp % 2
        self.groups = groups
        self.partner = (self.section, self.group * 2 + 1 - self.core)
        s = self.section
        self.side = [s + 1 - 2 * (s % 2), (s + 2) % 4]
        self.sides = [(t, self.dp) for t in self.side]
        self.across = 3 - s

    def far(self, j):
        group = (self.group + j) % self.groups
        return group, (self.section, group * 2 + self.core)

    def from_far(self, j):
        return (self.group + self.groups - j) % self.groups

    def all(self):
        return [self.partner] + self.sides + [self.far(j)[1] for j in range(1, self.groups)]


class Gather:
    def __init__(self, plan, way, per, cuts, w_ref, shards, biases, send, recv, partner_recv):
        self.p, self.way, self.per, self.cuts, self.w_ref = plan, way, per, cuts, w_ref
        self.shards, self.biases = shards, biases
        self.send, self.recv, self.partner_recv = send, recv, partner_recv
        self.near = range(1, way.groups)
        self.chunks, self.ahead = len(cuts) - 1, 3

    def at(self, k, owner, s=None):
        quarter = self.per // 4
        rows = aligned(owner * self.per, self.per, self.per)
        if s is not None:
            rows = aligned(owner * self.per + s * quarter, quarter, quarter)
        return self.w_ref.at[rows, self.cuts[k] : self.cuts[k + 1]]

    def source(self, j):
        return self.way.from_far(j) * 2 + self.way.core

    def copy(self, here, k, j, kind, place):
        return remote(here, here, self.send.at[k, j - 1, kind], self.recv.at[k, j - 1, kind], place)

    def to_far(self, k, j):
        return self.copy(self.at(k, self.way.dp, self.way.section), k, j, 0, self.way.far(j)[1])

    def to_side(self, k, j, i):
        return self.copy(self.at(k, self.source(j), self.way.section), k, j, 1 + i, self.way.sides[i])

    def to_across(self, k, j):
        i = (k + j) % 2
        return self.copy(self.at(k, self.source(j), self.way.side[i]), k, j, 3, self.way.sides[1 - i])

    def to_partner(self, k, j):
        here = self.at(k, self.source(j) if j else self.way.dp)
        return remote(here, here, self.send.at[k, max(j - 1, 0), 4 if j else 5], self.partner_recv.at[k, j], self.way.partner)

    def arrived(self, k, j, kind):
        s = [self.way.section, self.way.side[0], self.way.side[1], self.way.across][kind]
        self.copy(self.at(k, self.source(j), s), k, j, kind, self.way.partner).wait_recv()

    def cast(self, k):
        p, own = self.p, aligned(self.way.dp * self.per, self.per, self.per)
        low, high = self.cuts[k], self.cuts[k + 1]
        for ref, name in zip(self.shards, NAMES):
            at, size = p.at[name], ref.shape[1]
            wide = up(size + 1, LANES) if name.endswith(("entry", "head")) else size
            first, last = max(at, low), min(at + wide, high)
            full = min(last, at + size // LANES * LANES)
            if first < full:
                self.w_ref[own, first:full] = ref[:, first - at : full - at].astype(BF16)
            if first < last and last > full:
                rest = ref[:, full - at : size].astype(BF16)
                pad = jnp.zeros((self.per, last - at - size), BF16)
                self.w_ref[own, full:last] = jnp.concatenate([rest, pad], axis=1)
        at = p.at["bias"]
        if low <= at < high:
            count = len(self.biases)
            rows = jnp.concatenate([ref[...] for ref in self.biases] + [jnp.zeros((8 - count, self.per), F32)], axis=0)
            wide = jnp.concatenate([rows, jnp.zeros((8, LANES - self.per), F32)], axis=1)
            wide = jnp.concatenate([wide, jnp.zeros((LANES - 8, LANES), F32)], axis=0)
            self.w_ref[own, at : at + LANES] = wide.T[: self.per].astype(BF16)

    def first(self, k):
        self.cast(k)
        for j in self.near:
            self.to_far(k, j).start()
        self.to_partner(k, 0).start()

    def second(self, k):
        for j in self.near:
            self.arrived(k, j, 0)
            for i in range(2):
                self.to_side(k, j, i).start()

    def third(self, k):
        for j in self.near:
            self.arrived(k, j, 1)
            self.arrived(k, j, 2)
            self.to_across(k, j).start()

    def fourth(self, k):
        for j in self.near:
            self.arrived(k, j, 3)
            self.to_partner(k, j).start()

    def turn(self, t):
        for depth, stage in ((2, self.fourth), (1, self.third), (0, self.second)):
            if 0 <= t - depth < self.chunks:
                stage(t - depth)
        if t + self.ahead < self.chunks:
            self.first(t + self.ahead)

    def complete(self, k):
        for j in range(self.way.groups):
            there = (self.way.from_far(j) * 2 + 1 - self.way.core) if j else self.way.partner[1]
            here = self.at(k, there)
            remote(here, here, self.send.at[k, 0, 5], self.partner_recv.at[k, j], self.way.partner).wait_recv()

    def sent(self):
        for k in range(self.chunks):
            for j in self.near:
                for copy in (self.to_far(k, j), self.to_side(k, j, 0), self.to_side(k, j, 1), self.to_across(k, j)):
                    copy.wait_send()
                self.to_partner(k, j).wait_send()
            self.to_partner(k, 0).wait_send()


class Reduce:
    def __init__(self, plan, way, per, cuts, part_ref, core_in, far_in, far_out, stage_ref, out_ref, send, recv, local):
        self.p, self.way, self.per, self.cuts = plan, way, per, cuts
        self.part_ref, self.core_in, self.far_in, self.far_out = part_ref, core_in, far_in, far_out
        self.stage_ref, self.out_ref, self.send, self.recv, self.local = stage_ref, out_ref, send, recv, local
        self.near = range(1, way.groups)
        self.chunks = len(cuts) - 1

    def columns(self, k):
        return slice(self.cuts[k], self.cuts[k + 1])

    def to_partner(self, k, g):
        return remote(
            self.part_ref(g * 2 + 1 - self.way.core, k),
            self.core_in(g, k),
            self.send.at[k, g, 0],
            self.recv.at[k, g, 0],
            self.way.partner,
        )

    def to_far(self, k, j):
        here, there = self.far_out(j - 1, k), self.far_in(j - 1, k)
        return remote(here, there, self.send.at[k, j - 1, 1], self.recv.at[k, j - 1, 1], self.way.far(j)[1])

    def side(self, k, source, i, to):
        here = self.out_ref.at[source, :, self.columns(k)]
        return remote(here, here, self.send.at[k, i, 2], self.recv.at[k, i, 2], to)

    def to_side(self, k, i):
        here = self.stage_ref.at[:, self.columns(k)]
        there = self.out_ref.at[self.way.section, :, self.columns(k)]
        return remote(here, there, self.send.at[k, i, 2], self.recv.at[k, i, 2], self.way.sides[i])

    def keep(self, k):
        there = self.out_ref.at[self.way.section, :, self.columns(k)]
        return pltpu.make_async_copy(self.stage_ref.at[:, self.columns(k)], there, self.local.at[k])

    def to_across(self, k):
        i = k % 2
        return self.side(k, self.way.side[i], 2, self.way.sides[1 - i])

    def summed(self, k, group):
        own = self.part_ref(group * 2 + self.way.core, k)[...].astype(F32)
        return own + self.core_in(group, k)[...].astype(F32)

    def first(self, k):
        for g in range(self.way.groups):
            self.to_partner(k, g).start()

    def second(self, k):
        for g in range(self.way.groups):
            self.to_partner(k, g).wait_recv()
        for j in self.near:
            self.far_out(j - 1, k)[...] = self.summed(k, self.way.far(j)[0]).astype(BF16)
            self.to_far(k, j).start()

    def third(self, k):
        total = self.summed(k, self.way.group)
        for j in self.near:
            self.to_far(k, j).wait_recv()
            total += self.far_in(j - 1, k)[...].astype(F32)
        self.stage_ref[:, self.columns(k)] = total.astype(BF16)
        for i in range(2):
            self.to_side(k, i).start()
        self.keep(k).start()

    def fourth(self, k):
        i = k % 2
        for turn in (i, 1 - i):
            self.side(k, self.way.side[turn], turn, self.way.sides[turn]).wait_recv()
            if turn == i:
                self.to_across(k).start()

    def complete(self, k):
        self.side(k, self.way.across, 2, self.way.partner).wait_recv()

    def sent(self, k):
        for g in range(self.way.groups):
            self.to_partner(k, g).wait_send()
        for j in self.near:
            self.to_far(k, j).wait_send()
        for i in range(2):
            self.to_side(k, i).wait_send()
        self.to_across(k).wait_send()
        self.keep(k).wait()


class ReduceBias:
    def __init__(self, way, own_ref, core_in, far_ref, out_ref, send, recv):
        self.way, self.own_ref, self.core_in, self.far_ref, self.out_ref = way, own_ref, core_in, far_ref, out_ref
        self.send, self.recv = send, recv
        self.near = range(1, way.groups)

    def copy(self, here, there, n, place):
        return remote(here, there, self.send.at[n], self.recv.at[n], place)

    def to_partner(self):
        return self.copy(self.own_ref, self.core_in, 0, self.way.partner)

    def to_far(self, j):
        here = self.far_ref.at[self.way.group]
        return self.copy(here, here, j, self.way.far(j)[1])

    def side(self, source, n, to):
        here = self.out_ref.at[source]
        return self.copy(here, here, self.way.groups + n, to)

    def to_across(self):
        return self.side(self.way.side[0], 2, self.way.sides[1])

    def second(self):
        self.to_partner().wait_recv()
        self.far_ref[self.way.group] = self.own_ref[...] + self.core_in[...]
        for j in self.near:
            self.to_far(j).start()

    def third(self):
        for j in self.near:
            here = self.far_ref.at[self.way.from_far(j)]
            self.copy(here, here, j, self.way.partner).wait_recv()
        total = self.far_ref[0]
        for g in range(1, self.way.groups):
            total += self.far_ref[g]
        self.out_ref[self.way.section] = total
        for i in range(2):
            self.side(self.way.section, i, self.way.sides[i]).start()

    def fourth(self):
        self.side(self.way.side[0], 0, self.way.partner).wait_recv()
        self.to_across().start()
        self.side(self.way.side[1], 1, self.way.partner).wait_recv()

    def complete(self):
        self.side(self.way.across, 2, self.way.partner).wait_recv()
        self.to_partner().wait_send()
        for j in self.near:
            self.to_far(j).wait_send()
        for i in range(2):
            self.side(self.way.section, i, self.way.sides[i]).wait_send()
        self.to_across().wait_send()


def core_kernel(plan, per, groups, *refs):
    p = plan
    refs = list(refs)
    take = lambda count: [refs.pop(0) for _ in range(count)]
    history_ref, cotangent_ref, target_ref, horizon_ref, coarse_bias_ref, fine_bias_ref = take(6)
    if groups:
        shards_in = take(14)
    else:
        (packed_ref,) = take(1)
    theta_out, h3_out, gfine_out, pool_out = take(4)
    if groups:
        kept_out, slices_out, bias_out = take(3)
    else:
        slice_out, bias_out = take(2)
    w_ref, big_ref = take(2)
    h_refs, g_refs = take(6), take(6)
    r1_ref, pooled_ref, split_ref, theta_ref, gtheta_ref, gknot_ref = take(6)
    pw_ref, pwt_ref, turned_ref, even_ref, odd_ref, bias_ref = take(6)
    horizon_buf, coarse_bias_buf, fine_bias_buf, sems = take(4)
    if groups:
        shards = take(14)
        shard_sems, send, recv, partner_recv = take(4)
        head_bias_ref, bias_in, bias_far, stage_ref, ready, reduce_send, reduce_recv, bias_send, bias_recv = take(9)
        keep_sems = take(1)[0]
    else:
        head_bias_ref = bias_out
    hid, windows = p.hidden, p.windows
    section = lax.axis_index("section")
    chunk = min(512, windows)
    chunks = windows // chunk
    H = slice(0, hid)
    lanes_of = lambda n: aligned(n * chunk, chunk, chunk)
    place = p.at["fine_entry"]
    head_at = p.at["fine_head"]

    load = lambda source, out, sem: pltpu.make_async_copy(source, out, sems.at[sem])
    history_in = load(history_ref, big_ref.at[: p.length], 1)
    cotangent_in = load(cotangent_ref, big_ref.at[: p.length], 2)
    target_in = load(target_ref, big_ref.at[p.length : p.fine_out], 0)
    rows_in = [
        load(horizon_ref, horizon_buf, 3),
        load(coarse_bias_ref, coarse_bias_buf, 4),
        load(fine_bias_ref, fine_bias_buf, 5),
    ]
    theta_copy = load(theta_ref, theta_out, 6)
    h3_copy = load(h_refs[5].at[H], h3_out, 7)
    gfine_copy = load(g_refs[3], gfine_out, 8)
    pool_copy = load(pooled_ref, pool_out, 9)

    if groups:
        shards_load = [
            pltpu.make_async_copy(source, out, shard_sems.at[n]) for n, (source, out) in enumerate(zip(shards_in, shards))
        ]
        order = [0, 1, 2, 3, 8, 9, 10, 11, 12, 13, 4, 5, 6, 7]
        for n in order:
            shards_load[n].start()
        way = Ways(groups)
        middle = p.at["fine_middle"]
        third = (p.columns - middle) // 3 // LANES * LANES
        entry_cut = place + up((middle - place) // 2, LANES)
        cuts = (0, 2 * hid, place, entry_cut, middle, middle + third, middle + 2 * third, p.columns)
        gather = Gather(p, way, per, cuts, w_ref, shards[:8], shards[8:], send, recv, partner_recv)
        cotangent_in.start()
        for copy in rows_in:
            copy.start()
        barrier = pltpu.get_barrier_semaphore()
        signal(barrier, way.all())
        for n in order[:10]:
            shards_load[n].wait()
        pl.semaphore_wait(barrier, len(way.all()))
        gather.first(0)
        for n in order[10:]:
            shards_load[n].wait()
        for k in range(1, gather.ahead):
            gather.first(k)
    else:
        weights_in = load(packed_ref, w_ref, 10)
        weights_in.start()
        cotangent_in.start()
        for copy in rows_in:
            copy.start()

    def turn(t):
        if groups:
            gather.turn(t)

    def complete(*ks):
        if groups:
            for k in ks:
                gather.complete(k)

    tail = p.wide_out - p.length
    mark = lax.broadcasted_iota(jnp.int32, (tail, windows), 0) < POOL
    big_ref[p.length :, :] = mark.astype(F32).astype(BF16)
    pooled_ref[...] = jnp.zeros_like(pooled_ref)
    for index in range(6):
        h_refs[index][hid:, :] = jnp.ones((ONES, windows), BF16)
    for copy in rows_in:
        copy.wait()
    step = 6 * LANES

    def adjoint(low, high, fore):
        for first in range(low, high, step):
            count = min(step, high - first)
            hats = hat_weights(first, count, p, True, fore)

            @pl.loop(0, chunks)
            def _(n):
                lanes = lanes_of(n)
                part = dot(hats, big_ref[first : first + count, lanes]) * (-1.0 / KNOT)
                if first == 0:
                    gtheta_ref[:, lanes] = part
                else:
                    gtheta_ref[:, lanes] += part

    cotangent_in.wait()
    adjoint(0, p.wide_in, False)
    history_in.start()
    turn(0)
    turn(1)
    history_in.wait()

    unit = hid
    shape = (unit // POOL, unit)
    member = lax.broadcasted_iota(jnp.int32, shape, 1) - POOL * lax.broadcasted_iota(jnp.int32, shape, 0)
    turned_ref[: unit // POOL, :] = ((member >= 0) & (member < POOL)).astype(F32).astype(BF16)
    firsts = list(range(0, p.wide_in, unit))
    for number, first in enumerate(firsts):
        count = min(unit, p.wide_in - first)
        rows = slice(first // POOL, (first + count) // POOL)

        @pl.loop(0, chunks)
        def _(n):
            lanes = lanes_of(n)
            total = dot(turned_ref[: count // POOL, :count], big_ref[first : first + count, lanes])
            pooled_ref[rows, lanes] = (total * (1.0 / POOL)).astype(BF16)

        if number in (len(firsts) // 2, len(firsts) - 1):
            turn(2 + number // (len(firsts) - 1))
    complete(0, 1)
    if not groups:
        weights_in.wait()
    fore_parts = [(0, 8 * p.pair), (8 * p.pair, p.horizon)]
    fore_bias = column_of(fine_bias_buf, p.low, p.wide_out - p.low)
    placed = w_ref[:, p.at["bias"] : p.at["bias"] + LANES].astype(F32)
    lane = lax.broadcasted_iota(jnp.int32, (hid, LANES), 1)
    for number, (low, high) in enumerate(fore_parts):
        column = fore_bias[p.skip + low : p.skip + high]
        column = jnp.concatenate([column, jnp.zeros((hid - high + low, 1), F32)], axis=0)
        placed = jnp.where(lane == 6 + number, column, placed)
    bias_ref[...] = placed

    def pipeline(*layers):
        tile, pending = 0, nothing
        for before, produce, finish, after in layers:
            before()
            for n in range(chunks):
                lanes = slice(n * chunk, (n + 1) * chunk)
                out = (even_ref, odd_ref)[tile % 2]
                value = produce(lanes)
                out[: value.shape[0], :] = value
                pending()
                pending = functools.partial(finish, out, lanes)
                tile += 1
            after()
        pending()

    def nothing():
        pass

    def turn_weight(first, count):
        turned_ref[:count, :] = w_ref[:, first : first + count].T

    strip = ONES

    def activate(index):
        def finish(source, lanes):
            for r in range(0, hid, strip):
                rows = slice(r, r + strip)
                h, slope = gelu_both(source[rows, :] + bias_ref[rows, index : index + 1])
                h_refs[index][rows, lanes] = h.astype(BF16)
                g_refs[index][rows, lanes] = slope.astype(BF16)

        return finish

    def hidden(name, index, after=nothing):
        return (
            lambda: turn_weight(p.at[name], hid),
            lambda lanes: dot(turned_ref[H, :], h_refs[index - 1][H, lanes]),
            activate(index),
            after,
        )

    at_entry = p.at["coarse_entry"]
    at_head = p.at["coarse_head"]
    theta_bias = column_of(coarse_bias_buf, 0, p.theta_wide)

    def keep_theta(source, lanes):
        for r in range(0, p.theta_wide, strip):
            rows = slice(r, r + strip)
            theta = source[rows, :] + theta_bias[rows]
            if r < p.knot_rows:
                theta_ref[rows, lanes] = theta
            knots = jnp.where(lax.broadcasted_iota(jnp.int32, theta.shape, 0) + r < p.back, theta, 0.0)
            high = knots.astype(BF16)
            split_ref[rows, lanes] = high
            split_ref[p.theta_wide + r : p.theta_wide + r + strip, lanes] = (knots - high.astype(F32)).astype(BF16)

    pipeline(
        (
            nothing,
            lambda lanes: dot(w_ref[:, at_entry : at_entry + p.pool_wide], pooled_ref[:, lanes]),
            activate(0),
            lambda: turn(4),
        ),
        hidden("coarse_middle", 1, lambda: turn(5)),
        hidden("coarse_upper", 2),
        (
            lambda: turn_weight(at_head, p.theta_wide),
            lambda lanes: dot(turned_ref[: p.theta_wide, :], h_refs[2][H, lanes]),
            keep_theta,
            nothing,
        ),
    )
    theta_copy.start()
    turn(6)

    first_pair = p.start("fine_entry", section) // p.pair

    def interpolate(base, count, k, rest, later, lanes):
        own = theta_ref[pl.ds(base + jnp.minimum(k, count - 1), 1), lanes]
        after = theta_ref[pl.ds(base + jnp.minimum(k + 1, count - 1), 1), lanes]
        return own * rest + after * later

    everything = slice(0, windows)
    rest, later = fractions(windows)

    @pl.loop(0, p.r1_pairs)
    def _(i):
        pair = first_pair + i
        source = aligned(pair * p.pair, p.pair, ONES)
        made = jnp.concatenate(
            [interpolate(0, p.back, 2 * pair + j, rest, later, everything) for j in range(2)], axis=0
        )
        made = made * (pair < p.back // 2).astype(F32)
        r1_ref[aligned(i * p.pair, p.pair, ONES), :] = (big_ref[source, :].astype(F32) - made).astype(BF16)

    turn(7)
    complete(2, 3)

    total = jnp.zeros((hid, p.theta_wide), F32)
    for first in range(0, p.wide_in, step):
        count = min(step, p.wide_in - first)
        total += dot(w_ref[:, place + first : place + first + count], hat_weights(first, count, p))
    product = (total * (1.0 / KNOT)).astype(BF16)
    pwt_ref[...] = product
    pw_ref[...] = product.T
    turn(8)

    def fine_entry(lanes):
        a = dot(w_ref[:, place : place + p.wide_in], big_ref[: p.wide_in, lanes])
        for part in (0, p.theta_wide):
            a -= dot(pwt_ref[...], split_ref[part : part + p.theta_wide, lanes])
        return a

    def entry_made():
        cotangent_in.start()
        target_in.start()
        big_ref[p.fine_out :, :] = jnp.zeros((p.wide_out - p.fine_out, windows), BF16)
        if groups:
            signal(ready.at[0], way.all())
        complete(4)

    rest_c, later_c = fractions(chunk)

    def fore(number):
        low, high = fore_parts[number]

        def before():
            if number == 0:
                complete(5, 6)
                target_in.wait()
            first = head_at + p.low
            turned = w_ref[:, first : first + p.wide_out - p.low].T
            turned_ref[: high - low, :] = turned[p.skip + low : p.skip + high]

        def finish(source, lanes):
            for k in range(low // KNOT, high // KNOT, 2):
                here = slice(k * KNOT - low, (k + 2) * KNOT - low)
                second = source[here, :] + bias_ref[here, 6 + number : 7 + number]
                first = jnp.concatenate(
                    [interpolate(p.back, p.fore, k + j, rest_c, later_c, lanes) for j in range(2)], axis=0
                )
                counts = (lax.broadcasted_iota(jnp.int32, (2 * KNOT, chunk), 0) + k * KNOT) < horizon_buf[:, lanes]
                there = slice(p.length + k * KNOT, p.length + (k + 2) * KNOT)
                error = first + second - big_ref[there, lanes].astype(F32)
                big_ref[there, lanes] = jnp.where(counts, -error, 0.0).astype(BF16)

        return before, lambda lanes: dot(turned_ref[: high - low, :], h_refs[5][H, lanes]), finish, nothing

    pipeline(
        (nothing, fine_entry, activate(3), entry_made),
        hidden("fine_middle", 4),
        hidden("fine_upper", 5),
        fore(0),
        fore(1),
    )
    h3_copy.start()
    if groups:
        kept = [
            load(w_ref.at[:, p.at[name] : p.at[name] + wide], kept_out.at[:, p.at[name] : p.at[name] + wide], 10 + n)
            for n, (name, wide) in enumerate(zip(KEPT, (p.wide_in, p.wide_out)))
        ]
        for copy in kept:
            copy.start()
    cotangent_in.wait()

    def gradient_slice(name, left, right_ref, first, step=LANES, sign=1.0):
        left_side = left[...] if name.endswith("entry") else h_refs[left][...]
        for b in range(0, p.rows(name), step):
            width = min(step, p.rows(name) - b)
            value = sign * dot_rows(left_side, right_ref[aligned(first + b, width, ONES), :])
            to = place + p.slice_at[name] + b
            w_ref[:, to : to + width] = value[:hid].astype(BF16)
            if name in p.bias_at:
                for c in range(0, width, LANES):
                    row = p.bias_at[name] + (b + c) // LANES
                    head_bias_ref[row : row + 1, :] = value[hid : hid + 1, c : c + LANES]

    def square_slice(name, index):
        gradient_slice(name, index - 1, g_refs[index], p.start(name, section))

    def back(index, product, after=nothing):
        def finish(source, lanes):
            for r in range(0, hid, strip):
                rows = slice(r, r + strip)
                g_refs[index][rows, lanes] = (source[rows, :] * g_refs[index][rows, lanes].astype(F32)).astype(BF16)

        return nothing, product, finish, after

    def times(name, index):
        at = p.at[name]
        return lambda lanes: dot(w_ref[:, at : at + hid], g_refs[index][:, lanes])

    if groups:
        for copy in kept:
            copy.wait()
        gather.sent()
        cuts = (0, p.slice_at["fine_entry"], p.slice_at["coarse_middle"], p.slice_columns)
        width = lambda k: cuts[k + 1] - cuts[k]

        def arrivals(row, k):
            rows = slice(row * per, (row + 1) * per) if isinstance(row, int) else aligned(row * per, per, per)
            if k == 0:
                return split_ref.at[rows, : width(0)]
            first = head_at + cuts[k] - cuts[1]
            return w_ref.at[rows, first : first + width(k)]

        def departures(j, k):
            first = (k * groups + j) * per
            return big_ref.at[first : first + per, : width(k)]

        reduce = Reduce(
            p,
            way,
            per,
            cuts,
            lambda owner, k: w_ref.at[aligned(owner * per, per, per), place + cuts[k] : place + cuts[k + 1]],
            arrivals,
            lambda j, k: arrivals(groups + j, k),
            departures,
            stage_ref,
            slices_out,
            reduce_send,
            reduce_recv,
            keep_sems,
        )
        reduce_bias = ReduceBias(way, head_bias_ref, bias_in, bias_far, bias_out, bias_send, bias_recv)

    gradient_slice("fine_head", 5, big_ref, p.start("fine_head", section), 3 * LANES, -1.0)
    if groups:
        pl.semaphore_wait(ready.at[0], len(way.all()))
        reduce.first(0)

    adjoint(p.low, p.wide_out, True)

    def head_used():
        if groups:
            signal(ready.at[1], way.all())
            reduce.second(0)

    pipeline(
        back(5, lambda lanes: -dot(w_ref[:, head_at : head_at + p.wide_out], big_ref[:, lanes]), head_used),
        back(4, times("fine_upper", 5)),
        back(3, times("fine_middle", 4)),
    )
    gfine_copy.start()
    gradient_slice("fine_entry", g_refs[3], r1_ref, p.start("fine_entry", section) - first_pair * p.pair, 2 * LANES)
    square_slice("fine_middle", 4)
    square_slice("fine_upper", 5)
    if groups:
        pl.semaphore_wait(ready.at[1], len(way.all()))
        reduce.first(1)
        reduce.third(0)
    gknot_ref[p.knot_rows :, :] = jnp.zeros((p.theta_wide - p.knot_rows, windows), BF16)

    def knots_done(source, lanes):
        for r in range(0, p.knot_rows, strip):
            rows = slice(r, r + strip)
            gknot_ref[rows, lanes] = (gtheta_ref[rows, lanes] - source[rows, :]).astype(BF16)

    pipeline(
        (nothing, lambda lanes: dot(pw_ref[: p.knot_rows, :], g_refs[3][:, lanes]), knots_done, nothing),
        back(
            2,
            lambda lanes: dot(w_ref[:, at_head : at_head + p.theta_wide], gknot_ref[:, lanes]),
            lambda: reduce.second(1) if groups else None,
        ),
        back(1, times("coarse_upper", 2), lambda: reduce.fourth(0) if groups else None),
        back(0, times("coarse_middle", 1)),
    )
    gradient_slice("coarse_head", 2, gknot_ref, p.start("coarse_head", section))
    gradient_slice("coarse_entry", g_refs[0], pooled_ref, p.start("coarse_entry", section))
    square_slice("coarse_middle", 1)
    square_slice("coarse_upper", 2)
    if groups:
        reduce.first(2)
        reduce_bias.to_partner().start()
        reduce.third(1)
        reduce.second(2)
        reduce_bias.second()

    def pool_gradient(source, lanes):
        for r in range(0, p.pool_wide, strip):
            pooled_ref[r : r + strip, lanes] = (source[r : r + strip, :] * (1.0 / POOL)).astype(BF16)

    pipeline(
        (
            lambda: turn_weight(at_entry, p.pool_wide),
            lambda lanes: dot(turned_ref[: p.pool_wide, :], g_refs[0][:, lanes]),
            pool_gradient,
            nothing,
        )
    )
    pool_copy.start()
    if groups:
        reduce.fourth(1)
        reduce_bias.third()
        reduce.third(2)
        reduce_bias.fourth()
        reduce.fourth(2)
        for k in range(reduce.chunks):
            reduce.complete(k)
            reduce.sent(k)
        reduce_bias.complete()
    else:
        out = load(w_ref.at[:, place : place + p.slice_columns], slice_out, 10)
        out.start()
        out.wait()
    theta_copy.wait()
    h3_copy.wait()
    gfine_copy.wait()
    pool_copy.wait()


ANY = pl.BlockSpec(memory_space=pl.ANY)
VMEM = pl.BlockSpec(memory_space=pltpu.VMEM)


def core(plan, per, groups, history, cotangent, targets, horizon, coarse_bias, fine_bias, weights):
    p = plan
    hid, windows = p.hidden, p.windows
    flops = 2 * windows * hid * (2 * p.length + 2 * p.wide_out // 3 + 12 * hid + p.slice_columns)
    out_shape = [
        jax.ShapeDtypeStruct((p.knot_rows, windows), F32),
        jax.ShapeDtypeStruct((hid, windows), BF16),
        jax.ShapeDtypeStruct((hid, windows), BF16),
        jax.ShapeDtypeStruct((p.pool_wide, windows), BF16),
    ]
    out_specs = [ANY] * 4
    scratch = [
        pltpu.VMEM((hid, p.columns), BF16),
        pltpu.VMEM((p.wide_out, windows), BF16),
        *[pltpu.VMEM((hid + ONES, windows), BF16)] * 6,
        *[pltpu.VMEM((hid, windows), BF16)] * 6,
        pltpu.VMEM((p.r1_pairs * p.pair, windows), BF16),
        pltpu.VMEM((p.pool_wide, windows), BF16),
        pltpu.VMEM((2 * p.theta_wide, windows), BF16),
        pltpu.VMEM((p.knot_rows, windows), F32),
        pltpu.VMEM((p.knot_rows, windows), F32),
        pltpu.VMEM((p.theta_wide, windows), BF16),
        pltpu.VMEM((p.theta_wide, hid), BF16),
        pltpu.VMEM((hid, p.theta_wide), BF16),
        pltpu.VMEM((hid, hid), BF16),
        pltpu.VMEM((hid, min(512, windows)), F32),
        pltpu.VMEM((hid, min(512, windows)), F32),
        pltpu.VMEM((hid, LANES), F32),
        pltpu.VMEM(horizon.shape, jnp.int32),
        pltpu.VMEM(coarse_bias.shape, F32),
        pltpu.VMEM(fine_bias.shape, F32),
        pltpu.SemaphoreType.DMA((13,)),
    ]
    params = {}
    if groups:
        bias = (p.bias_rows, LANES)
        out_shape += [
            jax.ShapeDtypeStruct((hid, p.columns), BF16),
            jax.ShapeDtypeStruct((4, per, p.slice_columns), BF16),
            jax.ShapeDtypeStruct((4,) + bias, F32),
        ]
        out_specs += [ANY, ANY, VMEM]
        chunks, reduce_chunks = 7, 3
        scratch += [pltpu.VMEM(piece.shape, F32) for piece in weights]
        scratch += [
            pltpu.SemaphoreType.DMA((len(weights),)),
            pltpu.SemaphoreType.DMA((chunks, groups - 1, 6)),
            pltpu.SemaphoreType.DMA((chunks, groups - 1, 4)),
            pltpu.SemaphoreType.DMA((chunks, groups)),
            pltpu.VMEM(bias, F32),
            pltpu.VMEM(bias, F32),
            pltpu.VMEM((groups,) + bias, F32),
            pltpu.VMEM((per, p.slice_columns), BF16),
            pltpu.SemaphoreType.REGULAR((2,)),
            pltpu.SemaphoreType.DMA((reduce_chunks, max(groups, 3), 3)),
            pltpu.SemaphoreType.DMA((reduce_chunks, max(groups, 3), 3)),
            pltpu.SemaphoreType.DMA((groups + 3,)),
            pltpu.SemaphoreType.DMA((groups + 3,)),
            pltpu.SemaphoreType.DMA((reduce_chunks,)),
        ]
        params = {"collective_id": 0, "has_side_effects": True}
    else:
        out_shape += [jax.ShapeDtypeStruct((hid, p.slice_columns), BF16), jax.ShapeDtypeStruct((p.bias_rows, LANES), F32)]
        out_specs += [ANY, VMEM]
    return pl.pallas_call(
        functools.partial(core_kernel, p, per, groups),
        out_shape=tuple(out_shape),
        in_specs=[ANY] * (6 + len(weights)),
        out_specs=tuple(out_specs),
        scratch_shapes=scratch,
        compiler_params=pltpu.CompilerParams(vmem_limit_bytes=63 * MIB, **params),
        cost_estimate=pl.CostEstimate(flops=flops, bytes_accessed=windows * p.length * 4, transcendentals=0),
    )(history, cotangent, targets, horizon, coarse_bias, fine_bias, *weights)


def outputs_kernel(
    plan,
    block,
    steps,
    packed_ref,
    history_ref,
    cotangent_ref,
    theta_ref,
    h3_ref,
    gfine_ref,
    pool_ref,
    fine_bias_ref,
    slices_ref,
    bias_rows_ref,
    residual_ref,
    history_grad_ref,
    prediction_ref,
    *refs,
):
    grads = refs[:16]
    head_ref, entry_ref, side_ref, pool_grad, fore_ref, *products, turned_head, turned_entry, bias_ref, sems = refs[16:]
    back_refs, fine_refs = products[:2], products[2:]
    p = plan
    step = pl.program_id(0)
    windows = p.windows
    chunk = min(512, windows)
    chunks = windows // chunk
    lanes_of = lambda n: slice(n * chunk, (n + 1) * chunk) if isinstance(n, int) else aligned(n * chunk, chunk, chunk)
    knots = block // KNOT
    pooled = block // POOL
    rest, later = fractions(chunk)

    def fetch(name, out, at, slot, sem):
        first = aligned(p.at[name] + at * block, block, LANES)
        return pltpu.make_async_copy(packed_ref.at[:, first], out.at[slot], sems.at[sem, slot])

    def interpolate(k, count, base, lanes):
        low = jnp.minimum if not isinstance(k, int) else min
        own = theta_ref[pl.ds(base + low(k, count - 1), 1), lanes]
        after = theta_ref[pl.ds(base + low(k + 1, count - 1), 1), lanes]
        return own * rest + after * later

    fore_out = pltpu.make_async_copy(fore_ref, prediction_ref, sems.at[3, 0])
    wide = p.wide_out - p.low
    first_fore = p.at["fine_head"] + p.low
    side = pltpu.make_async_copy(packed_ref.at[:, first_fore : first_fore + wide], side_ref, sems.at[2, 0])

    @pl.when(step == 0)
    def _():
        fetch("fine_head", head_ref, 0, 0, 0).start()
        fetch("fine_entry", entry_ref, 0, 0, 1).start()
        side.start()
        pool_grad[...] = pool_ref[...].astype(F32)

    @pl.when(step == 2)
    def _():
        side.wait()
        turned_fore = side_ref[...].T
        fore_bias = column_of(fine_bias_ref, p.low, wide)

        @pl.loop(0, chunks)
        def _(n):
            lanes = lanes_of(n)
            back_refs[0][: p.horizon, :] = dot(turned_fore[p.skip : p.skip + p.horizon], h3_ref[:, lanes])
            for k in range(0, p.fore, 2):
                rows = slice(k * KNOT, (k + 2) * KNOT)
                second = back_refs[0][rows, :] + fore_bias[p.skip + k * KNOT : p.skip + (k + 2) * KNOT]
                first = jnp.concatenate([interpolate(k + j, p.fore, p.back, lanes) for j in range(2)], axis=0)
                fore_ref[rows, lanes] = first.astype(BF16).astype(F32) + second.astype(BF16).astype(F32)

        fore_out.start()

    @pl.when(step == 1)
    def _():
        unpack(p, slices_ref, bias_rows_ref, grads)

    slot = step % 2

    @pl.when(step + 1 < steps)
    def _():
        fetch("fine_head", head_ref, step + 1, 1 - slot, 0).start()
        fetch("fine_entry", entry_ref, step + 1, 1 - slot, 1).start()

    fetch("fine_head", head_ref, step, slot, 0).wait()
    fetch("fine_entry", entry_ref, step, slot, 1).wait()
    turned_head[...] = head_ref[slot].T
    turned_entry[...] = entry_ref[slot].T
    row = jnp.broadcast_to(fine_bias_ref[:, aligned(step * block, block, LANES)], (8, block))
    bias_ref[...] = row.T[:, :1]
    pair = 2 * KNOT

    def make(n, place):
        lanes = lanes_of(n)
        back_refs[place][...] = dot(turned_head[...], h3_ref[:, lanes])
        fine_refs[place][...] = dot(turned_entry[...], gfine_ref[:, lanes])

    def finish(n, place):
        lanes = lanes_of(n)
        for at in range(0, block, pair):
            rows = slice(at, at + pair)
            k = step * knots + at // KNOT
            made = jnp.concatenate([interpolate(k + j, p.back, 0, lanes) for j in range(2)], axis=0)
            back = back_refs[place][rows, :] + bias_ref[rows, :]
            residual_ref[rows, lanes] = (history_ref[rows, lanes].astype(F32) - made - back).astype(BF16)
            first = step * pooled + at // POOL
            spread = jnp.concatenate(
                [jnp.broadcast_to(pool_grad[pl.ds(first + j, 1), lanes], (POOL, chunk)) for j in range(pair // POOL)],
                axis=0,
            )
            fine = fine_refs[place][rows, :] + spread
            history_grad_ref[rows, lanes] = (cotangent_ref[rows, lanes].astype(F32) + fine).astype(BF16)

    for n in range(chunks + 1):
        if n < chunks:
            make(n, n % 2)
        if n > 0:
            finish(n - 1, (n - 1) % 2)

    @pl.when(step == steps - 1)
    def _():
        fore_out.wait()


def outputs(plan, packed, history, cotangent, theta, h3, gfine, pool, fine_bias, slices, bias_rows):
    p = plan
    hid, windows = p.hidden, p.windows
    block = 6 * LANES
    steps = -(-p.length // block)
    rows = pl.BlockSpec((block, windows), lambda i: (i, 0))
    wide = p.wide_out - p.low
    per = slices.shape[1]
    square, vector = (per, hid), (1, per)
    grads = []
    for entry, out in ((p.pooled, p.coarse_out), (p.length, p.fine_out)):
        grads += [(per, entry), vector, square, vector, square, vector, (per, out), (1, out)]
    return pl.pallas_call(
        functools.partial(outputs_kernel, p, block, steps),
        grid=(steps,),
        out_shape=(
            jax.ShapeDtypeStruct((p.length, windows), BF16),
            jax.ShapeDtypeStruct((p.length, windows), BF16),
            jax.ShapeDtypeStruct((p.horizon, windows), F32),
        )
        + tuple(jax.ShapeDtypeStruct(shape, F32) for shape in grads),
        in_specs=[ANY, rows, rows, VMEM, VMEM, VMEM, VMEM, VMEM, VMEM, VMEM],
        out_specs=(rows, rows, ANY) + (VMEM,) * len(grads),
        scratch_shapes=[
            pltpu.VMEM((2, hid, block), BF16),
            pltpu.VMEM((2, hid, block), BF16),
            pltpu.VMEM((hid, wide), BF16),
            pltpu.VMEM((p.pool_wide, windows), F32),
            pltpu.VMEM((p.horizon, windows), F32),
            *[pltpu.VMEM((block, min(512, windows)), F32)] * 4,
            pltpu.VMEM((block, hid), BF16),
            pltpu.VMEM((block, hid), BF16),
            pltpu.VMEM((block, 1), F32),
            pltpu.SemaphoreType.DMA((4, 2)),
        ],
        compiler_params=pltpu.CompilerParams(vmem_limit_bytes=56 * MIB),
        cost_estimate=pl.CostEstimate(
            flops=2 * windows * hid * (2 * p.length + p.horizon), bytes_accessed=windows * p.length * 8, transcendentals=0
        ),
    )(packed, history, cotangent, theta, h3, gfine, pool, fine_bias, slices, bias_rows)


def pack(plan, arrays, biases):
    p = plan
    names = sorted(p.at, key=p.at.get)
    ends = [p.at[name] for name in names[1:]] + [p.columns]
    columns = []
    for name, end in zip(names, ends):
        piece = arrays[name] if name != "bias" else biases
        columns.append(jnp.pad(piece.astype(BF16), ((0, 0), (0, end - p.at[name] - piece.shape[1]))))
    return jnp.concatenate(columns, axis=1)


def unpack(plan, slices_ref, bias_rows_ref, grads):
    p = plan
    hid = p.hidden

    def joined(name, out, source, row=None):
        size, done = out.shape[1], 0
        for section in range(p.sections):
            first = p.start(name, section)
            last = min(first + p.rows(name), size)
            if row is not None:
                for at in range(done, last, LANES):
                    width = min(LANES, last - at)
                    out[:, at : at + width] = source[section, pl.ds(row + (at - first) // LANES, 1), :][:, :width]
            elif done < last:
                at = p.slice_at[name] + done - first
                out[:, done:last] = source[section, :, at : at + last - done].astype(F32)
            done = max(done, last)

    def ones_column(name, row):
        section = p.sections - 1
        at = p.slice_at[name] + row - p.start(name, section)
        block = slices_ref[section, :, at // LANES * LANES : at // LANES * LANES + LANES].astype(F32)
        return block.T[at % LANES : at % LANES + 1]

    def own_part(name, out):
        per = out.shape[1]
        width = min(per, LANES)
        share = p.part[name][0]
        for at in range(0, per, width):
            first = lax.axis_index("dp") * per + at
            block = first // LANES
            row = bias_rows_ref[block // share, pl.ds(p.bias_at[name] + block % share, 1), :]
            wide = jnp.broadcast_to(row, (8, LANES))
            out[:, at : at + width] = pltpu.roll(wide, (LANES - first % LANES) % LANES, 1)[:1, :width]

    for base, block in ((0, "coarse_"), (8, "fine_")):
        entry, head = block + "entry", block + "head"
        joined(entry, grads[base], slices_ref)
        grads[base + 1][...] = ones_column(entry, grads[base].shape[1])
        for i, name in enumerate((block + "middle", block + "upper")):
            joined(name, grads[base + 2 + 2 * i], slices_ref)
            own_part(name, grads[base + 3 + 2 * i])
        joined(head, grads[base + 6], slices_ref)
        joined(head, grads[base + 7], bias_rows_ref, p.bias_at[head])


def body(mesh_shape, history, targets, horizon, cotangent, *params):
    (c_entry, c_entry_b, c_middle, c_middle_b, c_upper, c_upper_b, c_head, c_head_b) = params[:8]
    (f_entry, f_entry_b, f_middle, f_middle_b, f_upper, f_upper_b, f_head, f_head_b) = params[8:]
    sections = mesh_shape["section"]
    length, hidden = f_entry.shape[0], c_middle.shape[1]
    p = Plan(
        length, f_head.shape[1] - length, hidden, c_entry.shape[0], c_head.shape[1], sections, history.shape[0]
    )
    pieces = (c_entry.T, c_middle, c_upper, c_head, f_entry.T, f_middle, f_upper, f_head)
    bias_pieces = (c_entry_b, c_middle_b, c_upper_b, f_entry_b, f_middle_b, f_upper_b)
    dp_count, per = mesh_shape["dp"], c_middle.shape[0]
    rows = (history.T, cotangent.T)
    fine_bias = f_head_b[None, :]
    rest = (targets.T, horizon[None, :], c_head_b[None, :], fine_bias)
    groups = dp_count // 2
    if sections == 4 and dp_count % 2 == 0 and per % 64 == 0 and groups > 1:
        theta, h3, gfine, pool, packed, slices, bias_rows = core(
            p, per, groups, *rows, *rest, pieces + tuple(b[None, :] for b in bias_pieces)
        )
    else:
        packed = pack(p, dict(zip(NAMES, pieces)), jnp.stack(bias_pieces, axis=1))
        packed = lax.all_gather(packed, "dp", axis=0, tiled=True)
        theta, h3, gfine, pool, part, head_bias = core(p, per, 0, *rows, *rest, (packed,))
        own = lax.psum_scatter(part.astype(F32), "dp", scatter_dimension=0, tiled=True)
        slices = lax.all_gather(own, "section", axis=0)
        bias_rows = lax.all_gather(lax.psum(head_bias, "dp"), "section", axis=0)
    residual, history_grad, prediction, *grads = outputs(
        p, packed, *rows, theta, h3, gfine, pool, fine_bias, slices, bias_rows
    )
    grads = [g.T if i in (0, 8) else g if g.shape[0] > 1 else g[0] for i, g in enumerate(grads)]
    return (prediction.T, residual.T, history_grad.T) + tuple(grads)


def solution(mesh):
    by_row, by_column, by_entry, copied = P("dp", None), P(None, "dp"), P("dp"), P()
    block = (by_column, by_entry, by_row, by_entry, by_row, by_entry, by_row, copied)
    in_specs = (by_row, by_row, by_entry, by_row) + block + block
    out_specs = (by_row, by_row, by_row) + block + block
    return jax.shard_map(
        functools.partial(body, dict(mesh.shape)), mesh=mesh, in_specs=in_specs, out_specs=out_specs, check_vma=False
    )
```

```python
import functools

import jax
import jax.numpy as jnp
from jax import lax
from jax.experimental import pallas as pl
from jax.experimental.pallas import tpu as pltpu
from jax.sharding import PartitionSpec as P

POOL = 8
KNOT = 24
LANES = 128
ONES = 16
GELU_A = 0.7978845608028654
GELU_B = GELU_A * 0.044715
F32 = jnp.float32
BF16 = jnp.bfloat16
MIB = 1 << 20


def up(size, unit):
    return -(-size // unit) * unit


class Plan:
    def __init__(self, length, horizon, hidden, pooled, coarse_out, sections, windows):
        self.length, self.horizon, self.hidden = length, horizon, hidden
        self.pooled, self.coarse_out = pooled, coarse_out
        self.fine_out = length + horizon
        self.sections, self.windows = sections, windows
        self.back, self.fore = length // KNOT, horizon // KNOT
        self.wide_in, self.wide_out = up(length + 1, LANES), up(self.fine_out + 1, LANES)
        self.pool_wide, self.theta_wide = up(pooled + 1, LANES), up(coarse_out + 1, LANES)
        widths = [
            ("coarse_entry", self.pool_wide),
            ("coarse_middle", hidden),
            ("coarse_upper", hidden),
            ("coarse_head", self.theta_wide),
            ("bias", LANES),
            ("fine_entry", self.wide_in),
            ("fine_middle", hidden),
            ("fine_upper", hidden),
            ("fine_head", self.wide_out),
        ]
        self.at, place = {}, 0
        for name, width in widths:
            self.at[name] = place
            place += width
        self.columns = place
        self.low = length // LANES * LANES
        self.skip = length - self.low
        self.square = hidden // sections
        self.slice_at, self.part, place = {}, {}, 0
        for name, width in (
            ("head_back", self.wide_in),
            ("head_fore", self.wide_out - self.low),
            ("fine_upper", hidden),
            ("fine_middle", hidden),
            ("fine_entry", self.wide_in),
            ("coarse_middle", hidden),
            ("coarse_upper", hidden),
            ("coarse_head", self.theta_wide),
            ("coarse_entry", self.pool_wide),
        ):
            self.slice_at[name] = place
            total = width // LANES
            share = -(-total // sections)
            self.part[name] = share, total
            place += share * LANES
        self.slice_columns = place
        self.bias_at, place = {}, 0
        for name in ("head_back", "head_fore", "coarse_head", "coarse_middle", "coarse_upper", "fine_middle", "fine_upper"):
            self.bias_at[name] = place
            place += self.part[name][0]
        self.bias_rows = up(place, 8)
        self.knot_rows = up(coarse_out, ONES)
        self.pair = 2 * KNOT
        self.r1_pairs = -(-(self.rows("fine_entry") + self.pair - ONES) // self.pair)

    def rows(self, name):
        return self.part[name][0] * LANES

    def start(self, name, section):
        low = min if isinstance(section, int) else jnp.minimum
        share, total = self.part[name]
        return low(section * share, total - share) * LANES


def gelu_both(a):
    square = a * a
    v = 0.5 + 0.5 * jnp.tanh(a * (GELU_A + GELU_B * square))
    h = a * v
    return h, v + h * (1.0 - v) * (2.0 * GELU_A + (6.0 * GELU_B) * square)


def dot(a, b):
    return jnp.dot(a, b, preferred_element_type=F32)


def dot_rows(a, b):
    return lax.dot_general(a, b, (((1,), (1,)), ((), ())), preferred_element_type=F32)


def aligned(start, size, unit):
    return pl.ds(pl.multiple_of(start, unit), size)


def column_of(row_ref, first, count):
    size = row_ref.shape[1]
    columns = []
    for at in range(first, first + count, LANES):
        width = max(0, min(LANES, size - at))
        row = jnp.zeros((1, LANES), F32) if width == 0 else row_ref[:, at : at + width]
        if 0 < width < LANES:
            row = jnp.concatenate([row, jnp.zeros((1, LANES - width), F32)], axis=1)
        columns.append(jnp.broadcast_to(row, (LANES, LANES)).T[:, :1])
    return jnp.concatenate(columns, axis=0)


def hat_weights(first, count, plan, turned=False, fore=False):
    p = plan
    shape = (p.knot_rows, count) if turned else (count, p.theta_wide)
    row = lax.broadcasted_iota(jnp.int32, shape, 1 if turned else 0) + first
    knot = lax.broadcasted_iota(jnp.int32, shape, 0 if turned else 1)
    away = row - KNOT * knot
    weight = jnp.maximum(KNOT - jnp.abs(away), 0)
    last = (knot == p.back - 1) | (knot == p.back + p.fore - 1)
    weight = jnp.where(last & (away > 0) & (away < KNOT), KNOT, weight)
    own = (knot >= p.back) & (row >= p.length) if fore else (knot < p.back) & (row < p.length)
    inside = own & (row < p.fine_out) & (knot < p.back + p.fore)
    return jnp.where(inside, weight, 0).astype(F32).astype(BF16)


def fractions(width):
    later = lax.broadcasted_iota(jnp.int32, (KNOT, width), 0).astype(F32) * (1.0 / KNOT)
    return 1.0 - later, later


NAMES = (
    "coarse_entry",
    "coarse_middle",
    "coarse_upper",
    "coarse_head",
    "fine_entry",
    "fine_middle",
    "fine_upper",
    "fine_head",
)
KEPT = ("fine_entry", "fine_head")


def remote(source, target, send_sem, recv_sem, place):
    return pltpu.make_async_remote_copy(
        src_ref=source,
        dst_ref=target,
        send_sem=send_sem,
        recv_sem=recv_sem,
        device_id=place,
        device_id_type=pl.DeviceIdType.MESH,
    )


def signal(semaphore, places):
    for place in places:
        pl.semaphore_signal(semaphore, inc=1, device_id=place, device_id_type=pl.DeviceIdType.MESH)


class Ways:
    def __init__(self, groups):
        self.section, self.dp = lax.axis_index("section"), lax.axis_index("dp")
        self.group, self.core = self.dp // 2, self.dp % 2
        self.groups = groups
        self.partner = (self.section, self.group * 2 + 1 - self.core)
        s = self.section
        self.side = [s + 1 - 2 * (s % 2), (s + 2) % 4]
        self.sides = [(t, self.dp) for t in self.side]
        self.across = 3 - s

    def far(self, j):
        group = (self.group + j) % self.groups
        return group, (self.section, group * 2 + self.core)

    def from_far(self, j):
        return (self.group + self.groups - j) % self.groups

    def all(self):
        return [self.partner] + self.sides + [self.far(j)[1] for j in range(1, self.groups)]


class Gather:
    def __init__(self, plan, way, per, cuts, w_ref, shards, biases, send, recv, partner_recv):
        self.p, self.way, self.per, self.cuts, self.w_ref = plan, way, per, cuts, w_ref
        self.shards, self.biases = shards, biases
        self.send, self.recv, self.partner_recv = send, recv, partner_recv
        self.near = range(1, way.groups)
        self.chunks, self.ahead = len(cuts) - 1, 3

    def at(self, k, owner, s=None):
        quarter = self.per // 4
        rows = aligned(owner * self.per, self.per, self.per)
        if s is not None:
            rows = aligned(owner * self.per + s * quarter, quarter, quarter)
        return self.w_ref.at[rows, self.cuts[k] : self.cuts[k + 1]]

    def source(self, j):
        return self.way.from_far(j) * 2 + self.way.core

    def copy(self, here, k, j, kind, place):
        return remote(here, here, self.send.at[k, j - 1, kind], self.recv.at[k, j - 1, kind], place)

    def to_far(self, k, j):
        return self.copy(self.at(k, self.way.dp, self.way.section), k, j, 0, self.way.far(j)[1])

    def to_side(self, k, j, i):
        return self.copy(self.at(k, self.source(j), self.way.section), k, j, 1 + i, self.way.sides[i])

    def to_across(self, k, j):
        i = (k + j) % 2
        return self.copy(self.at(k, self.source(j), self.way.side[i]), k, j, 3, self.way.sides[1 - i])

    def to_partner(self, k, j):
        here = self.at(k, self.source(j) if j else self.way.dp)
        return remote(here, here, self.send.at[k, max(j - 1, 0), 4 if j else 5], self.partner_recv.at[k, j], self.way.partner)

    def arrived(self, k, j, kind):
        s = [self.way.section, self.way.side[0], self.way.side[1], self.way.across][kind]
        self.copy(self.at(k, self.source(j), s), k, j, kind, self.way.partner).wait_recv()

    def cast(self, k):
        p, own = self.p, aligned(self.way.dp * self.per, self.per, self.per)
        low, high = self.cuts[k], self.cuts[k + 1]
        for ref, name in zip(self.shards, NAMES):
            at, size = p.at[name], ref.shape[1]
            wide = up(size + 1, LANES) if name.endswith(("entry", "head")) else size
            first, last = max(at, low), min(at + wide, high)
            full = min(last, at + size // LANES * LANES)
            if first < full:
                self.w_ref[own, first:full] = ref[:, first - at : full - at].astype(BF16)
            if first < last and last > full:
                rest = ref[:, full - at : size].astype(BF16)
                pad = jnp.zeros((self.per, last - at - size), BF16)
                self.w_ref[own, full:last] = jnp.concatenate([rest, pad], axis=1)
        at = p.at["bias"]
        if low <= at < high:
            count = len(self.biases)
            rows = jnp.concatenate([ref[...] for ref in self.biases] + [jnp.zeros((8 - count, self.per), F32)], axis=0)
            wide = jnp.concatenate([rows, jnp.zeros((8, LANES - self.per), F32)], axis=1)
            wide = jnp.concatenate([wide, jnp.zeros((LANES - 8, LANES), F32)], axis=0)
            self.w_ref[own, at : at + LANES] = wide.T[: self.per].astype(BF16)

    def first(self, k):
        self.cast(k)
        for j in self.near:
            self.to_far(k, j).start()
        self.to_partner(k, 0).start()

    def second(self, k):
        for j in self.near:
            self.arrived(k, j, 0)
            for i in range(2):
                self.to_side(k, j, i).start()

    def third(self, k):
        for j in self.near:
            self.arrived(k, j, 1)
            self.arrived(k, j, 2)
            self.to_across(k, j).start()

    def fourth(self, k):
        for j in self.near:
            self.arrived(k, j, 3)
            self.to_partner(k, j).start()

    def complete(self, k):
        for j in range(self.way.groups):
            there = (self.way.from_far(j) * 2 + 1 - self.way.core) if j else self.way.partner[1]
            here = self.at(k, there)
            remote(here, here, self.send.at[k, 0, 5], self.partner_recv.at[k, j], self.way.partner).wait_recv()

    def sent(self, k):
        for j in self.near:
            for copy in (self.to_far(k, j), self.to_side(k, j, 0), self.to_side(k, j, 1), self.to_across(k, j)):
                copy.wait_send()
            self.to_partner(k, j).wait_send()
        self.to_partner(k, 0).wait_send()


class Reduce:
    def __init__(self, plan, way, per, cuts, part_ref, core_in, far_in, far_out, stage_ref, out_ref, send, recv, local):
        self.p, self.way, self.per, self.cuts = plan, way, per, cuts
        self.part_ref, self.core_in, self.far_in, self.far_out = part_ref, core_in, far_in, far_out
        self.stage_ref, self.out_ref, self.send, self.recv, self.local = stage_ref, out_ref, send, recv, local
        self.near = range(1, way.groups)
        self.chunks = len(cuts) - 1

    def columns(self, k):
        return slice(self.cuts[k], self.cuts[k + 1])

    def to_partner(self, k, g):
        return remote(
            self.part_ref(g * 2 + 1 - self.way.core, k),
            self.core_in(g, k),
            self.send.at[k, g, 0],
            self.recv.at[k, g, 0],
            self.way.partner,
        )

    def to_far(self, k, j):
        here, there = self.far_out(j - 1, k), self.far_in(j - 1, k)
        return remote(here, there, self.send.at[k, j - 1, 1], self.recv.at[k, j - 1, 1], self.way.far(j)[1])

    def side(self, k, source, i, to):
        here = self.out_ref.at[source, :, self.columns(k)]
        return remote(here, here, self.send.at[k, i, 2], self.recv.at[k, i, 2], to)

    def to_side(self, k, i):
        here = self.stage_ref.at[:, self.columns(k)]
        there = self.out_ref.at[self.way.section, :, self.columns(k)]
        return remote(here, there, self.send.at[k, i, 2], self.recv.at[k, i, 2], self.way.sides[i])

    def keep(self, k):
        there = self.out_ref.at[self.way.section, :, self.columns(k)]
        return pltpu.make_async_copy(self.stage_ref.at[:, self.columns(k)], there, self.local.at[k])

    def to_across(self, k):
        i = k % 2
        return self.side(k, self.way.side[i], 2, self.way.sides[1 - i])

    def summed(self, k, group):
        own = self.part_ref(group * 2 + self.way.core, k)[...].astype(F32)
        return own + self.core_in(group, k)[...].astype(F32)

    def first(self, k):
        for g in range(self.way.groups):
            self.to_partner(k, g).start()

    def second(self, k):
        for g in range(self.way.groups):
            self.to_partner(k, g).wait_recv()
        for j in self.near:
            self.far_out(j - 1, k)[...] = self.summed(k, self.way.far(j)[0]).astype(BF16)
            self.to_far(k, j).start()

    def third(self, k):
        total = self.summed(k, self.way.group)
        for j in self.near:
            self.to_far(k, j).wait_recv()
            total += self.far_in(j - 1, k)[...].astype(F32)
        self.stage_ref[:, self.columns(k)] = total.astype(BF16)
        for i in range(2):
            self.to_side(k, i).start()
        self.keep(k).start()

    def fourth(self, k):
        i = k % 2
        for turn in (i, 1 - i):
            self.side(k, self.way.side[turn], turn, self.way.sides[turn]).wait_recv()
            if turn == i:
                self.to_across(k).start()

    def complete(self, k):
        self.side(k, self.way.across, 2, self.way.partner).wait_recv()

    def sent_far(self, k):
        for j in self.near:
            self.to_far(k, j).wait_send()

    def sent(self, k):
        for g in range(self.way.groups):
            self.to_partner(k, g).wait_send()
        for i in range(2):
            self.to_side(k, i).wait_send()
        self.to_across(k).wait_send()
        self.keep(k).wait()


class ReduceBias:
    def __init__(self, way, own_ref, core_in, far_ref, out_ref, send, recv):
        self.way, self.own_ref, self.core_in, self.far_ref, self.out_ref = way, own_ref, core_in, far_ref, out_ref
        self.send, self.recv = send, recv
        self.near = range(1, way.groups)

    def copy(self, here, there, n, place):
        return remote(here, there, self.send.at[n], self.recv.at[n], place)

    def to_partner(self):
        return self.copy(self.own_ref, self.core_in, 0, self.way.partner)

    def to_far(self, j):
        here = self.far_ref.at[self.way.group]
        return self.copy(here, here, j, self.way.far(j)[1])

    def side(self, source, n, to):
        here = self.out_ref.at[source]
        return self.copy(here, here, self.way.groups + n, to)

    def to_across(self):
        return self.side(self.way.side[0], 2, self.way.sides[1])

    def second(self):
        self.to_partner().wait_recv()
        self.far_ref[self.way.group] = self.own_ref[...] + self.core_in[...]
        for j in self.near:
            self.to_far(j).start()

    def third(self):
        for j in self.near:
            here = self.far_ref.at[self.way.from_far(j)]
            self.copy(here, here, j, self.way.partner).wait_recv()
        total = self.far_ref[0]
        for g in range(1, self.way.groups):
            total += self.far_ref[g]
        self.out_ref[self.way.section] = total
        for i in range(2):
            self.side(self.way.section, i, self.way.sides[i]).start()

    def fourth(self):
        self.side(self.way.side[0], 0, self.way.partner).wait_recv()
        self.to_across().start()
        self.side(self.way.side[1], 1, self.way.partner).wait_recv()

    def complete(self):
        self.side(self.way.across, 2, self.way.partner).wait_recv()
        self.to_partner().wait_send()
        for j in self.near:
            self.to_far(j).wait_send()
        for i in range(2):
            self.side(self.way.section, i, self.way.sides[i]).wait_send()
        self.to_across().wait_send()


def core_kernel(plan, per, groups, *refs):
    p = plan
    refs = list(refs)
    take = lambda count: [refs.pop(0) for _ in range(count)]
    history_ref, cotangent_ref, target_ref, horizon_ref, coarse_bias_ref, fine_bias_ref = take(6)
    if groups:
        shards_in = take(14)
    else:
        (packed_ref,) = take(1)
    theta_out, h3_out, gfine_out, pool_out = take(4)
    if groups:
        kept_out, slices_out, bias_out = take(3)
    else:
        slice_out, bias_out = take(2)
    w_ref, big_ref = take(2)
    h_refs, g_refs = take(6), take(6)
    r1_ref, pooled_ref, split_ref, theta_ref, gtheta_ref, gknot_ref = take(6)
    pw_ref, pwt_ref, turned_ref, even_ref, odd_ref, bias_ref = take(6)
    horizon_buf, coarse_bias_buf, fine_bias_buf, sems = take(4)
    if groups:
        shards = take(14)
        shard_sems, send, recv, partner_recv = take(4)
        head_bias_ref, bias_in, bias_far, stage_ref, ready, reduce_send, reduce_recv, bias_send, bias_recv = take(9)
        keep_sems = take(1)[0]
    else:
        head_bias_ref = bias_out
    hid, windows = p.hidden, p.windows
    section = lax.axis_index("section")
    chunk = min(512, windows // 2)
    chunks = windows // chunk
    H = slice(0, hid)
    lanes_of = lambda n: aligned(n * chunk, chunk, chunk)
    place = p.at["fine_entry"]
    head_at = p.at["fine_head"]

    load = lambda source, out, sem: pltpu.make_async_copy(source, out, sems.at[sem])
    history_in = load(history_ref, big_ref.at[: p.length], 1)
    cotangent_in = load(cotangent_ref, big_ref.at[: p.length], 2)
    target_in = load(target_ref, big_ref.at[p.length : p.fine_out], 0)
    rows_in = [
        load(horizon_ref, horizon_buf, 3),
        load(coarse_bias_ref, coarse_bias_buf, 4),
        load(fine_bias_ref, fine_bias_buf, 5),
    ]
    theta_copy = load(theta_ref, theta_out, 6)
    h3_copy = load(h_refs[5].at[H], h3_out, 7)
    gfine_copy = load(g_refs[3], gfine_out, 8)
    pool_copy = load(pooled_ref, pool_out, 9)

    if groups:
        shards_load = [
            pltpu.make_async_copy(source, out, shard_sems.at[n]) for n, (source, out) in enumerate(zip(shards_in, shards))
        ]
        order = [0, 1, 2, 3, 8, 9, 10, 11, 12, 13, 4, 5, 6, 7]
        for n in order:
            shards_load[n].start()
        way = Ways(groups)
        middle = p.at["fine_middle"]
        third = (p.columns - middle) // 3 // LANES * LANES
        entry_cut = place + up((middle - place) // 2, LANES)
        cuts = (0, 2 * hid, place, entry_cut, middle, middle + third, middle + 2 * third, p.columns)
        gather = Gather(p, way, per, cuts, w_ref, shards[:8], shards[8:], send, recv, partner_recv)
        cotangent_in.start()
        for copy in rows_in:
            copy.start()
        barrier = pltpu.get_barrier_semaphore()
        signal(barrier, way.all())
        for n in order[:10]:
            shards_load[n].wait()
        pl.semaphore_wait(barrier, len(way.all()))
        gather.first(0)
        for n in order[10:]:
            shards_load[n].wait()
        for k in range(1, gather.ahead):
            gather.first(k)
    else:
        weights_in = load(packed_ref, w_ref, 10)
        weights_in.start()
        cotangent_in.start()
        for copy in rows_in:
            copy.start()

    def move(*steps):
        if groups:
            for stage, k in steps:
                {2: gather.second, 3: gather.third, 4: gather.fourth}[stage](k)
                if stage == 2 and k + gather.ahead < gather.chunks:
                    gather.first(k + gather.ahead)

    def complete(*ks):
        if groups:
            for k in ks:
                gather.complete(k)

    tail = p.wide_out - p.length
    mark = lax.broadcasted_iota(jnp.int32, (tail, windows), 0) < POOL
    big_ref[p.length :, :] = mark.astype(F32).astype(BF16)
    pooled_ref[...] = jnp.zeros_like(pooled_ref)
    for index in range(6):
        h_refs[index][hid:, :] = jnp.ones((ONES, windows), BF16)
    for copy in rows_in:
        copy.wait()
    step = 6 * LANES

    def adjoint(first, count, fore):
        hats = hat_weights(first, count, p, True, fore)

        @pl.loop(0, chunks)
        def _(n):
            lanes = lanes_of(n)
            rows = slice(first, first + count) if isinstance(first, int) else aligned(first, count, ONES)
            gtheta_ref[:, lanes] += dot(hats, big_ref[rows, lanes]) * (-1.0 / KNOT)

    cotangent_in.wait()
    gtheta_ref[...] = jnp.zeros_like(gtheta_ref)
    quarter = p.wide_in // 4
    pl.loop(0, 4)(lambda i: adjoint(i * quarter, quarter, False))
    history_in.start()
    move((2, 0), (2, 1), (3, 0))
    history_in.wait()

    unit = hid
    shape = (unit // POOL, unit)
    member = lax.broadcasted_iota(jnp.int32, shape, 1) - POOL * lax.broadcasted_iota(jnp.int32, shape, 0)
    turned_ref[: unit // POOL, :] = ((member >= 0) & (member < POOL)).astype(F32).astype(BF16)
    firsts = list(range(0, p.wide_in, unit))
    for number, first in enumerate(firsts):
        count = min(unit, p.wide_in - first)
        rows = slice(first // POOL, (first + count) // POOL)

        @pl.loop(0, chunks)
        def _(n):
            lanes = lanes_of(n)
            total = dot(turned_ref[: count // POOL, :count], big_ref[first : first + count, lanes])
            pooled_ref[rows, lanes] = (total * (1.0 / POOL)).astype(BF16)

        if number == len(firsts) // 2:
            move((4, 0), (3, 1), (2, 2))
    move((4, 1), (3, 2), (2, 3))
    complete(0, 1)
    if not groups:
        weights_in.wait()
    fore_parts = [(0, 8 * p.pair), (8 * p.pair, p.horizon)]
    fore_bias = column_of(fine_bias_buf, p.low, p.wide_out - p.low)
    placed = w_ref[:, p.at["bias"] : p.at["bias"] + LANES].astype(F32)
    lane = lax.broadcasted_iota(jnp.int32, (hid, LANES), 1)
    for number, (low, high) in enumerate(fore_parts):
        column = fore_bias[p.skip + low : p.skip + high]
        column = jnp.concatenate([column, jnp.zeros((hid - high + low, 1), F32)], axis=0)
        placed = jnp.where(lane == 6 + number, column, placed)
    bias_ref[...] = placed

    def pipeline(*layers):
        tile, pending = 0, nothing
        for before, produce, finish, after in layers:
            before()
            for n in range(chunks):
                lanes = slice(n * chunk, (n + 1) * chunk)
                out = (even_ref, odd_ref)[tile % 2]
                value = produce(lanes)
                out[: value.shape[0], :] = value
                pending()
                pending = functools.partial(finish, out, lanes)
                tile += 1
            after()
        pending()

    def nothing():
        pass

    def looped(*layers):
        for before, produce, finish, after in layers:
            before()

            @pl.loop(0, chunks)
            def _(n, produce=produce, finish=finish):
                value = produce(lanes_of(n))
                even_ref[: value.shape[0], :] = value
                finish(even_ref, lanes_of(n))

            after()

    def turn_weight(first, count):
        turned_ref[:count, :] = w_ref[:, first : first + count].T

    strip = ONES

    def activate(index):
        def finish(source, lanes):
            for r in range(0, hid, strip):
                rows = slice(r, r + strip)
                h, slope = gelu_both(source[rows, :] + bias_ref[rows, index : index + 1])
                h_refs[index][rows, lanes] = h.astype(BF16)
                g_refs[index][rows, lanes] = slope.astype(BF16)

        return finish

    def hidden(name, index, after=nothing):
        return (
            lambda: turn_weight(p.at[name], hid),
            lambda lanes: dot(turned_ref[H, :], h_refs[index - 1][H, lanes]),
            activate(index),
            after,
        )

    at_entry = p.at["coarse_entry"]
    at_head = p.at["coarse_head"]
    theta_bias = column_of(coarse_bias_buf, 0, p.theta_wide)

    def keep_theta(source, lanes):
        for r in range(0, p.theta_wide, strip):
            rows = slice(r, r + strip)
            theta = source[rows, :] + theta_bias[rows]
            if r < p.knot_rows:
                theta_ref[rows, lanes] = theta
            knots = jnp.where(lax.broadcasted_iota(jnp.int32, theta.shape, 0) + r < p.back, theta, 0.0)
            high = knots.astype(BF16)
            split_ref[rows, lanes] = high
            split_ref[p.theta_wide + r : p.theta_wide + r + strip, lanes] = (knots - high.astype(F32)).astype(BF16)

    forward = pipeline if groups else looped
    forward(
        (
            nothing,
            lambda lanes: dot(w_ref[:, at_entry : at_entry + p.pool_wide], pooled_ref[:, lanes]),
            activate(0),
            nothing,
        ),
        hidden("coarse_middle", 1, lambda: move((4, 2), (2, 4))),
        hidden("coarse_upper", 2, lambda: move((3, 3))),
        (
            lambda: turn_weight(at_head, p.theta_wide),
            lambda lanes: dot(turned_ref[: p.theta_wide, :], h_refs[2][H, lanes]),
            keep_theta,
            nothing,
        ),
    )
    theta_copy.start()

    def keep(name, wide, sem):
        columns = slice(p.at[name], p.at[name] + wide)
        return load(w_ref.at[:, columns], kept_out.at[:, columns], sem)

    first_pair = p.start("fine_entry", section) // p.pair

    def interpolate(base, count, k, rest, later, lanes):
        own = theta_ref[pl.ds(base + jnp.minimum(k, count - 1), 1), lanes]
        after = theta_ref[pl.ds(base + jnp.minimum(k + 1, count - 1), 1), lanes]
        return own * rest + after * later

    everything = slice(0, windows)
    rest, later = fractions(windows)

    @pl.loop(0, p.r1_pairs)
    def _(i):
        pair = first_pair + i
        source = aligned(pair * p.pair, p.pair, ONES)
        made = jnp.concatenate(
            [interpolate(0, p.back, 2 * pair + j, rest, later, everything) for j in range(2)], axis=0
        )
        made = made * (pair < p.back // 2).astype(F32)
        r1_ref[aligned(i * p.pair, p.pair, ONES), :] = (big_ref[source, :].astype(F32) - made).astype(BF16)

    move((4, 3), (2, 5), (3, 4))
    complete(2, 3)
    kept = []
    if groups:
        kept.append(keep("fine_entry", p.wide_in, 10))
        kept[0].start()

    total = jnp.zeros((hid, p.theta_wide), F32)
    for first in range(0, p.wide_in, step):
        count = min(step, p.wide_in - first)
        total += dot(w_ref[:, place + first : place + first + count], hat_weights(first, count, p))
    product = (total * (1.0 / KNOT)).astype(BF16)
    pwt_ref[...] = product
    pw_ref[...] = product.T
    move((4, 4), (2, 6), (3, 5))

    def fine_entry(lanes):
        a = dot(w_ref[:, place : place + p.wide_in], big_ref[: p.wide_in, lanes])
        for part in (0, p.theta_wide):
            a -= dot(pwt_ref[...], split_ref[part : part + p.theta_wide, lanes])
        return a

    def entry_made():
        cotangent_in.start()
        target_in.start()
        big_ref[p.fine_out :, :] = jnp.zeros((p.wide_out - p.fine_out, windows), BF16)
        if groups:
            signal(ready.at[0], way.all())
        move((4, 5), (3, 6))
        complete(4)

    rest_c, later_c = fractions(chunk)

    def fore(number):
        low, high = fore_parts[number]

        def before():
            first = head_at + p.low + low
            turned = w_ref[:, first : first + up(high - low + p.skip, LANES)].T
            turned_ref[: high - low, :] = turned[p.skip : p.skip + high - low]

        def finish(source, lanes):
            for k in range(low // KNOT, high // KNOT, 2):
                here = slice(k * KNOT - low, (k + 2) * KNOT - low)
                second = source[here, :] + bias_ref[here, 6 + number : 7 + number]
                first = jnp.concatenate(
                    [interpolate(p.back, p.fore, k + j, rest_c, later_c, lanes) for j in range(2)], axis=0
                )
                counts = (lax.broadcasted_iota(jnp.int32, (2 * KNOT, chunk), 0) + k * KNOT) < horizon_buf[:, lanes]
                there = slice(p.length + k * KNOT, p.length + (k + 2) * KNOT)
                error = first + second - big_ref[there, lanes].astype(F32)
                big_ref[there, lanes] = jnp.where(counts, -error, 0.0).astype(BF16)

        return before, lambda lanes: dot(turned_ref[: high - low, :], h_refs[5][H, lanes]), finish, nothing

    looped((nothing, fine_entry, activate(3), entry_made))
    forward(hidden("fine_middle", 4, lambda: move((4, 6))), hidden("fine_upper", 5))
    h3_copy.start()
    cotangent_in.wait()
    target_in.wait()

    def gradient_slice(name, left, right_ref, first, step=LANES, sign=1.0):
        left_ref = left if name.endswith("entry") else h_refs[left]

        def part(b):
            value = sign * dot_rows(left_ref[...], right_ref[aligned(first + b * step, step, ONES), :])
            w_ref[:, aligned(place + p.slice_at[name] + b * step, step, LANES)] = value[:hid].astype(BF16)
            if name in p.bias_at:
                for c in range(step // LANES):
                    row = p.bias_at[name] + b * (step // LANES) + c
                    head_bias_ref[pl.ds(row, 1), :] = value[hid : hid + 1, c * LANES : (c + 1) * LANES]

        count = p.rows(name) // step
        if count > 1:
            pl.loop(0, count)(part)
        else:
            part(0)

    def square_slice(name, index):
        gradient_slice(name, index - 1, g_refs[index], p.start(name, section))

    def back(index, product, after=nothing):
        def finish(source, lanes):
            for r in range(0, hid, strip):
                rows = slice(r, r + strip)
                g_refs[index][rows, lanes] = (source[rows, :] * g_refs[index][rows, lanes].astype(F32)).astype(BF16)

        return nothing, product, finish, after

    def times(name, index):
        at = p.at[name]
        return lambda lanes: dot(w_ref[:, at : at + hid], g_refs[index][:, lanes])

    if groups:
        cuts = (0, p.slice_at["head_fore"], p.slice_at["fine_entry"], p.slice_at["coarse_middle"], p.slice_columns)
        width = lambda k: cuts[k + 1] - cuts[k]

        def arrivals(row, k):
            rows = slice(row * per, (row + 1) * per) if isinstance(row, int) else aligned(row * per, per, per)
            if k == 0:
                return split_ref.at[rows, : width(0)]
            first = head_at + cuts[k] - cuts[1]
            return w_ref.at[rows, first : first + width(k)]

        def departures(j, k):
            if k == 0:
                return gknot_ref.at[j * per : (j + 1) * per, : width(0)]
            first = (k * groups + j) * per
            return big_ref.at[first : first + per, : width(k)]

        reduce = Reduce(
            p,
            way,
            per,
            cuts,
            lambda owner, k: w_ref.at[aligned(owner * per, per, per), place + cuts[k] : place + cuts[k + 1]],
            arrivals,
            lambda j, k: arrivals(groups + j, k),
            departures,
            stage_ref,
            slices_out,
            reduce_send,
            reduce_recv,
            keep_sems,
        )
        reduce_bias = ReduceBias(way, head_bias_ref, bias_in, bias_far, bias_out, bias_send, bias_recv)
        kept[0].wait()
        gather.sent(2)
        gather.sent(3)

    gradient_slice("head_back", 5, big_ref, p.start("head_back", section), 2 * LANES, -1.0)
    if groups:
        pl.semaphore_wait(ready.at[0], len(way.all()))
        reduce.first(0)
    complete(5, 6)
    looped(fore(0), fore(1))
    if groups:
        kept.append(keep("fine_head", p.wide_out, 11))
        kept[1].start()
        reduce.second(0)

    adjoint(p.low, p.wide_out - p.low, True)
    looped(back(5, lambda lanes: -dot(w_ref[:, head_at : head_at + p.wide_out], big_ref[:, lanes])))
    if groups:
        kept[1].wait()
        for k in (0, 1, 4, 5, 6):
            gather.sent(k)
        signal(ready.at[1], way.all())
    looped(back(4, times("fine_upper", 5)))
    gradient_slice("head_fore", 5, big_ref, p.start("head_fore", section) + p.low, LANES, -1.0)
    square_slice("fine_upper", 5)
    square_slice("fine_middle", 4)
    if groups:
        pl.semaphore_wait(ready.at[1], len(way.all()))
        reduce.first(1)
    looped(back(3, times("fine_middle", 4)))
    gfine_copy.start()
    gradient_slice("fine_entry", g_refs[3], r1_ref, p.start("fine_entry", section) - first_pair * p.pair, 2 * LANES)
    if groups:
        reduce.first(2)
        reduce.second(1)
        reduce.third(0)
        reduce.sent_far(0)
    gknot_ref[p.knot_rows :, :] = jnp.zeros((p.theta_wide - p.knot_rows, windows), BF16)

    def knots_done(source, lanes):
        for r in range(0, p.knot_rows, strip):
            rows = slice(r, r + strip)
            gknot_ref[rows, lanes] = (gtheta_ref[rows, lanes] - source[rows, :]).astype(BF16)

    looped(
        (nothing, lambda lanes: dot(pw_ref[: p.knot_rows, :], g_refs[3][:, lanes]), knots_done, nothing),
        back(2, lambda lanes: dot(w_ref[:, at_head : at_head + p.theta_wide], gknot_ref[:, lanes])),
    )
    if groups:
        reduce.second(2)
    looped(back(1, times("coarse_upper", 2)))
    if groups:
        reduce.fourth(0)
    looped(back(0, times("coarse_middle", 1)))
    gradient_slice("coarse_head", 2, gknot_ref, p.start("coarse_head", section))
    gradient_slice("coarse_entry", g_refs[0], pooled_ref, p.start("coarse_entry", section))
    square_slice("coarse_middle", 1)
    square_slice("coarse_upper", 2)
    if groups:
        reduce.first(3)
        reduce_bias.to_partner().start()
        reduce.third(1)
        reduce.second(3)
        reduce_bias.second()

    def pool_gradient(source, lanes):
        for r in range(0, p.pool_wide, strip):
            pooled_ref[r : r + strip, lanes] = (source[r : r + strip, :] * (1.0 / POOL)).astype(BF16)

    looped(
        (
            lambda: turn_weight(at_entry, p.pool_wide),
            lambda lanes: dot(turned_ref[: p.pool_wide, :], g_refs[0][:, lanes]),
            pool_gradient,
            nothing,
        )
    )
    pool_copy.start()
    if groups:
        reduce.fourth(1)
        reduce_bias.third()
        reduce.third(2)
        reduce_bias.fourth()
        reduce.third(3)
        reduce.fourth(2)
        reduce.fourth(3)
        for k in range(reduce.chunks):
            reduce.complete(k)
            reduce.sent(k)
            if k > 0:
                reduce.sent_far(k)
        reduce_bias.complete()
    else:
        out = load(w_ref.at[:, place : place + p.slice_columns], slice_out, 10)
        out.start()
        out.wait()
    theta_copy.wait()
    h3_copy.wait()
    gfine_copy.wait()
    pool_copy.wait()


ANY = pl.BlockSpec(memory_space=pl.ANY)
VMEM = pl.BlockSpec(memory_space=pltpu.VMEM)


def core(plan, per, groups, history, cotangent, targets, horizon, coarse_bias, fine_bias, weights):
    p = plan
    hid, windows = p.hidden, p.windows
    flops = 2 * windows * hid * (2 * p.length + 2 * p.wide_out // 3 + 12 * hid + p.slice_columns)
    out_shape = [
        jax.ShapeDtypeStruct((p.knot_rows, windows), F32),
        jax.ShapeDtypeStruct((hid, windows), BF16),
        jax.ShapeDtypeStruct((hid, windows), BF16),
        jax.ShapeDtypeStruct((p.pool_wide, windows), BF16),
    ]
    out_specs = [ANY] * 4
    scratch = [
        pltpu.VMEM((hid, p.columns), BF16),
        pltpu.VMEM((p.wide_out, windows), BF16),
        *[pltpu.VMEM((hid + ONES, windows), BF16)] * 6,
        *[pltpu.VMEM((hid, windows), BF16)] * 6,
        pltpu.VMEM((p.r1_pairs * p.pair, windows), BF16),
        pltpu.VMEM((p.pool_wide, windows), BF16),
        pltpu.VMEM((2 * p.theta_wide, windows), BF16),
        pltpu.VMEM((p.knot_rows, windows), F32),
        pltpu.VMEM((p.knot_rows, windows), F32),
        pltpu.VMEM((p.theta_wide, windows), BF16),
        pltpu.VMEM((p.theta_wide, hid), BF16),
        pltpu.VMEM((hid, p.theta_wide), BF16),
        pltpu.VMEM((hid, hid), BF16),
        pltpu.VMEM((hid, min(512, windows // 2)), F32),
        pltpu.VMEM((hid, min(512, windows // 2)), F32),
        pltpu.VMEM((hid, LANES), F32),
        pltpu.VMEM(horizon.shape, jnp.int32),
        pltpu.VMEM(coarse_bias.shape, F32),
        pltpu.VMEM(fine_bias.shape, F32),
        pltpu.SemaphoreType.DMA((13,)),
    ]
    params = {}
    if groups:
        bias = (p.bias_rows, LANES)
        out_shape += [
            jax.ShapeDtypeStruct((hid, p.columns), BF16),
            jax.ShapeDtypeStruct((4, per, p.slice_columns), BF16),
            jax.ShapeDtypeStruct((4,) + bias, F32),
        ]
        out_specs += [ANY, ANY, VMEM]
        chunks, reduce_chunks = 7, 4
        scratch += [pltpu.VMEM(piece.shape, F32) for piece in weights]
        scratch += [
            pltpu.SemaphoreType.DMA((len(weights),)),
            pltpu.SemaphoreType.DMA((chunks, groups - 1, 6)),
            pltpu.SemaphoreType.DMA((chunks, groups - 1, 4)),
            pltpu.SemaphoreType.DMA((chunks, groups)),
            pltpu.VMEM(bias, F32),
            pltpu.VMEM(bias, F32),
            pltpu.VMEM((groups,) + bias, F32),
            pltpu.VMEM((per, p.slice_columns), BF16),
            pltpu.SemaphoreType.REGULAR((2,)),
            pltpu.SemaphoreType.DMA((reduce_chunks, max(groups, 3), 3)),
            pltpu.SemaphoreType.DMA((reduce_chunks, max(groups, 3), 3)),
            pltpu.SemaphoreType.DMA((groups + 3,)),
            pltpu.SemaphoreType.DMA((groups + 3,)),
            pltpu.SemaphoreType.DMA((reduce_chunks,)),
        ]
        params = {"collective_id": 0, "has_side_effects": True}
    else:
        out_shape += [jax.ShapeDtypeStruct((hid, p.slice_columns), BF16), jax.ShapeDtypeStruct((p.bias_rows, LANES), F32)]
        out_specs += [ANY, VMEM]
    return pl.pallas_call(
        functools.partial(core_kernel, p, per, groups),
        out_shape=tuple(out_shape),
        in_specs=[ANY] * (6 + len(weights)),
        out_specs=tuple(out_specs),
        scratch_shapes=scratch,
        compiler_params=pltpu.CompilerParams(vmem_limit_bytes=63 * MIB, **params),
        cost_estimate=pl.CostEstimate(flops=flops, bytes_accessed=windows * p.length * 4, transcendentals=0),
    )(history, cotangent, targets, horizon, coarse_bias, fine_bias, *weights)


def outputs_kernel(
    plan,
    block,
    steps,
    packed_ref,
    history_ref,
    cotangent_ref,
    theta_ref,
    h3_ref,
    gfine_ref,
    pool_ref,
    fine_bias_ref,
    slices_ref,
    bias_rows_ref,
    residual_ref,
    history_grad_ref,
    prediction_ref,
    *refs,
):
    grads = refs[:16]
    head_ref, entry_ref, side_ref, pool_grad, fore_ref, *products, turned_head, turned_entry, bias_ref, sems = refs[16:]
    back_refs, fine_refs = products[:2], products[2:]
    p = plan
    step = pl.program_id(0)
    windows = p.windows
    chunk = min(512, windows)
    chunks = windows // chunk
    lanes_of = lambda n: slice(n * chunk, (n + 1) * chunk) if isinstance(n, int) else aligned(n * chunk, chunk, chunk)
    knots = block // KNOT
    pooled = block // POOL
    rest, later = fractions(chunk)

    def fetch(name, out, at, slot, sem):
        first = aligned(p.at[name] + at * block, block, LANES)
        return pltpu.make_async_copy(packed_ref.at[:, first], out.at[slot], sems.at[sem, slot])

    def interpolate(k, count, base, lanes):
        low = jnp.minimum if not isinstance(k, int) else min
        own = theta_ref[pl.ds(base + low(k, count - 1), 1), lanes]
        after = theta_ref[pl.ds(base + low(k + 1, count - 1), 1), lanes]
        return own * rest + after * later

    fore_out = pltpu.make_async_copy(fore_ref, prediction_ref, sems.at[3, 0])
    wide = p.wide_out - p.low
    first_fore = p.at["fine_head"] + p.low
    side = pltpu.make_async_copy(packed_ref.at[:, first_fore : first_fore + wide], side_ref, sems.at[2, 0])

    @pl.when(step == 0)
    def _():
        fetch("fine_head", head_ref, 0, 0, 0).start()
        fetch("fine_entry", entry_ref, 0, 0, 1).start()
        side.start()
        pool_grad[...] = pool_ref[...].astype(F32)

    @pl.when(step == 2)
    def _():
        side.wait()
        turned_fore = side_ref[...].T
        fore_bias = column_of(fine_bias_ref, p.low, wide)

        @pl.loop(0, chunks)
        def _(n):
            lanes = lanes_of(n)
            back_refs[0][: p.horizon, :] = dot(turned_fore[p.skip : p.skip + p.horizon], h3_ref[:, lanes])
            for k in range(0, p.fore, 2):
                rows = slice(k * KNOT, (k + 2) * KNOT)
                second = back_refs[0][rows, :] + fore_bias[p.skip + k * KNOT : p.skip + (k + 2) * KNOT]
                first = jnp.concatenate([interpolate(k + j, p.fore, p.back, lanes) for j in range(2)], axis=0)
                fore_ref[rows, lanes] = first.astype(BF16).astype(F32) + second.astype(BF16).astype(F32)

        fore_out.start()

    @pl.when(step == 1)
    def _():
        unpack(p, slices_ref, bias_rows_ref, grads)

    slot = step % 2

    @pl.when(step + 1 < steps)
    def _():
        fetch("fine_head", head_ref, step + 1, 1 - slot, 0).start()
        fetch("fine_entry", entry_ref, step + 1, 1 - slot, 1).start()

    fetch("fine_head", head_ref, step, slot, 0).wait()
    fetch("fine_entry", entry_ref, step, slot, 1).wait()
    turned_head[...] = head_ref[slot].T
    turned_entry[...] = entry_ref[slot].T
    row = jnp.broadcast_to(fine_bias_ref[:, aligned(step * block, block, LANES)], (8, block))
    bias_ref[...] = row.T[:, :1]
    pair = 2 * KNOT

    def make(n, place):
        lanes = lanes_of(n)
        back_refs[place][...] = dot(turned_head[...], h3_ref[:, lanes])
        fine_refs[place][...] = dot(turned_entry[...], gfine_ref[:, lanes])

    def finish(n, place):
        lanes = lanes_of(n)
        for at in range(0, block, pair):
            rows = slice(at, at + pair)
            k = step * knots + at // KNOT
            made = jnp.concatenate([interpolate(k + j, p.back, 0, lanes) for j in range(2)], axis=0)
            back = back_refs[place][rows, :] + bias_ref[rows, :]
            residual_ref[rows, lanes] = (history_ref[rows, lanes].astype(F32) - made - back).astype(BF16)
            first = step * pooled + at // POOL
            spread = jnp.concatenate(
                [jnp.broadcast_to(pool_grad[pl.ds(first + j, 1), lanes], (POOL, chunk)) for j in range(pair // POOL)],
                axis=0,
            )
            fine = fine_refs[place][rows, :] + spread
            history_grad_ref[rows, lanes] = (cotangent_ref[rows, lanes].astype(F32) + fine).astype(BF16)

    for n in range(chunks + 1):
        if n < chunks:
            make(n, n % 2)
        if n > 0:
            finish(n - 1, (n - 1) % 2)

    @pl.when(step == steps - 1)
    def _():
        fore_out.wait()


def outputs(plan, packed, history, cotangent, theta, h3, gfine, pool, fine_bias, slices, bias_rows):
    p = plan
    hid, windows = p.hidden, p.windows
    block = 6 * LANES
    steps = -(-p.length // block)
    rows = pl.BlockSpec((block, windows), lambda i: (i, 0))
    wide = p.wide_out - p.low
    per = slices.shape[1]
    square, vector = (per, hid), (1, per)
    grads = []
    for entry, out in ((p.pooled, p.coarse_out), (p.length, p.fine_out)):
        grads += [(per, entry), vector, square, vector, square, vector, (per, out), (1, out)]
    return pl.pallas_call(
        functools.partial(outputs_kernel, p, block, steps),
        grid=(steps,),
        out_shape=(
            jax.ShapeDtypeStruct((p.length, windows), BF16),
            jax.ShapeDtypeStruct((p.length, windows), BF16),
            jax.ShapeDtypeStruct((p.horizon, windows), F32),
        )
        + tuple(jax.ShapeDtypeStruct(shape, F32) for shape in grads),
        in_specs=[ANY, rows, rows, VMEM, VMEM, VMEM, VMEM, VMEM, VMEM, VMEM],
        out_specs=(rows, rows, ANY) + (VMEM,) * len(grads),
        scratch_shapes=[
            pltpu.VMEM((2, hid, block), BF16),
            pltpu.VMEM((2, hid, block), BF16),
            pltpu.VMEM((hid, wide), BF16),
            pltpu.VMEM((p.pool_wide, windows), F32),
            pltpu.VMEM((p.horizon, windows), F32),
            *[pltpu.VMEM((block, min(512, windows)), F32)] * 4,
            pltpu.VMEM((block, hid), BF16),
            pltpu.VMEM((block, hid), BF16),
            pltpu.VMEM((block, 1), F32),
            pltpu.SemaphoreType.DMA((4, 2)),
        ],
        compiler_params=pltpu.CompilerParams(vmem_limit_bytes=56 * MIB),
        cost_estimate=pl.CostEstimate(
            flops=2 * windows * hid * (2 * p.length + p.horizon), bytes_accessed=windows * p.length * 8, transcendentals=0
        ),
    )(packed, history, cotangent, theta, h3, gfine, pool, fine_bias, slices, bias_rows)


def pack(plan, arrays, biases):
    p = plan
    names = sorted(p.at, key=p.at.get)
    ends = [p.at[name] for name in names[1:]] + [p.columns]
    columns = []
    for name, end in zip(names, ends):
        piece = arrays[name] if name != "bias" else biases
        columns.append(jnp.pad(piece.astype(BF16), ((0, 0), (0, end - p.at[name] - piece.shape[1]))))
    return jnp.concatenate(columns, axis=1)


def unpack(plan, slices_ref, bias_rows_ref, grads):
    p = plan
    hid = p.hidden

    def joined(name, out, source, row=None, base=0, low=0, high=None):
        high, done = out.shape[1] if high is None else high, low
        for section in range(p.sections):
            first = base + p.start(name, section)
            last = min(first + p.rows(name), high)
            if row is not None:
                for at in range(max(done // LANES * LANES, first), last, LANES):
                    begin, end = max(at, done), min(at + LANES, last)
                    if begin < end:
                        here = source[section, pl.ds(row + (at - first) // LANES, 1), :]
                        out[:, begin:end] = here[:, begin - at : end - at]
            elif done < last:
                at = p.slice_at[name] + done - first
                out[:, done:last] = source[section, :, at : at + last - done].astype(F32)
            done = max(done, last)

    def ones_column(name, row):
        section = p.sections - 1
        at = p.slice_at[name] + row - p.start(name, section)
        block = slices_ref[section, :, at // LANES * LANES : at // LANES * LANES + LANES].astype(F32)
        return block.T[at % LANES : at % LANES + 1]

    def own_part(name, out):
        per = out.shape[1]
        width = min(per, LANES)
        share = p.part[name][0]
        for at in range(0, per, width):
            first = lax.axis_index("dp") * per + at
            block = first // LANES
            row = bias_rows_ref[block // share, pl.ds(p.bias_at[name] + block % share, 1), :]
            wide = jnp.broadcast_to(row, (8, LANES))
            out[:, at : at + width] = pltpu.roll(wide, (LANES - first % LANES) % LANES, 1)[:1, :width]

    for base, block in ((0, "coarse_"), (8, "fine_")):
        entry, head = block + "entry", block + "head"
        joined(entry, grads[base], slices_ref)
        grads[base + 1][...] = ones_column(entry, grads[base].shape[1])
        for i, name in enumerate((block + "middle", block + "upper")):
            joined(name, grads[base + 2 + 2 * i], slices_ref)
            own_part(name, grads[base + 3 + 2 * i])
        for number, source in ((6, slices_ref), (7, bias_rows_ref)):
            row = lambda name: p.bias_at[name] if number == 7 else None
            if base == 0:
                joined(head, grads[number], source, row(head))
            else:
                joined("head_back", grads[8 + number], source, row("head_back"), 0, 0, p.length)
                joined("head_fore", grads[8 + number], source, row("head_fore"), p.low, p.length)


def body(mesh_shape, history, targets, horizon, cotangent, *params):
    (c_entry, c_entry_b, c_middle, c_middle_b, c_upper, c_upper_b, c_head, c_head_b) = params[:8]
    (f_entry, f_entry_b, f_middle, f_middle_b, f_upper, f_upper_b, f_head, f_head_b) = params[8:]
    sections = mesh_shape["section"]
    length, hidden = f_entry.shape[0], c_middle.shape[1]
    p = Plan(
        length, f_head.shape[1] - length, hidden, c_entry.shape[0], c_head.shape[1], sections, history.shape[0]
    )
    pieces = (c_entry.T, c_middle, c_upper, c_head, f_entry.T, f_middle, f_upper, f_head)
    bias_pieces = (c_entry_b, c_middle_b, c_upper_b, f_entry_b, f_middle_b, f_upper_b)
    dp_count, per = mesh_shape["dp"], c_middle.shape[0]
    rows = (history.T, cotangent.T)
    fine_bias = f_head_b[None, :]
    rest = (targets.T, horizon[None, :], c_head_b[None, :], fine_bias)
    groups = dp_count // 2
    if sections == 4 and dp_count % 2 == 0 and per % 64 == 0 and groups > 1:
        theta, h3, gfine, pool, packed, slices, bias_rows = core(
            p, per, groups, *rows, *rest, pieces + tuple(b[None, :] for b in bias_pieces)
        )
    else:
        packed = pack(p, dict(zip(NAMES, pieces)), jnp.stack(bias_pieces, axis=1))
        packed = lax.all_gather(packed, "dp", axis=0, tiled=True)
        theta, h3, gfine, pool, part, head_bias = core(p, per, 0, *rows, *rest, (packed,))
        own = lax.psum_scatter(part.astype(F32), "dp", scatter_dimension=0, tiled=True)
        slices = lax.all_gather(own, "section", axis=0)
        bias_rows = lax.all_gather(lax.psum(head_bias, "dp"), "section", axis=0)
    residual, history_grad, prediction, *grads = outputs(
        p, packed, *rows, theta, h3, gfine, pool, fine_bias, slices, bias_rows
    )
    grads = [g.T if i in (0, 8) else g if g.shape[0] > 1 else g[0] for i, g in enumerate(grads)]
    return (prediction.T, residual.T, history_grad.T) + tuple(grads)


def solution(mesh):
    by_row, by_column, by_entry, copied = P("dp", None), P(None, "dp"), P("dp"), P()
    block = (by_column, by_entry, by_row, by_entry, by_row, by_entry, by_row, copied)
    in_specs = (by_row, by_row, by_entry, by_row) + block + block
    out_specs = (by_row, by_row, by_row) + block + block
    return jax.shard_map(
        functools.partial(body, dict(mesh.shape)), mesh=mesh, in_specs=in_specs, out_specs=out_specs, check_vma=False
    )
```

```python
import functools

import jax
import jax.numpy as jnp
from jax import lax
from jax.experimental import pallas as pl
from jax.experimental.pallas import tpu as pltpu
from jax.sharding import PartitionSpec as P

POOL = 8
KNOT = 24
LANES = 128
ONES = 16
GELU_A = 0.7978845608028654
GELU_B = GELU_A * 0.044715
F32 = jnp.float32
BF16 = jnp.bfloat16
MIB = 1 << 20


def up(size, unit):
    return -(-size // unit) * unit


class Plan:
    def __init__(self, length, horizon, hidden, pooled, coarse_out, sections, windows):
        self.length, self.horizon, self.hidden = length, horizon, hidden
        self.pooled, self.coarse_out = pooled, coarse_out
        self.fine_out = length + horizon
        self.sections, self.windows = sections, windows
        self.back, self.fore = length // KNOT, horizon // KNOT
        self.wide_in, self.wide_out = up(length + 1, LANES), up(self.fine_out + 1, LANES)
        self.pool_wide, self.theta_wide = up(pooled + 1, LANES), up(coarse_out + 1, LANES)
        widths = [
            ("coarse_entry", self.pool_wide),
            ("bias", LANES),
            ("coarse_middle", hidden),
            ("coarse_upper", hidden),
            ("coarse_head", self.theta_wide),
            ("fine_entry", self.wide_in),
            ("fine_middle", hidden),
            ("fine_upper", hidden),
            ("fine_head", self.wide_out),
        ]
        self.at, place = {}, 0
        for name, width in widths:
            self.at[name] = place
            place += width
        self.columns = place
        self.low = length // LANES * LANES
        self.skip = length - self.low
        self.square = hidden // sections
        self.slice_at, self.part, place = {}, {}, 0
        for name, width in (
            ("head_back", self.wide_in),
            ("head_fore", self.wide_out - self.low),
            ("fine_upper", hidden),
            ("fine_middle", hidden),
            ("fine_entry", self.wide_in),
            ("coarse_head", self.theta_wide),
            ("coarse_upper", hidden),
            ("coarse_middle", hidden),
            ("coarse_entry", self.pool_wide),
        ):
            self.slice_at[name] = place
            total = width // LANES
            share = -(-total // sections)
            self.part[name] = share, total
            place += share * LANES
        self.slice_columns = place
        self.bias_at, place = {}, 0
        for name in ("head_back", "head_fore", "coarse_head", "coarse_middle", "coarse_upper", "fine_middle", "fine_upper"):
            self.bias_at[name] = place
            place += self.part[name][0]
        self.bias_rows = up(place, 8)
        self.knot_rows = up(coarse_out, ONES)
        self.pair = 2 * KNOT
        self.r1_pairs = -(-(self.rows("fine_entry") + self.pair - ONES) // self.pair)

    def rows(self, name):
        return self.part[name][0] * LANES

    def start(self, name, section):
        low = min if isinstance(section, int) else jnp.minimum
        share, total = self.part[name]
        return low(section * share, total - share) * LANES


def gelu_both(a):
    square = a * a
    v = 0.5 + 0.5 * jnp.tanh(a * (GELU_A + GELU_B * square))
    h = a * v
    return h, v + h * (1.0 - v) * (2.0 * GELU_A + (6.0 * GELU_B) * square)


def dot(a, b):
    return jnp.dot(a, b, preferred_element_type=F32)


def dot_rows(a, b):
    return lax.dot_general(a, b, (((1,), (1,)), ((), ())), preferred_element_type=F32)


def aligned(start, size, unit):
    return pl.ds(pl.multiple_of(start, unit), size)


def column_of(row_ref, first, count):
    size = row_ref.shape[1]
    columns = []
    for at in range(first, first + count, LANES):
        width = max(0, min(LANES, size - at))
        row = jnp.zeros((1, LANES), F32) if width == 0 else row_ref[:, at : at + width]
        if 0 < width < LANES:
            row = jnp.concatenate([row, jnp.zeros((1, LANES - width), F32)], axis=1)
        columns.append(jnp.broadcast_to(row, (LANES, LANES)).T[:, :1])
    return jnp.concatenate(columns, axis=0)


def hat_weights(first, count, plan, turned=False, fore=False):
    p = plan
    shape = (p.knot_rows, count) if turned else (count, p.theta_wide)
    row = lax.broadcasted_iota(jnp.int32, shape, 1 if turned else 0) + first
    knot = lax.broadcasted_iota(jnp.int32, shape, 0 if turned else 1)
    away = row - KNOT * knot
    weight = jnp.maximum(KNOT - jnp.abs(away), 0)
    last = (knot == p.back - 1) | (knot == p.back + p.fore - 1)
    weight = jnp.where(last & (away > 0) & (away < KNOT), KNOT, weight)
    own = (knot >= p.back) & (row >= p.length) if fore else (knot < p.back) & (row < p.length)
    inside = own & (row < p.fine_out) & (knot < p.back + p.fore)
    return jnp.where(inside, weight, 0).astype(F32).astype(BF16)


def fractions(width):
    later = lax.broadcasted_iota(jnp.int32, (KNOT, width), 0).astype(F32) * (1.0 / KNOT)
    return 1.0 - later, later


NAMES = (
    "coarse_entry",
    "coarse_middle",
    "coarse_upper",
    "coarse_head",
    "fine_entry",
    "fine_middle",
    "fine_upper",
    "fine_head",
)
KEPT = ("fine_entry", "fine_head")


def remote(source, target, send_sem, recv_sem, place):
    return pltpu.make_async_remote_copy(
        src_ref=source,
        dst_ref=target,
        send_sem=send_sem,
        recv_sem=recv_sem,
        device_id=place,
        device_id_type=pl.DeviceIdType.MESH,
    )


def signal(semaphore, places):
    for place in places:
        pl.semaphore_signal(semaphore, inc=1, device_id=place, device_id_type=pl.DeviceIdType.MESH)


class Ways:
    def __init__(self, groups):
        self.section, self.dp = lax.axis_index("section"), lax.axis_index("dp")
        self.group, self.core = self.dp // 2, self.dp % 2
        self.groups = groups
        self.partner = (self.section, self.group * 2 + 1 - self.core)
        s = self.section
        self.side = [s + 1 - 2 * (s % 2), (s + 2) % 4]
        self.sides = [(t, self.dp) for t in self.side]
        self.across = 3 - s
        self.corner = (self.across, self.dp)

    def far(self, j):
        group = (self.group + j) % self.groups
        return group, (self.section, group * 2 + self.core)

    def from_far(self, j):
        return (self.group + self.groups - j) % self.groups

    def all(self):
        return [self.partner, self.corner] + self.sides + [self.far(j)[1] for j in range(1, self.groups)]


class Gather:
    def __init__(self, plan, way, per, cuts, w_ref, shards, biases, send, recv, partner_recv):
        self.p, self.way, self.per, self.cuts, self.w_ref = plan, way, per, cuts, w_ref
        self.shards, self.biases = shards, biases
        self.send, self.recv, self.partner_recv = send, recv, partner_recv
        self.near = range(1, way.groups)
        self.chunks, self.ahead = len(cuts) - 1, 3

    def at(self, k, owner, s=None):
        quarter = self.per // 4
        rows = aligned(owner * self.per, self.per, self.per)
        if s is not None:
            rows = aligned(owner * self.per + s * quarter, quarter, quarter)
        return self.w_ref.at[rows, self.cuts[k] : self.cuts[k + 1]]

    def source(self, j):
        return self.way.from_far(j) * 2 + self.way.core

    def copy(self, here, k, j, kind, place):
        return remote(here, here, self.send.at[k, j - 1, kind], self.recv.at[k, j - 1, kind], place)

    def to_far(self, k, j):
        return self.copy(self.at(k, self.way.dp, self.way.section), k, j, 0, self.way.far(j)[1])

    def to_side(self, k, j, i):
        return self.copy(self.at(k, self.source(j), self.way.section), k, j, 1 + i, self.way.sides[i])

    def to_across(self, k, j):
        if k == 0:
            return self.copy(self.at(k, self.source(j), self.way.section), k, j, 3, self.way.corner)
        i = (k + j) % 2
        return self.copy(self.at(k, self.source(j), self.way.side[i]), k, j, 3, self.way.sides[1 - i])

    def to_partner(self, k, j):
        here = self.at(k, self.source(j) if j else self.way.dp)
        return remote(here, here, self.send.at[k, max(j - 1, 0), 4 if j else 5], self.partner_recv.at[k, j], self.way.partner)

    def arrived(self, k, j, kind):
        s = [self.way.section, self.way.side[0], self.way.side[1], self.way.across][kind]
        self.copy(self.at(k, self.source(j), s), k, j, kind, self.way.partner).wait_recv()

    def cast(self, k):
        p, own = self.p, aligned(self.way.dp * self.per, self.per, self.per)
        low, high = self.cuts[k], self.cuts[k + 1]
        for ref, name in zip(self.shards, NAMES):
            at, size = p.at[name], ref.shape[1]
            wide = up(size + 1, LANES) if name.endswith(("entry", "head")) else size
            first, last = max(at, low), min(at + wide, high)
            full = min(last, at + size // LANES * LANES)
            if first < full:
                self.w_ref[own, first:full] = ref[:, first - at : full - at].astype(BF16)
            if first < last and last > full:
                rest = ref[:, full - at : size].astype(BF16)
                pad = jnp.zeros((self.per, last - at - size), BF16)
                self.w_ref[own, full:last] = jnp.concatenate([rest, pad], axis=1)
        at = p.at["bias"]
        if low <= at < high:
            count = len(self.biases)
            rows = jnp.concatenate([ref[...] for ref in self.biases] + [jnp.zeros((8 - count, self.per), F32)], axis=0)
            wide = jnp.concatenate([rows, jnp.zeros((8, LANES - self.per), F32)], axis=1)
            wide = jnp.concatenate([wide, jnp.zeros((LANES - 8, LANES), F32)], axis=0)
            self.w_ref[own, at : at + LANES] = wide.T[: self.per].astype(BF16)

    def first(self, k):
        self.cast(k)
        for j in self.near:
            self.to_far(k, j).start()
        self.to_partner(k, 0).start()

    def second(self, k):
        for j in self.near:
            self.arrived(k, j, 0)
            for i in range(2):
                self.to_side(k, j, i).start()
            if k == 0:
                self.to_across(k, j).start()

    def third(self, k):
        for j in self.near:
            self.arrived(k, j, 1)
            self.arrived(k, j, 2)
            if k > 0:
                self.to_across(k, j).start()

    def fourth(self, k):
        for j in self.near:
            self.arrived(k, j, 3)
            self.to_partner(k, j).start()

    def complete(self, k):
        for j in range(self.way.groups):
            there = (self.way.from_far(j) * 2 + 1 - self.way.core) if j else self.way.partner[1]
            here = self.at(k, there)
            remote(here, here, self.send.at[k, 0, 5], self.partner_recv.at[k, j], self.way.partner).wait_recv()

    def sent(self, k):
        for j in self.near:
            for copy in (self.to_far(k, j), self.to_side(k, j, 0), self.to_side(k, j, 1), self.to_across(k, j)):
                copy.wait_send()
            self.to_partner(k, j).wait_send()
        self.to_partner(k, 0).wait_send()


class Reduce:
    def __init__(self, plan, way, per, cuts, part_ref, core_in, far_in, far_out, stage_ref, out_ref, send, recv, local):
        self.p, self.way, self.per, self.cuts = plan, way, per, cuts
        self.part_ref, self.core_in, self.far_in, self.far_out = part_ref, core_in, far_in, far_out
        self.stage_ref, self.out_ref, self.send, self.recv, self.local = stage_ref, out_ref, send, recv, local
        self.near = range(1, way.groups)
        self.chunks = len(cuts) - 1

    def columns(self, k):
        return slice(self.cuts[k], self.cuts[k + 1])

    def to_partner(self, k, g):
        return remote(
            self.part_ref(g * 2 + 1 - self.way.core, k),
            self.core_in(g, k),
            self.send.at[k, g, 0],
            self.recv.at[k, g, 0],
            self.way.partner,
        )

    def to_far(self, k, j):
        here, there = self.far_out(j - 1, k), self.far_in(j - 1, k)
        return remote(here, there, self.send.at[k, j - 1, 1], self.recv.at[k, j - 1, 1], self.way.far(j)[1])

    def side(self, k, source, i, to):
        here = self.out_ref.at[source, :, self.columns(k)]
        return remote(here, here, self.send.at[k, i, 2], self.recv.at[k, i, 2], to)

    def to_side(self, k, i):
        here = self.stage_ref.at[:, self.columns(k)]
        there = self.out_ref.at[self.way.section, :, self.columns(k)]
        place = (self.way.sides + [self.way.corner])[i]
        return remote(here, there, self.send.at[k, i, 2], self.recv.at[k, i, 2], place)

    def keep(self, k):
        there = self.out_ref.at[self.way.section, :, self.columns(k)]
        return pltpu.make_async_copy(self.stage_ref.at[:, self.columns(k)], there, self.local.at[k])

    def summed(self, k, group):
        own = self.part_ref(group * 2 + self.way.core, k)[...].astype(F32)
        return own + self.core_in(group, k)[...].astype(F32)

    def first(self, k):
        for g in range(self.way.groups):
            self.to_partner(k, g).start()

    def second(self, k):
        for g in range(self.way.groups):
            self.to_partner(k, g).wait_recv()
        for j in self.near:
            self.far_out(j - 1, k)[...] = self.summed(k, self.way.far(j)[0]).astype(BF16)
            self.to_far(k, j).start()

    def third(self, k):
        total = self.summed(k, self.way.group)
        for j in self.near:
            self.to_far(k, j).wait_recv()
            total += self.far_in(j - 1, k)[...].astype(F32)
        self.stage_ref[:, self.columns(k)] = total.astype(BF16)
        for i in range(3):
            self.to_side(k, i).start()
        self.keep(k).start()

    def complete(self, k):
        for i, source in enumerate(self.way.side + [self.way.across]):
            self.side(k, source, i, self.way.partner).wait_recv()

    def sent_far(self, k):
        for j in self.near:
            self.to_far(k, j).wait_send()

    def sent(self, k):
        for g in range(self.way.groups):
            self.to_partner(k, g).wait_send()
        for i in range(3):
            self.to_side(k, i).wait_send()
        self.keep(k).wait()


class ReduceBias:
    def __init__(self, way, own_ref, core_in, far_ref, out_ref, send, recv):
        self.way, self.own_ref, self.core_in, self.far_ref, self.out_ref = way, own_ref, core_in, far_ref, out_ref
        self.send, self.recv = send, recv
        self.near = range(1, way.groups)

    def copy(self, here, there, n, place):
        return remote(here, there, self.send.at[n], self.recv.at[n], place)

    def to_partner(self):
        return self.copy(self.own_ref, self.core_in, 0, self.way.partner)

    def to_far(self, j):
        here = self.far_ref.at[self.way.group]
        return self.copy(here, here, j, self.way.far(j)[1])

    def side(self, source, n, to):
        here = self.out_ref.at[source]
        return self.copy(here, here, self.way.groups + n, to)

    def to_side(self, i):
        return self.side(self.way.section, i, (self.way.sides + [self.way.corner])[i])

    def second(self):
        self.to_partner().wait_recv()
        self.far_ref[self.way.group] = self.own_ref[...] + self.core_in[...]
        for j in self.near:
            self.to_far(j).start()

    def third(self):
        for j in self.near:
            here = self.far_ref.at[self.way.from_far(j)]
            self.copy(here, here, j, self.way.partner).wait_recv()
        total = self.far_ref[0]
        for g in range(1, self.way.groups):
            total += self.far_ref[g]
        self.out_ref[self.way.section] = total
        for i in range(3):
            self.to_side(i).start()

    def complete(self):
        for i, source in enumerate(self.way.side + [self.way.across]):
            self.side(source, i, self.way.partner).wait_recv()
        self.to_partner().wait_send()
        for j in self.near:
            self.to_far(j).wait_send()
        for i in range(3):
            self.to_side(i).wait_send()


def core_kernel(plan, per, groups, *refs):
    p = plan
    refs = list(refs)
    take = lambda count: [refs.pop(0) for _ in range(count)]
    history_ref, cotangent_ref, target_ref, horizon_ref, coarse_bias_ref, fine_bias_ref = take(6)
    if groups:
        shards_in = take(14)
    else:
        (packed_ref,) = take(1)
    theta_out, h3_out, gfine_out, pool_out = take(4)
    if groups:
        kept_out, slices_out, bias_out = take(3)
    else:
        slice_out, bias_out = take(2)
    w_ref, big_ref = take(2)
    h_refs, g_refs = take(6), take(6)
    r1_ref, pooled_ref, split_ref, theta_ref, gtheta_ref, gknot_ref = take(6)
    pw_ref, pwt_ref, turned_ref, even_ref, odd_ref, bias_ref = take(6)
    horizon_rows, horizon_buf, coarse_bias_buf, fine_bias_buf, sems = take(5)
    if groups:
        shards = take(14)
        shard_sems, send, recv, partner_recv = take(4)
        head_bias_ref, bias_in, bias_far, stage_ref, ready, reduce_send, reduce_recv, bias_send, bias_recv = take(9)
        keep_sems = take(1)[0]
    else:
        head_bias_ref = bias_out
    hid, windows = p.hidden, p.windows
    section = lax.axis_index("section")
    chunk = min(512, windows // 2)
    chunks = windows // chunk
    H = slice(0, hid)
    lanes_of = lambda n: aligned(n * chunk, chunk, chunk)
    place = p.at["fine_entry"]
    head_at = p.at["fine_head"]

    load = lambda source, out, sem: pltpu.make_async_copy(source, out, sems.at[sem])
    history_in = load(history_ref, big_ref.at[: p.length], 1)
    cotangent_in = load(cotangent_ref, big_ref.at[: p.length], 2)
    target_in = load(target_ref, big_ref.at[p.length : p.fine_out], 0)
    rows_in = [
        load(horizon_ref, horizon_rows, 3),
        load(coarse_bias_ref, coarse_bias_buf, 4),
        load(fine_bias_ref, fine_bias_buf, 5),
    ]
    theta_copy = load(theta_ref, theta_out, 6)
    h3_copy = load(h_refs[5].at[H], h3_out, 7)
    gfine_copy = load(g_refs[3], gfine_out, 8)
    pool_copy = load(pooled_ref, pool_out, 9)

    if groups:
        shards_load = [
            pltpu.make_async_copy(source, out, shard_sems.at[n]) for n, (source, out) in enumerate(zip(shards_in, shards))
        ]
        order = [0, 1, 2, 3, 8, 9, 10, 11, 12, 13, 4, 5, 6, 7]
        for n in order:
            shards_load[n].start()
        way = Ways(groups)
        middle = p.at["fine_middle"]
        third = (p.columns - middle) // 3 // LANES * LANES
        entry_cut = place + up((middle - place) // 2, LANES)
        cuts = (0, p.at["coarse_middle"], place, entry_cut, middle, middle + third, middle + 2 * third, p.columns)
        gather = Gather(p, way, per, cuts, w_ref, shards[:8], shards[8:], send, recv, partner_recv)
        cotangent_in.start()
        for copy in rows_in:
            copy.start()
        barrier = pltpu.get_barrier_semaphore()
        signal(barrier, way.all())
        for n in order[:10]:
            shards_load[n].wait()
        pl.semaphore_wait(barrier, len(way.all()))
        gather.first(0)
        for n in order[10:]:
            shards_load[n].wait()
        for k in range(1, gather.ahead):
            gather.first(k)
    else:
        weights_in = load(packed_ref, w_ref, 10)
        weights_in.start()
        cotangent_in.start()
        for copy in rows_in:
            copy.start()

    def move(*steps):
        if groups:
            for stage, k in steps:
                {2: gather.second, 3: gather.third, 4: gather.fourth}[stage](k)
                if stage == 2 and k + gather.ahead < gather.chunks:
                    gather.first(k + gather.ahead)

    def complete(*ks):
        if groups:
            for k in ks:
                gather.complete(k)

    tail = p.wide_out - p.length
    mark = lax.broadcasted_iota(jnp.int32, (tail, windows), 0) < POOL
    big_ref[p.length :, :] = mark.astype(F32).astype(BF16)
    pooled_ref[...] = jnp.zeros_like(pooled_ref)
    for index in range(6):
        h_refs[index][hid:, :] = jnp.ones((ONES, windows), BF16)
    for copy in rows_in:
        copy.wait()
    for n in range(windows // LANES):
        horizon_buf[:, n * LANES : (n + 1) * LANES] = horizon_rows[n : n + 1, :]
    step = 6 * LANES

    def adjoint(first, count, fore):
        hats = hat_weights(first, count, p, True, fore)

        @pl.loop(0, chunks)
        def _(n):
            lanes = lanes_of(n)
            rows = slice(first, first + count) if isinstance(first, int) else aligned(first, count, ONES)
            gtheta_ref[:, lanes] += dot(hats, big_ref[rows, lanes]) * (-1.0 / KNOT)

    cotangent_in.wait()
    gtheta_ref[...] = jnp.zeros_like(gtheta_ref)
    quarter = p.wide_in // 4
    pl.loop(0, 4)(lambda i: adjoint(i * quarter, quarter, False))
    history_in.start()
    move((2, 0), (2, 1), (3, 0))
    history_in.wait()

    unit = hid
    shape = (unit // POOL, unit)
    member = lax.broadcasted_iota(jnp.int32, shape, 1) - POOL * lax.broadcasted_iota(jnp.int32, shape, 0)
    turned_ref[: unit // POOL, :] = ((member >= 0) & (member < POOL)).astype(F32).astype(BF16)
    firsts = list(range(0, p.wide_in, unit))
    for number, first in enumerate(firsts):
        count = min(unit, p.wide_in - first)
        rows = slice(first // POOL, (first + count) // POOL)

        @pl.loop(0, chunks)
        def _(n):
            lanes = lanes_of(n)
            total = dot(turned_ref[: count // POOL, :count], big_ref[first : first + count, lanes])
            pooled_ref[rows, lanes] = (total * (1.0 / POOL)).astype(BF16)

        if number == len(firsts) // 2:
            move((4, 0))
    move((3, 1), (2, 2))
    complete(0)
    if not groups:
        weights_in.wait()
    fore_parts = [(0, 8 * p.pair), (8 * p.pair, p.horizon)]
    fore_bias = column_of(fine_bias_buf, p.low, p.wide_out - p.low)
    placed = w_ref[:, p.at["bias"] : p.at["bias"] + LANES].astype(F32)
    lane = lax.broadcasted_iota(jnp.int32, (hid, LANES), 1)
    for number, (low, high) in enumerate(fore_parts):
        column = fore_bias[p.skip + low : p.skip + high]
        column = jnp.concatenate([column, jnp.zeros((hid - high + low, 1), F32)], axis=0)
        placed = jnp.where(lane == 6 + number, column, placed)
    bias_ref[...] = placed

    def pipeline(*layers):
        tile, pending = 0, nothing
        for before, produce, finish, after in layers:
            before()
            for n in range(chunks):
                lanes = slice(n * chunk, (n + 1) * chunk)
                out = (even_ref, odd_ref)[tile % 2]
                value = produce(lanes)
                out[: value.shape[0], :] = value
                pending()
                pending = functools.partial(finish, out, lanes)
                tile += 1
            after()
        pending()

    def nothing():
        pass

    def looped(*layers):
        for before, produce, finish, after in layers:
            before()

            @pl.loop(0, chunks)
            def _(n, produce=produce, finish=finish):
                value = produce(lanes_of(n))
                even_ref[: value.shape[0], :] = value
                finish(even_ref, lanes_of(n))

            after()

    def turn_weight(first, count):
        turned_ref[:count, :] = w_ref[:, first : first + count].T

    strip = ONES

    def activate(index):
        def finish(source, lanes):
            for r in range(0, hid, strip):
                rows = slice(r, r + strip)
                h, slope = gelu_both(source[rows, :] + bias_ref[rows, index : index + 1])
                h_refs[index][rows, lanes] = h.astype(BF16)
                g_refs[index][rows, lanes] = slope.astype(BF16)

        return finish

    def hidden(name, index, after=nothing):
        return (
            lambda: turn_weight(p.at[name], hid),
            lambda lanes: dot(turned_ref[H, :], h_refs[index - 1][H, lanes]),
            activate(index),
            after,
        )

    at_entry = p.at["coarse_entry"]
    at_head = p.at["coarse_head"]
    theta_bias = column_of(coarse_bias_buf, 0, p.theta_wide)

    def keep_theta(source, lanes):
        for r in range(0, p.theta_wide, strip):
            rows = slice(r, r + strip)
            theta = source[rows, :] + theta_bias[rows]
            if r < p.knot_rows:
                theta_ref[rows, lanes] = theta
            knots = jnp.where(lax.broadcasted_iota(jnp.int32, theta.shape, 0) + r < p.back, theta, 0.0)
            high = knots.astype(BF16)
            split_ref[rows, lanes] = high
            split_ref[p.theta_wide + r : p.theta_wide + r + strip, lanes] = (knots - high.astype(F32)).astype(BF16)

    def coarse_rest():
        move((4, 1), (3, 2), (2, 3))
        complete(1)

    forward = pipeline if groups else looped
    forward(
        (
            nothing,
            lambda lanes: dot(w_ref[:, at_entry : at_entry + p.pool_wide], pooled_ref[:, lanes]),
            activate(0),
            coarse_rest,
        ),
        hidden("coarse_middle", 1, lambda: move((4, 2), (2, 4))),
        hidden("coarse_upper", 2, lambda: move((3, 3))),
        (
            lambda: turn_weight(at_head, p.theta_wide),
            lambda lanes: dot(turned_ref[: p.theta_wide, :], h_refs[2][H, lanes]),
            keep_theta,
            nothing,
        ),
    )
    theta_copy.start()

    def keep(name, wide, sem):
        columns = slice(p.at[name], p.at[name] + wide)
        return load(w_ref.at[:, columns], kept_out.at[:, columns], sem)

    first_pair = p.start("fine_entry", section) // p.pair

    def interpolate(base, count, k, rest, later, lanes):
        own = theta_ref[pl.ds(base + jnp.minimum(k, count - 1), 1), lanes]
        after = theta_ref[pl.ds(base + jnp.minimum(k + 1, count - 1), 1), lanes]
        return own * rest + after * later

    everything = slice(0, windows)
    rest, later = fractions(windows)

    @pl.loop(0, p.r1_pairs)
    def _(i):
        pair = first_pair + i
        source = aligned(pair * p.pair, p.pair, ONES)
        made = jnp.concatenate(
            [interpolate(0, p.back, 2 * pair + j, rest, later, everything) for j in range(2)], axis=0
        )
        made = made * (pair < p.back // 2).astype(F32)
        r1_ref[aligned(i * p.pair, p.pair, ONES), :] = (big_ref[source, :].astype(F32) - made).astype(BF16)

    move((4, 3), (2, 5), (3, 4))
    complete(2, 3)
    kept = []
    if groups:
        kept.append(keep("fine_entry", p.wide_in, 10))
        kept[0].start()

    total = jnp.zeros((hid, p.theta_wide), F32)
    for first in range(0, p.wide_in, step):
        count = min(step, p.wide_in - first)
        total += dot(w_ref[:, place + first : place + first + count], hat_weights(first, count, p))
    product = (total * (1.0 / KNOT)).astype(BF16)
    pwt_ref[...] = product
    pw_ref[...] = product.T
    move((4, 4), (2, 6), (3, 5))

    def fine_entry(lanes):
        a = dot(w_ref[:, place : place + p.wide_in], big_ref[: p.wide_in, lanes])
        for part in (0, p.theta_wide):
            a -= dot(pwt_ref[...], split_ref[part : part + p.theta_wide, lanes])
        return a

    def entry_made():
        cotangent_in.start()
        target_in.start()
        big_ref[p.fine_out :, :] = jnp.zeros((p.wide_out - p.fine_out, windows), BF16)
        if groups:
            signal(ready.at[0], way.all())
        move((4, 5), (3, 6))
        complete(4)

    rest_c, later_c = fractions(chunk)

    def fore(number):
        low, high = fore_parts[number]

        def before():
            first = head_at + p.low + low
            turned = w_ref[:, first : first + up(high - low + p.skip, LANES)].T
            turned_ref[: high - low, :] = turned[p.skip : p.skip + high - low]

        def finish(source, lanes):
            for k in range(low // KNOT, high // KNOT, 2):
                here = slice(k * KNOT - low, (k + 2) * KNOT - low)
                second = source[here, :] + bias_ref[here, 6 + number : 7 + number]
                first = jnp.concatenate(
                    [interpolate(p.back, p.fore, k + j, rest_c, later_c, lanes) for j in range(2)], axis=0
                )
                counts = (lax.broadcasted_iota(jnp.int32, (2 * KNOT, chunk), 0) + k * KNOT) < horizon_buf[:, lanes]
                there = slice(p.length + k * KNOT, p.length + (k + 2) * KNOT)
                error = first + second - big_ref[there, lanes].astype(F32)
                big_ref[there, lanes] = jnp.where(counts, -error, 0.0).astype(BF16)

        return before, lambda lanes: dot(turned_ref[: high - low, :], h_refs[5][H, lanes]), finish, nothing

    looped((nothing, fine_entry, activate(3), entry_made))
    forward(hidden("fine_middle", 4, lambda: move((4, 6))), hidden("fine_upper", 5))
    h3_copy.start()
    cotangent_in.wait()
    target_in.wait()

    def gradient_slice(name, left, right_ref, first, step=LANES, sign=1.0):
        left_ref = left if name.endswith("entry") else h_refs[left]

        def part(b):
            value = sign * dot_rows(left_ref[...], right_ref[aligned(first + b * step, step, ONES), :])
            w_ref[:, aligned(place + p.slice_at[name] + b * step, step, LANES)] = value[:hid].astype(BF16)
            if name in p.bias_at:
                for c in range(step // LANES):
                    row = p.bias_at[name] + b * (step // LANES) + c
                    head_bias_ref[pl.ds(row, 1), :] = value[hid : hid + 1, c * LANES : (c + 1) * LANES]

        count = p.rows(name) // step
        if count > 1:
            pl.loop(0, count)(part)
        else:
            part(0)

    def square_slice(name, index):
        gradient_slice(name, index - 1, g_refs[index], p.start(name, section))

    def back(index, product, after=nothing):
        def finish(source, lanes):
            for r in range(0, hid, strip):
                rows = slice(r, r + strip)
                g_refs[index][rows, lanes] = (source[rows, :] * g_refs[index][rows, lanes].astype(F32)).astype(BF16)

        return nothing, product, finish, after

    def times(name, index):
        at = p.at[name]
        return lambda lanes: dot(w_ref[:, at : at + hid], g_refs[index][:, lanes])

    if groups:
        cuts = (0, p.slice_at["head_fore"], p.slice_at["fine_entry"])
        cuts += (p.slice_at["coarse_head"], p.slice_at["coarse_middle"], p.slice_columns)
        width = lambda k: cuts[k + 1] - cuts[k]

        def arrivals(row, k):
            rows = slice(row * per, (row + 1) * per) if isinstance(row, int) else aligned(row * per, per, per)
            if k == 0:
                return split_ref.at[rows, : width(0)]
            first = head_at + cuts[k] - cuts[1]
            return w_ref.at[rows, first : first + width(k)]

        def departures(j, k):
            if k == 0:
                return gknot_ref.at[j * per : (j + 1) * per, : width(0)]
            first = (k * groups + j) * per
            return big_ref.at[first : first + per, : width(k)]

        reduce = Reduce(
            p,
            way,
            per,
            cuts,
            lambda owner, k: w_ref.at[aligned(owner * per, per, per), place + cuts[k] : place + cuts[k + 1]],
            arrivals,
            lambda j, k: arrivals(groups + j, k),
            departures,
            stage_ref,
            slices_out,
            reduce_send,
            reduce_recv,
            keep_sems,
        )
        reduce_bias = ReduceBias(way, head_bias_ref, bias_in, bias_far, bias_out, bias_send, bias_recv)
        kept[0].wait()
        gather.sent(2)
        gather.sent(3)

    gradient_slice("head_back", 5, big_ref, p.start("head_back", section), 2 * LANES, -1.0)
    if groups:
        pl.semaphore_wait(ready.at[0], len(way.all()))
        reduce.first(0)
    complete(5, 6)
    looped(fore(0), fore(1))
    if groups:
        kept.append(keep("fine_head", p.wide_out, 11))
        kept[1].start()
        reduce.second(0)

    adjoint(p.low, p.wide_out - p.low, True)
    looped(back(5, lambda lanes: -dot(w_ref[:, head_at : head_at + p.wide_out], big_ref[:, lanes])))
    if groups:
        kept[1].wait()
        for k in (0, 1, 4, 5, 6):
            gather.sent(k)
        signal(ready.at[1], way.all())
    looped(back(4, times("fine_upper", 5)))
    gradient_slice("head_fore", 5, big_ref, p.start("head_fore", section) + p.low, LANES, -1.0)
    square_slice("fine_upper", 5)
    square_slice("fine_middle", 4)
    if groups:
        pl.semaphore_wait(ready.at[1], len(way.all()))
        reduce.first(1)
    looped(back(3, times("fine_middle", 4)))
    gfine_copy.start()
    gradient_slice("fine_entry", g_refs[3], r1_ref, p.start("fine_entry", section) - first_pair * p.pair, 2 * LANES)
    if groups:
        reduce.first(2)
        reduce.second(1)
        reduce.third(0)
        reduce.sent_far(0)
    gknot_ref[p.knot_rows :, :] = jnp.zeros((p.theta_wide - p.knot_rows, windows), BF16)

    def knots_done(source, lanes):
        for r in range(0, p.knot_rows, strip):
            rows = slice(r, r + strip)
            gknot_ref[rows, lanes] = (gtheta_ref[rows, lanes] - source[rows, :]).astype(BF16)

    looped(
        (nothing, lambda lanes: dot(pw_ref[: p.knot_rows, :], g_refs[3][:, lanes]), knots_done, nothing),
        back(2, lambda lanes: dot(w_ref[:, at_head : at_head + p.theta_wide], gknot_ref[:, lanes])),
    )
    gradient_slice("coarse_head", 2, gknot_ref, p.start("coarse_head", section))
    square_slice("coarse_upper", 2)
    if groups:
        reduce.first(3)
        reduce.second(2)
    looped(back(1, times("coarse_upper", 2)))
    if groups:
        reduce.third(1)
        reduce.second(3)
    square_slice("coarse_middle", 1)
    looped(back(0, times("coarse_middle", 1)))
    gradient_slice("coarse_entry", g_refs[0], pooled_ref, p.start("coarse_entry", section))
    if groups:
        reduce.first(4)
        reduce_bias.to_partner().start()
        reduce.second(4)
        reduce_bias.second()

    def pool_gradient(source, lanes):
        for r in range(0, p.pool_wide, strip):
            pooled_ref[r : r + strip, lanes] = (source[r : r + strip, :] * (1.0 / POOL)).astype(BF16)

    looped(
        (
            lambda: turn_weight(at_entry, p.pool_wide),
            lambda lanes: dot(turned_ref[: p.pool_wide, :], g_refs[0][:, lanes]),
            pool_gradient,
            nothing,
        )
    )
    pool_copy.start()
    if groups:
        reduce.third(2)
        reduce_bias.third()
        reduce.third(3)
        reduce.third(4)
        for k in range(reduce.chunks):
            reduce.complete(k)
            reduce.sent(k)
            if k > 0:
                reduce.sent_far(k)
        reduce_bias.complete()
    else:
        out = load(w_ref.at[:, place : place + p.slice_columns], slice_out, 10)
        out.start()
        out.wait()
    theta_copy.wait()
    h3_copy.wait()
    gfine_copy.wait()
    pool_copy.wait()


ANY = pl.BlockSpec(memory_space=pl.ANY)
VMEM = pl.BlockSpec(memory_space=pltpu.VMEM)


def core(plan, per, groups, history, cotangent, targets, horizon, coarse_bias, fine_bias, weights):
    p = plan
    hid, windows = p.hidden, p.windows
    flops = 2 * windows * hid * (2 * p.length + 2 * p.wide_out // 3 + 12 * hid + p.slice_columns)
    out_shape = [
        jax.ShapeDtypeStruct((p.knot_rows, windows), F32),
        jax.ShapeDtypeStruct((hid, windows), BF16),
        jax.ShapeDtypeStruct((hid, windows), BF16),
        jax.ShapeDtypeStruct((p.pool_wide, windows), BF16),
    ]
    out_specs = [ANY] * 4
    scratch = [
        pltpu.VMEM((hid, p.columns), BF16),
        pltpu.VMEM((p.wide_out, windows), BF16),
        *[pltpu.VMEM((hid + ONES, windows), BF16)] * 6,
        *[pltpu.VMEM((hid, windows), BF16)] * 6,
        pltpu.VMEM((p.r1_pairs * p.pair, windows), BF16),
        pltpu.VMEM((p.pool_wide, windows), BF16),
        pltpu.VMEM((2 * p.theta_wide, windows), BF16),
        pltpu.VMEM((p.knot_rows, windows), F32),
        pltpu.VMEM((p.knot_rows, windows), F32),
        pltpu.VMEM((p.theta_wide, windows), BF16),
        pltpu.VMEM((p.theta_wide, hid), BF16),
        pltpu.VMEM((hid, p.theta_wide), BF16),
        pltpu.VMEM((hid, hid), BF16),
        pltpu.VMEM((hid, min(512, windows // 2)), F32),
        pltpu.VMEM((hid, min(512, windows // 2)), F32),
        pltpu.VMEM((hid, LANES), F32),
        pltpu.VMEM(horizon.shape, jnp.int32),
        pltpu.VMEM((1, windows), jnp.int32),
        pltpu.VMEM(coarse_bias.shape, F32),
        pltpu.VMEM(fine_bias.shape, F32),
        pltpu.SemaphoreType.DMA((13,)),
    ]
    params = {}
    if groups:
        bias = (p.bias_rows, LANES)
        out_shape += [
            jax.ShapeDtypeStruct((hid, p.columns), BF16),
            jax.ShapeDtypeStruct((4, per, p.slice_columns), BF16),
            jax.ShapeDtypeStruct((4,) + bias, F32),
        ]
        out_specs += [ANY, ANY, VMEM]
        chunks, reduce_chunks = 7, 5
        scratch += [pltpu.VMEM(piece.shape, F32) for piece in weights]
        scratch += [
            pltpu.SemaphoreType.DMA((len(weights),)),
            pltpu.SemaphoreType.DMA((chunks, groups - 1, 6)),
            pltpu.SemaphoreType.DMA((chunks, groups - 1, 4)),
            pltpu.SemaphoreType.DMA((chunks, groups)),
            pltpu.VMEM(bias, F32),
            pltpu.VMEM(bias, F32),
            pltpu.VMEM((groups,) + bias, F32),
            pltpu.VMEM((per, p.slice_columns), BF16),
            pltpu.SemaphoreType.REGULAR((2,)),
            pltpu.SemaphoreType.DMA((reduce_chunks, max(groups, 3), 3)),
            pltpu.SemaphoreType.DMA((reduce_chunks, max(groups, 3), 3)),
            pltpu.SemaphoreType.DMA((groups + 3,)),
            pltpu.SemaphoreType.DMA((groups + 3,)),
            pltpu.SemaphoreType.DMA((reduce_chunks,)),
        ]
        params = {"collective_id": 0, "has_side_effects": True}
    else:
        out_shape += [jax.ShapeDtypeStruct((hid, p.slice_columns), BF16), jax.ShapeDtypeStruct((p.bias_rows, LANES), F32)]
        out_specs += [ANY, VMEM]
    return pl.pallas_call(
        functools.partial(core_kernel, p, per, groups),
        out_shape=tuple(out_shape),
        in_specs=[ANY] * (6 + len(weights)),
        out_specs=tuple(out_specs),
        scratch_shapes=scratch,
        compiler_params=pltpu.CompilerParams(vmem_limit_bytes=63 * MIB, **params),
        cost_estimate=pl.CostEstimate(flops=flops, bytes_accessed=windows * p.length * 4, transcendentals=0),
    )(history, cotangent, targets, horizon, coarse_bias, fine_bias, *weights)


def outputs_kernel(
    plan,
    block,
    steps,
    packed_ref,
    history_ref,
    cotangent_ref,
    theta_ref,
    h3_ref,
    gfine_ref,
    pool_ref,
    fine_bias_ref,
    slices_ref,
    bias_rows_ref,
    residual_ref,
    history_grad_ref,
    prediction_ref,
    *refs,
):
    grads = refs[:16]
    head_ref, entry_ref, side_ref, pool_grad, fore_ref, *products, turned_head, turned_entry, bias_ref, sems = refs[16:]
    back_refs, fine_refs = products[:2], products[2:]
    p = plan
    step = pl.program_id(0)
    windows = p.windows
    chunk = min(512, windows)
    chunks = windows // chunk
    lanes_of = lambda n: slice(n * chunk, (n + 1) * chunk) if isinstance(n, int) else aligned(n * chunk, chunk, chunk)
    knots = block // KNOT
    pooled = block // POOL
    rest, later = fractions(chunk)

    def fetch(name, out, at, slot, sem):
        first = aligned(p.at[name] + at * block, block, LANES)
        return pltpu.make_async_copy(packed_ref.at[:, first], out.at[slot], sems.at[sem, slot])

    def interpolate(k, count, base, lanes):
        low = jnp.minimum if not isinstance(k, int) else min
        own = theta_ref[pl.ds(base + low(k, count - 1), 1), lanes]
        after = theta_ref[pl.ds(base + low(k + 1, count - 1), 1), lanes]
        return own * rest + after * later

    fore_out = pltpu.make_async_copy(fore_ref, prediction_ref, sems.at[3, 0])
    wide = p.wide_out - p.low
    first_fore = p.at["fine_head"] + p.low
    side = pltpu.make_async_copy(packed_ref.at[:, first_fore : first_fore + wide], side_ref, sems.at[2, 0])

    @pl.when(step == 0)
    def _():
        fetch("fine_head", head_ref, 0, 0, 0).start()
        fetch("fine_entry", entry_ref, 0, 0, 1).start()
        side.start()
        pool_grad[...] = pool_ref[...].astype(F32)

    @pl.when(step == 2)
    def _():
        side.wait()
        turned_fore = side_ref[...].T
        fore_bias = column_of(fine_bias_ref, p.low, wide)

        @pl.loop(0, chunks)
        def _(n):
            lanes = lanes_of(n)
            back_refs[0][: p.horizon, :] = dot(turned_fore[p.skip : p.skip + p.horizon], h3_ref[:, lanes])
            for k in range(0, p.fore, 2):
                rows = slice(k * KNOT, (k + 2) * KNOT)
                second = back_refs[0][rows, :] + fore_bias[p.skip + k * KNOT : p.skip + (k + 2) * KNOT]
                first = jnp.concatenate([interpolate(k + j, p.fore, p.back, lanes) for j in range(2)], axis=0)
                fore_ref[rows, lanes] = first.astype(BF16).astype(F32) + second.astype(BF16).astype(F32)

        fore_out.start()

    @pl.when(step == 1)
    def _():
        unpack(p, slices_ref, bias_rows_ref, grads)

    slot = step % 2

    @pl.when(step + 1 < steps)
    def _():
        fetch("fine_head", head_ref, step + 1, 1 - slot, 0).start()
        fetch("fine_entry", entry_ref, step + 1, 1 - slot, 1).start()

    fetch("fine_head", head_ref, step, slot, 0).wait()
    fetch("fine_entry", entry_ref, step, slot, 1).wait()
    turned_head[...] = head_ref[slot].T
    turned_entry[...] = entry_ref[slot].T
    row = jnp.broadcast_to(fine_bias_ref[:, aligned(step * block, block, LANES)], (8, block))
    bias_ref[...] = row.T[:, :1]
    pair = 2 * KNOT

    def make(n, place):
        lanes = lanes_of(n)
        back_refs[place][...] = dot(turned_head[...], h3_ref[:, lanes])
        fine_refs[place][...] = dot(turned_entry[...], gfine_ref[:, lanes])

    def finish(n, place):
        lanes = lanes_of(n)
        for at in range(0, block, pair):
            rows = slice(at, at + pair)
            k = step * knots + at // KNOT
            made = jnp.concatenate([interpolate(k + j, p.back, 0, lanes) for j in range(2)], axis=0)
            back = back_refs[place][rows, :] + bias_ref[rows, :]
            residual_ref[rows, lanes] = (history_ref[rows, lanes].astype(F32) - made - back).astype(BF16)
            first = step * pooled + at // POOL
            spread = jnp.concatenate(
                [jnp.broadcast_to(pool_grad[pl.ds(first + j, 1), lanes], (POOL, chunk)) for j in range(pair // POOL)],
                axis=0,
            )
            fine = fine_refs[place][rows, :] + spread
            history_grad_ref[rows, lanes] = (cotangent_ref[rows, lanes].astype(F32) + fine).astype(BF16)

    for n in range(chunks + 1):
        if n < chunks:
            make(n, n % 2)
        if n > 0:
            finish(n - 1, (n - 1) % 2)

    @pl.when(step == steps - 1)
    def _():
        fore_out.wait()


def outputs(plan, packed, history, cotangent, theta, h3, gfine, pool, fine_bias, slices, bias_rows):
    p = plan
    hid, windows = p.hidden, p.windows
    block = 6 * LANES
    steps = -(-p.length // block)
    rows = pl.BlockSpec((block, windows), lambda i: (i, 0))
    wide = p.wide_out - p.low
    per = slices.shape[1]
    square, vector = (per, hid), (1, per)
    grads = []
    for entry, out in ((p.pooled, p.coarse_out), (p.length, p.fine_out)):
        grads += [(per, entry), vector, square, vector, square, vector, (per, out), (1, out)]
    return pl.pallas_call(
        functools.partial(outputs_kernel, p, block, steps),
        grid=(steps,),
        out_shape=(
            jax.ShapeDtypeStruct((p.length, windows), BF16),
            jax.ShapeDtypeStruct((p.length, windows), BF16),
            jax.ShapeDtypeStruct((p.horizon, windows), F32),
        )
        + tuple(jax.ShapeDtypeStruct(shape, F32) for shape in grads),
        in_specs=[ANY, rows, rows, VMEM, VMEM, VMEM, VMEM, VMEM, VMEM, VMEM],
        out_specs=(rows, rows, ANY) + (VMEM,) * len(grads),
        scratch_shapes=[
            pltpu.VMEM((2, hid, block), BF16),
            pltpu.VMEM((2, hid, block), BF16),
            pltpu.VMEM((hid, wide), BF16),
            pltpu.VMEM((p.pool_wide, windows), F32),
            pltpu.VMEM((p.horizon, windows), F32),
            *[pltpu.VMEM((block, min(512, windows)), F32)] * 4,
            pltpu.VMEM((block, hid), BF16),
            pltpu.VMEM((block, hid), BF16),
            pltpu.VMEM((block, 1), F32),
            pltpu.SemaphoreType.DMA((4, 2)),
        ],
        compiler_params=pltpu.CompilerParams(vmem_limit_bytes=56 * MIB),
        cost_estimate=pl.CostEstimate(
            flops=2 * windows * hid * (2 * p.length + p.horizon), bytes_accessed=windows * p.length * 8, transcendentals=0
        ),
    )(packed, history, cotangent, theta, h3, gfine, pool, fine_bias, slices, bias_rows)


def pack(plan, arrays, biases):
    p = plan
    names = sorted(p.at, key=p.at.get)
    ends = [p.at[name] for name in names[1:]] + [p.columns]
    columns = []
    for name, end in zip(names, ends):
        piece = arrays[name] if name != "bias" else biases
        columns.append(jnp.pad(piece.astype(BF16), ((0, 0), (0, end - p.at[name] - piece.shape[1]))))
    return jnp.concatenate(columns, axis=1)


def unpack(plan, slices_ref, bias_rows_ref, grads):
    p = plan
    hid = p.hidden

    def joined(name, out, source, row=None, base=0, low=0, high=None):
        high, done = out.shape[1] if high is None else high, low
        for section in range(p.sections):
            first = base + p.start(name, section)
            last = min(first + p.rows(name), high)
            if row is not None:
                for at in range(max(done // LANES * LANES, first), last, LANES):
                    begin, end = max(at, done), min(at + LANES, last)
                    if begin < end:
                        here = source[section, pl.ds(row + (at - first) // LANES, 1), :]
                        out[:, begin:end] = here[:, begin - at : end - at]
            elif done < last:
                at = p.slice_at[name] + done - first
                out[:, done:last] = source[section, :, at : at + last - done].astype(F32)
            done = max(done, last)

    def ones_column(name, row):
        section = p.sections - 1
        at = p.slice_at[name] + row - p.start(name, section)
        block = slices_ref[section, :, at // LANES * LANES : at // LANES * LANES + LANES].astype(F32)
        return block.T[at % LANES : at % LANES + 1]

    def own_part(name, out):
        per = out.shape[1]
        width = min(per, LANES)
        share = p.part[name][0]
        for at in range(0, per, width):
            first = lax.axis_index("dp") * per + at
            block = first // LANES
            row = bias_rows_ref[block // share, pl.ds(p.bias_at[name] + block % share, 1), :]
            wide = jnp.broadcast_to(row, (8, LANES))
            out[:, at : at + width] = pltpu.roll(wide, (LANES - first % LANES) % LANES, 1)[:1, :width]

    for base, block in ((0, "coarse_"), (8, "fine_")):
        entry, head = block + "entry", block + "head"
        joined(entry, grads[base], slices_ref)
        grads[base + 1][...] = ones_column(entry, grads[base].shape[1])
        for i, name in enumerate((block + "middle", block + "upper")):
            joined(name, grads[base + 2 + 2 * i], slices_ref)
            own_part(name, grads[base + 3 + 2 * i])
        for number, source in ((6, slices_ref), (7, bias_rows_ref)):
            row = lambda name: p.bias_at[name] if number == 7 else None
            if base == 0:
                joined(head, grads[number], source, row(head))
            else:
                joined("head_back", grads[8 + number], source, row("head_back"), 0, 0, p.length)
                joined("head_fore", grads[8 + number], source, row("head_fore"), p.low, p.length)


def body(mesh_shape, history, targets, horizon, cotangent, *params):
    (c_entry, c_entry_b, c_middle, c_middle_b, c_upper, c_upper_b, c_head, c_head_b) = params[:8]
    (f_entry, f_entry_b, f_middle, f_middle_b, f_upper, f_upper_b, f_head, f_head_b) = params[8:]
    sections = mesh_shape["section"]
    length, hidden = f_entry.shape[0], c_middle.shape[1]
    p = Plan(
        length, f_head.shape[1] - length, hidden, c_entry.shape[0], c_head.shape[1], sections, history.shape[0]
    )
    pieces = (c_entry.T, c_middle, c_upper, c_head, f_entry.T, f_middle, f_upper, f_head)
    bias_pieces = (c_entry_b, c_middle_b, c_upper_b, f_entry_b, f_middle_b, f_upper_b)
    dp_count, per = mesh_shape["dp"], c_middle.shape[0]
    rows = (history.T, cotangent.T)
    fine_bias = f_head_b[None, :]
    rest = (targets.T, horizon.reshape(-1, LANES), c_head_b[None, :], fine_bias)
    groups = dp_count // 2
    if sections == 4 and dp_count % 2 == 0 and per % 64 == 0 and groups > 1:
        theta, h3, gfine, pool, packed, slices, bias_rows = core(
            p, per, groups, *rows, *rest, pieces + tuple(b[None, :] for b in bias_pieces)
        )
    else:
        packed = pack(p, dict(zip(NAMES, pieces)), jnp.stack(bias_pieces, axis=1))
        packed = lax.all_gather(packed, "dp", axis=0, tiled=True)
        theta, h3, gfine, pool, part, head_bias = core(p, per, 0, *rows, *rest, (packed,))
        own = lax.psum_scatter(part.astype(F32), "dp", scatter_dimension=0, tiled=True)
        slices = lax.all_gather(own, "section", axis=0)
        bias_rows = lax.all_gather(lax.psum(head_bias, "dp"), "section", axis=0)
    residual, history_grad, prediction, *grads = outputs(
        p, packed, *rows, theta, h3, gfine, pool, fine_bias, slices, bias_rows
    )
    grads = [g.T if i in (0, 8) else g if g.shape[0] > 1 else g[0] for i, g in enumerate(grads)]
    return (prediction.T, residual.T, history_grad.T) + tuple(grads)


def solution(mesh):
    by_row, by_column, by_entry, copied = P("dp", None), P(None, "dp"), P("dp"), P()
    block = (by_column, by_entry, by_row, by_entry, by_row, by_entry, by_row, copied)
    in_specs = (by_row, by_row, by_entry, by_row) + block + block
    out_specs = (by_row, by_row, by_row) + block + block
    return jax.shard_map(
        functools.partial(body, dict(mesh.shape)), mesh=mesh, in_specs=in_specs, out_specs=out_specs, check_vma=False
    )
```

```python
import functools

import jax
import jax.numpy as jnp
from jax import lax
from jax.experimental import pallas as pl
from jax.experimental.pallas import tpu as pltpu
from jax.sharding import PartitionSpec as P

POOL = 8
KNOT = 24
LANES = 128
ONES = 16
GELU_A = 0.7978845608028654
GELU_B = GELU_A * 0.044715
F32 = jnp.float32
BF16 = jnp.bfloat16
MIB = 1 << 20


def up(size, unit):
    return -(-size // unit) * unit


class Plan:
    def __init__(self, length, horizon, hidden, pooled, coarse_out, sections, windows):
        self.length, self.horizon, self.hidden = length, horizon, hidden
        self.pooled, self.coarse_out = pooled, coarse_out
        self.fine_out = length + horizon
        self.sections, self.windows = sections, windows
        self.back, self.fore = length // KNOT, horizon // KNOT
        self.wide_in, self.wide_out = up(length + 1, LANES), up(self.fine_out + 1, LANES)
        self.pool_wide, self.theta_wide = up(pooled + 1, LANES), up(coarse_out + 1, LANES)
        widths = [
            ("coarse_entry", self.pool_wide),
            ("bias", LANES),
            ("coarse_middle", hidden),
            ("coarse_upper", hidden),
            ("coarse_head", self.theta_wide),
            ("fine_entry", self.wide_in),
            ("fine_middle", hidden),
            ("fine_upper", hidden),
            ("fine_head", self.wide_out),
        ]
        self.at, place = {}, 0
        for name, width in widths:
            self.at[name] = place
            place += width
        self.columns = place
        self.low = length // LANES * LANES
        self.skip = length - self.low
        self.square = hidden // sections
        self.slice_at, self.part, place = {}, {}, 0
        for name, width in (
            ("head_back", self.wide_in),
            ("head_fore", self.wide_out - self.low),
            ("fine_upper", hidden),
            ("fine_middle", hidden),
            ("fine_entry", self.wide_in),
            ("coarse_head", self.theta_wide),
            ("coarse_upper", hidden),
            ("coarse_middle", hidden),
            ("coarse_entry", self.pool_wide),
        ):
            self.slice_at[name] = place
            total = width // LANES
            share = -(-total // sections)
            self.part[name] = share, total
            place += share * LANES
        self.slice_columns = place
        self.bias_at, place = {}, 0
        for name in ("head_back", "head_fore", "coarse_head", "coarse_middle", "coarse_upper", "fine_middle", "fine_upper"):
            self.bias_at[name] = place
            place += self.part[name][0]
        self.bias_rows = up(place, 8)
        self.knot_rows = up(coarse_out, ONES)
        self.pair = 2 * KNOT
        self.r1_pairs = -(-(self.rows("fine_entry") + self.pair - ONES) // self.pair)

    def rows(self, name):
        return self.part[name][0] * LANES

    def start(self, name, section):
        low = min if isinstance(section, int) else jnp.minimum
        share, total = self.part[name]
        return low(section * share, total - share) * LANES


def gelu_both(a):
    square = a * a
    v = 0.5 + 0.5 * jnp.tanh(a * (GELU_A + GELU_B * square))
    h = a * v
    return h, v + h * (1.0 - v) * (2.0 * GELU_A + (6.0 * GELU_B) * square)


def dot(a, b):
    return jnp.dot(a, b, preferred_element_type=F32)


def dot_rows(a, b):
    return lax.dot_general(a, b, (((1,), (1,)), ((), ())), preferred_element_type=F32)


def aligned(start, size, unit):
    return pl.ds(pl.multiple_of(start, unit), size)


def column_of(row_ref, first, count):
    size = row_ref.shape[1]
    columns = []
    for at in range(first, first + count, LANES):
        width = max(0, min(LANES, size - at))
        row = jnp.zeros((1, LANES), F32) if width == 0 else row_ref[:, at : at + width]
        if 0 < width < LANES:
            row = jnp.concatenate([row, jnp.zeros((1, LANES - width), F32)], axis=1)
        columns.append(jnp.broadcast_to(row, (LANES, LANES)).T[:, :1])
    return jnp.concatenate(columns, axis=0)


def hat_weights(first, count, plan, turned=False, fore=False):
    p = plan
    shape = (p.knot_rows, count) if turned else (count, p.theta_wide)
    row = lax.broadcasted_iota(jnp.int32, shape, 1 if turned else 0) + first
    knot = lax.broadcasted_iota(jnp.int32, shape, 0 if turned else 1)
    away = row - KNOT * knot
    weight = jnp.maximum(KNOT - jnp.abs(away), 0)
    last = (knot == p.back - 1) | (knot == p.back + p.fore - 1)
    weight = jnp.where(last & (away > 0) & (away < KNOT), KNOT, weight)
    own = (knot >= p.back) & (row >= p.length) if fore else (knot < p.back) & (row < p.length)
    inside = own & (row < p.fine_out) & (knot < p.back + p.fore)
    return jnp.where(inside, weight, 0).astype(F32).astype(BF16)


def fractions(width):
    later = lax.broadcasted_iota(jnp.int32, (KNOT, width), 0).astype(F32) * (1.0 / KNOT)
    return 1.0 - later, later


NAMES = (
    "coarse_entry",
    "coarse_middle",
    "coarse_upper",
    "coarse_head",
    "fine_entry",
    "fine_middle",
    "fine_upper",
    "fine_head",
)
KEPT = ("fine_entry", "fine_head")


def remote(source, target, send_sem, recv_sem, place):
    return pltpu.make_async_remote_copy(
        src_ref=source,
        dst_ref=target,
        send_sem=send_sem,
        recv_sem=recv_sem,
        device_id=place,
        device_id_type=pl.DeviceIdType.MESH,
    )


def signal(semaphore, places):
    for place in places:
        pl.semaphore_signal(semaphore, inc=1, device_id=place, device_id_type=pl.DeviceIdType.MESH)


class Ways:
    def __init__(self, groups):
        self.section, self.dp = lax.axis_index("section"), lax.axis_index("dp")
        self.group, self.core = self.dp // 2, self.dp % 2
        self.groups = groups
        self.partner = (self.section, self.group * 2 + 1 - self.core)
        s = self.section
        self.side = [s + 1 - 2 * (s % 2), (s + 2) % 4]
        self.sides = [(t, self.dp) for t in self.side]
        self.across = 3 - s
        self.corner = (self.across, self.dp)

    def far(self, j):
        group = (self.group + j) % self.groups
        return group, (self.section, group * 2 + self.core)

    def from_far(self, j):
        return (self.group + self.groups - j) % self.groups

    def all(self):
        return [self.partner, self.corner] + self.sides + [self.far(j)[1] for j in range(1, self.groups)]


class Gather:
    def __init__(self, plan, way, per, cuts, w_ref, shards, biases, send, recv, partner_recv):
        self.p, self.way, self.per, self.cuts, self.w_ref = plan, way, per, cuts, w_ref
        self.shards, self.biases = shards, biases
        self.send, self.recv, self.partner_recv = send, recv, partner_recv
        self.near = range(1, way.groups)
        self.chunks, self.ahead = len(cuts) - 1, 3

    def at(self, k, owner, s=None):
        quarter = self.per // 4
        rows = aligned(owner * self.per, self.per, self.per)
        if s is not None:
            rows = aligned(owner * self.per + s * quarter, quarter, quarter)
        return self.w_ref.at[rows, self.cuts[k] : self.cuts[k + 1]]

    def source(self, j):
        return self.way.from_far(j) * 2 + self.way.core

    def copy(self, here, k, j, kind, place):
        return remote(here, here, self.send.at[k, j - 1, kind], self.recv.at[k, j - 1, kind], place)

    def to_far(self, k, j):
        return self.copy(self.at(k, self.way.dp, self.way.section), k, j, 0, self.way.far(j)[1])

    def to_side(self, k, j, i):
        return self.copy(self.at(k, self.source(j), self.way.section), k, j, 1 + i, self.way.sides[i])

    def to_across(self, k, j):
        if k == 0:
            return self.copy(self.at(k, self.source(j), self.way.section), k, j, 3, self.way.corner)
        i = (k + j) % 2
        return self.copy(self.at(k, self.source(j), self.way.side[i]), k, j, 3, self.way.sides[1 - i])

    def to_partner(self, k, j):
        here = self.at(k, self.source(j) if j else self.way.dp)
        return remote(here, here, self.send.at[k, max(j - 1, 0), 4 if j else 5], self.partner_recv.at[k, j], self.way.partner)

    def arrived(self, k, j, kind):
        s = [self.way.section, self.way.side[0], self.way.side[1], self.way.across][kind]
        self.copy(self.at(k, self.source(j), s), k, j, kind, self.way.partner).wait_recv()

    def cast(self, k):
        p, own = self.p, aligned(self.way.dp * self.per, self.per, self.per)
        low, high = self.cuts[k], self.cuts[k + 1]
        for ref, name in zip(self.shards, NAMES):
            at, size = p.at[name], ref.shape[1]
            wide = up(size + 1, LANES) if name.endswith(("entry", "head")) else size
            first, last = max(at, low), min(at + wide, high)
            full = min(last, at + size // LANES * LANES)
            if first < full:
                self.w_ref[own, first:full] = ref[:, first - at : full - at].astype(BF16)
            if first < last and last > full:
                rest = ref[:, full - at : size].astype(BF16)
                pad = jnp.zeros((self.per, last - at - size), BF16)
                self.w_ref[own, full:last] = jnp.concatenate([rest, pad], axis=1)
        at = p.at["bias"]
        if low <= at < high:
            count = len(self.biases)
            rows = jnp.concatenate([ref[...] for ref in self.biases] + [jnp.zeros((8 - count, self.per), F32)], axis=0)
            wide = jnp.concatenate([rows, jnp.zeros((8, LANES - self.per), F32)], axis=1)
            wide = jnp.concatenate([wide, jnp.zeros((LANES - 8, LANES), F32)], axis=0)
            self.w_ref[own, at : at + LANES] = wide.T[: self.per].astype(BF16)

    def first(self, k):
        self.cast(k)
        for j in self.near:
            self.to_far(k, j).start()
        self.to_partner(k, 0).start()

    def second(self, k):
        for j in self.near:
            self.arrived(k, j, 0)
            for i in range(2):
                self.to_side(k, j, i).start()
            if k == 0:
                self.to_across(k, j).start()

    def third(self, k):
        for j in self.near:
            self.arrived(k, j, 1)
            self.arrived(k, j, 2)
            if k > 0:
                self.to_across(k, j).start()

    def fourth(self, k):
        for j in self.near:
            self.arrived(k, j, 3)
            self.to_partner(k, j).start()

    def complete(self, k):
        for j in range(self.way.groups):
            there = (self.way.from_far(j) * 2 + 1 - self.way.core) if j else self.way.partner[1]
            here = self.at(k, there)
            remote(here, here, self.send.at[k, 0, 5], self.partner_recv.at[k, j], self.way.partner).wait_recv()

    def sent(self, k):
        for j in self.near:
            for copy in (self.to_far(k, j), self.to_side(k, j, 0), self.to_side(k, j, 1), self.to_across(k, j)):
                copy.wait_send()
            self.to_partner(k, j).wait_send()
        self.to_partner(k, 0).wait_send()


class Reduce:
    def __init__(self, plan, way, per, cuts, part_ref, core_in, far_in, far_out, stage_ref, out_ref, send, recv, local):
        self.p, self.way, self.per, self.cuts = plan, way, per, cuts
        self.part_ref, self.core_in, self.far_in, self.far_out = part_ref, core_in, far_in, far_out
        self.stage_ref, self.out_ref, self.send, self.recv, self.local = stage_ref, out_ref, send, recv, local
        self.near = range(1, way.groups)
        self.chunks = len(cuts) - 1

    def columns(self, k):
        return slice(self.cuts[k], self.cuts[k + 1])

    def to_partner(self, k, g):
        return remote(
            self.part_ref(g * 2 + 1 - self.way.core, k),
            self.core_in(g, k),
            self.send.at[k, g, 0],
            self.recv.at[k, g, 0],
            self.way.partner,
        )

    def to_far(self, k, j):
        here, there = self.far_out(j - 1, k), self.far_in(j - 1, k)
        return remote(here, there, self.send.at[k, j - 1, 1], self.recv.at[k, j - 1, 1], self.way.far(j)[1])

    def side(self, k, source, i, to):
        here = self.out_ref.at[source, :, self.columns(k)]
        return remote(here, here, self.send.at[k, i, 2], self.recv.at[k, i, 2], to)

    def to_side(self, k, i):
        here = self.stage_ref.at[:, self.columns(k)]
        there = self.out_ref.at[self.way.section, :, self.columns(k)]
        place = (self.way.sides + [self.way.corner])[i]
        return remote(here, there, self.send.at[k, i, 2], self.recv.at[k, i, 2], place)

    def keep(self, k):
        there = self.out_ref.at[self.way.section, :, self.columns(k)]
        return pltpu.make_async_copy(self.stage_ref.at[:, self.columns(k)], there, self.local.at[k])

    def summed(self, k, group):
        own = self.part_ref(group * 2 + self.way.core, k)[...].astype(F32)
        return own + self.core_in(group, k)[...].astype(F32)

    def first(self, k):
        for g in range(self.way.groups):
            self.to_partner(k, g).start()

    def second(self, k):
        for g in range(self.way.groups):
            self.to_partner(k, g).wait_recv()
        for j in self.near:
            self.far_out(j - 1, k)[...] = self.summed(k, self.way.far(j)[0]).astype(BF16)
            self.to_far(k, j).start()

    def third(self, k):
        total = self.summed(k, self.way.group)
        for j in self.near:
            self.to_far(k, j).wait_recv()
            total += self.far_in(j - 1, k)[...].astype(F32)
        self.stage_ref[:, self.columns(k)] = total.astype(BF16)
        for i in range(3):
            self.to_side(k, i).start()
        self.keep(k).start()

    def complete(self, k):
        for i, source in enumerate(self.way.side + [self.way.across]):
            self.side(k, source, i, self.way.partner).wait_recv()

    def sent_far(self, k):
        for j in self.near:
            self.to_far(k, j).wait_send()

    def sent(self, k):
        for g in range(self.way.groups):
            self.to_partner(k, g).wait_send()
        for i in range(3):
            self.to_side(k, i).wait_send()
        self.keep(k).wait()


class ReduceBias:
    def __init__(self, way, own_ref, core_in, far_ref, out_ref, send, recv):
        self.way, self.own_ref, self.core_in, self.far_ref, self.out_ref = way, own_ref, core_in, far_ref, out_ref
        self.send, self.recv = send, recv
        self.near = range(1, way.groups)

    def copy(self, here, there, n, place):
        return remote(here, there, self.send.at[n], self.recv.at[n], place)

    def to_partner(self):
        return self.copy(self.own_ref, self.core_in, 0, self.way.partner)

    def to_far(self, j):
        here = self.far_ref.at[self.way.group]
        return self.copy(here, here, j, self.way.far(j)[1])

    def side(self, source, n, to):
        here = self.out_ref.at[source]
        return self.copy(here, here, self.way.groups + n, to)

    def to_side(self, i):
        return self.side(self.way.section, i, (self.way.sides + [self.way.corner])[i])

    def second(self):
        self.to_partner().wait_recv()
        self.far_ref[self.way.group] = self.own_ref[...] + self.core_in[...]
        for j in self.near:
            self.to_far(j).start()

    def third(self):
        for j in self.near:
            here = self.far_ref.at[self.way.from_far(j)]
            self.copy(here, here, j, self.way.partner).wait_recv()
        total = self.far_ref[0]
        for g in range(1, self.way.groups):
            total += self.far_ref[g]
        self.out_ref[self.way.section] = total
        for i in range(3):
            self.to_side(i).start()

    def complete(self):
        for i, source in enumerate(self.way.side + [self.way.across]):
            self.side(source, i, self.way.partner).wait_recv()
        self.to_partner().wait_send()
        for j in self.near:
            self.to_far(j).wait_send()
        for i in range(3):
            self.to_side(i).wait_send()


def core_kernel(plan, per, groups, *refs):
    p = plan
    refs = list(refs)
    take = lambda count: [refs.pop(0) for _ in range(count)]
    history_ref, cotangent_ref, target_ref, horizon_ref, coarse_bias_ref, fine_bias_ref = take(6)
    if groups:
        shards_in = take(14)
    else:
        (packed_ref,) = take(1)
    theta_out, h3_out, gfine_out, pool_out, row_out = take(5)
    if groups:
        kept_out, slices_out, bias_out = take(3)
    else:
        slice_out, bias_out = take(2)
    w_ref, big_ref = take(2)
    h_refs, g_refs = take(6), take(6)
    r1_ref, pooled_ref, split_ref, theta_ref, gtheta_ref, gknot_ref = take(6)
    pw_ref, pwt_ref, turned_ref, even_ref, odd_ref, bias_ref = take(6)
    horizon_rows, horizon_buf, coarse_bias_buf, fine_bias_buf, sems = take(5)
    if groups:
        shards = take(14)
        shard_sems, send, recv, partner_recv = take(4)
        head_bias_ref, bias_in, bias_far, stage_ref, ready, reduce_send, reduce_recv, bias_send, bias_recv = take(9)
        keep_sems = take(1)[0]
    else:
        head_bias_ref = bias_out
    hid, windows = p.hidden, p.windows
    section = lax.axis_index("section")
    chunk = min(512, windows // 2)
    chunks = windows // chunk
    H = slice(0, hid)
    lanes_of = lambda n: aligned(n * chunk, chunk, chunk)
    place = p.at["fine_entry"]
    head_at = p.at["fine_head"]

    load = lambda source, out, sem: pltpu.make_async_copy(source, out, sems.at[sem])
    history_in = load(history_ref, big_ref.at[: p.length], 1)
    cotangent_in = load(cotangent_ref, big_ref.at[: p.length], 2)
    target_in = load(target_ref, big_ref.at[p.length : p.fine_out], 0)
    rows_in = [
        load(horizon_ref, horizon_rows, 3),
        load(coarse_bias_ref, coarse_bias_buf, 4),
        load(fine_bias_ref, fine_bias_buf, 5),
    ]
    theta_copy = load(theta_ref, theta_out, 6)
    h3_copy = load(h_refs[5].at[H], h3_out, 7)
    gfine_copy = load(g_refs[3], gfine_out, 8)
    pool_copy = load(pooled_ref, pool_out, 9)

    if groups:
        shards_load = [
            pltpu.make_async_copy(source, out, shard_sems.at[n]) for n, (source, out) in enumerate(zip(shards_in, shards))
        ]
        order = [0, 1, 2, 3, 8, 9, 10, 11, 12, 13, 4, 5, 6, 7]
        for n in order:
            shards_load[n].start()
        way = Ways(groups)
        middle = p.at["fine_middle"]
        third = (p.columns - middle) // 3 // LANES * LANES
        entry_cut = place + up((middle - place) // 2, LANES)
        cuts = (0, p.at["coarse_middle"], place, entry_cut, middle, middle + third, middle + 2 * third, p.columns)
        gather = Gather(p, way, per, cuts, w_ref, shards[:8], shards[8:], send, recv, partner_recv)
        cotangent_in.start()
        for copy in rows_in:
            copy.start()
        barrier = pltpu.get_barrier_semaphore()
        signal(barrier, way.all())
        for n in order[:10]:
            shards_load[n].wait()
        pl.semaphore_wait(barrier, len(way.all()))
        gather.first(0)
        for n in order[10:]:
            shards_load[n].wait()
        for k in range(1, gather.ahead):
            gather.first(k)
    else:
        weights_in = load(packed_ref, w_ref, 10)
        weights_in.start()
        cotangent_in.start()
        for copy in rows_in:
            copy.start()

    def move(*steps):
        if groups:
            for stage, k in steps:
                {2: gather.second, 3: gather.third, 4: gather.fourth}[stage](k)
                if stage == 2 and k + gather.ahead < gather.chunks:
                    gather.first(k + gather.ahead)

    def complete(*ks):
        if groups:
            for k in ks:
                gather.complete(k)

    tail = p.wide_out - p.length
    mark = lax.broadcasted_iota(jnp.int32, (tail, windows), 0) < POOL
    big_ref[p.length :, :] = mark.astype(F32).astype(BF16)
    pooled_ref[...] = jnp.zeros_like(pooled_ref)
    for index in range(6):
        h_refs[index][hid:, :] = jnp.ones((ONES, windows), BF16)
    for copy in rows_in:
        copy.wait()
    for at in range(0, p.fine_out, LANES):
        part = slice(at, min(at + LANES, p.fine_out))
        row_out[:, part] = fine_bias_buf[part].reshape(1, part.stop - at)
    for n in range(windows // LANES):
        horizon_buf[:, n * LANES : (n + 1) * LANES] = horizon_rows[n : n + 1, :]
    step = 6 * LANES

    def adjoint(first, count, fore):
        hats = hat_weights(first, count, p, True, fore)

        @pl.loop(0, chunks)
        def _(n):
            lanes = lanes_of(n)
            rows = slice(first, first + count) if isinstance(first, int) else aligned(first, count, ONES)
            gtheta_ref[:, lanes] += dot(hats, big_ref[rows, lanes]) * (-1.0 / KNOT)

    cotangent_in.wait()
    gtheta_ref[...] = jnp.zeros_like(gtheta_ref)
    quarter = p.wide_in // 4
    pl.loop(0, 4)(lambda i: adjoint(i * quarter, quarter, False))
    history_in.start()
    move((2, 0), (2, 1), (3, 0))
    history_in.wait()

    unit = hid
    shape = (unit // POOL, unit)
    member = lax.broadcasted_iota(jnp.int32, shape, 1) - POOL * lax.broadcasted_iota(jnp.int32, shape, 0)
    turned_ref[: unit // POOL, :] = ((member >= 0) & (member < POOL)).astype(F32).astype(BF16)
    firsts = list(range(0, p.wide_in, unit))
    for number, first in enumerate(firsts):
        count = min(unit, p.wide_in - first)
        rows = slice(first // POOL, (first + count) // POOL)

        @pl.loop(0, chunks)
        def _(n):
            lanes = lanes_of(n)
            total = dot(turned_ref[: count // POOL, :count], big_ref[first : first + count, lanes])
            pooled_ref[rows, lanes] = (total * (1.0 / POOL)).astype(BF16)

        if number == len(firsts) // 2:
            move((4, 0))
    move((3, 1), (2, 2))
    complete(0)
    if not groups:
        weights_in.wait()
    fore_parts = [(0, 8 * p.pair), (8 * p.pair, p.horizon)]
    fore_bias = column_of(row_out, p.low, p.wide_out - p.low)
    placed = w_ref[:, p.at["bias"] : p.at["bias"] + LANES].astype(F32)
    lane = lax.broadcasted_iota(jnp.int32, (hid, LANES), 1)
    for number, (low, high) in enumerate(fore_parts):
        column = fore_bias[p.skip + low : p.skip + high]
        column = jnp.concatenate([column, jnp.zeros((hid - high + low, 1), F32)], axis=0)
        placed = jnp.where(lane == 6 + number, column, placed)
    bias_ref[...] = placed

    def pipeline(*layers):
        tile, pending = 0, nothing
        for before, produce, finish, after in layers:
            before()
            for n in range(chunks):
                lanes = slice(n * chunk, (n + 1) * chunk)
                out = (even_ref, odd_ref)[tile % 2]
                value = produce(lanes)
                out[: value.shape[0], :] = value
                pending()
                pending = functools.partial(finish, out, lanes)
                tile += 1
            after()
        pending()

    def nothing():
        pass

    def looped(*layers):
        for before, produce, finish, after in layers:
            before()

            @pl.loop(0, chunks)
            def _(n, produce=produce, finish=finish):
                value = produce(lanes_of(n))
                even_ref[: value.shape[0], :] = value
                finish(even_ref, lanes_of(n))

            after()

    def turn_weight(first, count):
        turned_ref[:count, :] = w_ref[:, first : first + count].T

    strip = ONES

    def activate(index):
        def finish(source, lanes):
            for r in range(0, hid, strip):
                rows = slice(r, r + strip)
                h, slope = gelu_both(source[rows, :] + bias_ref[rows, index : index + 1])
                h_refs[index][rows, lanes] = h.astype(BF16)
                g_refs[index][rows, lanes] = slope.astype(BF16)

        return finish

    def hidden(name, index, after=nothing):
        return (
            lambda: turn_weight(p.at[name], hid),
            lambda lanes: dot(turned_ref[H, :], h_refs[index - 1][H, lanes]),
            activate(index),
            after,
        )

    at_entry = p.at["coarse_entry"]
    at_head = p.at["coarse_head"]
    theta_bias = column_of(coarse_bias_buf, 0, p.theta_wide)

    def keep_theta(source, lanes):
        for r in range(0, p.theta_wide, strip):
            rows = slice(r, r + strip)
            theta = source[rows, :] + theta_bias[rows]
            if r < p.knot_rows:
                theta_ref[rows, lanes] = theta
            knots = jnp.where(lax.broadcasted_iota(jnp.int32, theta.shape, 0) + r < p.back, theta, 0.0)
            high = knots.astype(BF16)
            split_ref[rows, lanes] = high
            split_ref[p.theta_wide + r : p.theta_wide + r + strip, lanes] = (knots - high.astype(F32)).astype(BF16)

    def coarse_rest():
        move((4, 1), (3, 2), (2, 3))
        complete(1)

    forward = pipeline if groups else looped
    forward(
        (
            nothing,
            lambda lanes: dot(w_ref[:, at_entry : at_entry + p.pool_wide], pooled_ref[:, lanes]),
            activate(0),
            coarse_rest,
        ),
        hidden("coarse_middle", 1, lambda: move((4, 2), (2, 4))),
        hidden("coarse_upper", 2, lambda: move((3, 3))),
        (
            lambda: turn_weight(at_head, p.theta_wide),
            lambda lanes: dot(turned_ref[: p.theta_wide, :], h_refs[2][H, lanes]),
            keep_theta,
            nothing,
        ),
    )
    theta_copy.start()

    def keep(name, wide, sem):
        columns = slice(p.at[name], p.at[name] + wide)
        return load(w_ref.at[:, columns], kept_out.at[:, columns], sem)

    first_pair = p.start("fine_entry", section) // p.pair

    def interpolate(base, count, k, rest, later, lanes):
        own = theta_ref[pl.ds(base + jnp.minimum(k, count - 1), 1), lanes]
        after = theta_ref[pl.ds(base + jnp.minimum(k + 1, count - 1), 1), lanes]
        return own * rest + after * later

    everything = slice(0, windows)
    rest, later = fractions(windows)

    @pl.loop(0, p.r1_pairs)
    def _(i):
        pair = first_pair + i
        source = aligned(pair * p.pair, p.pair, ONES)
        made = jnp.concatenate(
            [interpolate(0, p.back, 2 * pair + j, rest, later, everything) for j in range(2)], axis=0
        )
        made = made * (pair < p.back // 2).astype(F32)
        r1_ref[aligned(i * p.pair, p.pair, ONES), :] = (big_ref[source, :].astype(F32) - made).astype(BF16)

    move((4, 3), (2, 5), (3, 4))
    complete(2, 3)
    kept = []
    if groups:
        kept.append(keep("fine_entry", p.wide_in, 10))
        kept[0].start()

    total = jnp.zeros((hid, p.theta_wide), F32)
    for first in range(0, p.wide_in, step):
        count = min(step, p.wide_in - first)
        total += dot(w_ref[:, place + first : place + first + count], hat_weights(first, count, p))
    product = (total * (1.0 / KNOT)).astype(BF16)
    pwt_ref[...] = product
    pw_ref[...] = product.T
    move((4, 4), (2, 6), (3, 5))

    def fine_entry(lanes):
        a = dot(w_ref[:, place : place + p.wide_in], big_ref[: p.wide_in, lanes])
        for part in (0, p.theta_wide):
            a -= dot(pwt_ref[...], split_ref[part : part + p.theta_wide, lanes])
        return a

    def entry_made():
        cotangent_in.start()
        target_in.start()
        big_ref[p.fine_out :, :] = jnp.zeros((p.wide_out - p.fine_out, windows), BF16)
        if groups:
            signal(ready.at[0], way.all())
        move((4, 5), (3, 6))
        complete(4)

    rest_c, later_c = fractions(chunk)

    def fore(number):
        low, high = fore_parts[number]

        def before():
            first = head_at + p.low + low
            turned = w_ref[:, first : first + up(high - low + p.skip, LANES)].T
            turned_ref[: high - low, :] = turned[p.skip : p.skip + high - low]

        def finish(source, lanes):
            for k in range(low // KNOT, high // KNOT, 2):
                here = slice(k * KNOT - low, (k + 2) * KNOT - low)
                second = source[here, :] + bias_ref[here, 6 + number : 7 + number]
                first = jnp.concatenate(
                    [interpolate(p.back, p.fore, k + j, rest_c, later_c, lanes) for j in range(2)], axis=0
                )
                counts = (lax.broadcasted_iota(jnp.int32, (2 * KNOT, chunk), 0) + k * KNOT) < horizon_buf[:, lanes]
                there = slice(p.length + k * KNOT, p.length + (k + 2) * KNOT)
                error = first + second - big_ref[there, lanes].astype(F32)
                big_ref[there, lanes] = jnp.where(counts, -error, 0.0).astype(BF16)

        return before, lambda lanes: dot(turned_ref[: high - low, :], h_refs[5][H, lanes]), finish, nothing

    looped((nothing, fine_entry, activate(3), entry_made))
    forward(hidden("fine_middle", 4, lambda: move((4, 6))), hidden("fine_upper", 5))
    h3_copy.start()
    cotangent_in.wait()
    target_in.wait()

    def gradient_slice(name, left, right_ref, first, step=LANES, sign=1.0):
        left_ref = left if name.endswith("entry") else h_refs[left]

        def part(b):
            value = sign * dot_rows(left_ref[...], right_ref[aligned(first + b * step, step, ONES), :])
            w_ref[:, aligned(place + p.slice_at[name] + b * step, step, LANES)] = value[:hid].astype(BF16)
            if name in p.bias_at:
                for c in range(step // LANES):
                    row = p.bias_at[name] + b * (step // LANES) + c
                    head_bias_ref[pl.ds(row, 1), :] = value[hid : hid + 1, c * LANES : (c + 1) * LANES]

        count = p.rows(name) // step
        if count > 1:
            pl.loop(0, count)(part)
        else:
            part(0)

    def square_slice(name, index):
        gradient_slice(name, index - 1, g_refs[index], p.start(name, section))

    def back(index, product, after=nothing):
        def finish(source, lanes):
            for r in range(0, hid, strip):
                rows = slice(r, r + strip)
                g_refs[index][rows, lanes] = (source[rows, :] * g_refs[index][rows, lanes].astype(F32)).astype(BF16)

        return nothing, product, finish, after

    def times(name, index):
        at = p.at[name]
        return lambda lanes: dot(w_ref[:, at : at + hid], g_refs[index][:, lanes])

    if groups:
        cuts = (0, p.slice_at["head_fore"], p.slice_at["fine_entry"])
        cuts += (p.slice_at["coarse_head"], p.slice_at["coarse_middle"], p.slice_columns)
        width = lambda k: cuts[k + 1] - cuts[k]

        def arrivals(row, k):
            rows = slice(row * per, (row + 1) * per) if isinstance(row, int) else aligned(row * per, per, per)
            if k == 0:
                return split_ref.at[rows, : width(0)]
            first = head_at + cuts[k] - cuts[1]
            return w_ref.at[rows, first : first + width(k)]

        def departures(j, k):
            if k == 0:
                return gknot_ref.at[j * per : (j + 1) * per, : width(0)]
            first = (k * groups + j) * per
            return big_ref.at[first : first + per, : width(k)]

        reduce = Reduce(
            p,
            way,
            per,
            cuts,
            lambda owner, k: w_ref.at[aligned(owner * per, per, per), place + cuts[k] : place + cuts[k + 1]],
            arrivals,
            lambda j, k: arrivals(groups + j, k),
            departures,
            stage_ref,
            slices_out,
            reduce_send,
            reduce_recv,
            keep_sems,
        )
        reduce_bias = ReduceBias(way, head_bias_ref, bias_in, bias_far, bias_out, bias_send, bias_recv)
        kept[0].wait()
        gather.sent(2)
        gather.sent(3)

    gradient_slice("head_back", 5, big_ref, p.start("head_back", section), 2 * LANES, -1.0)
    if groups:
        pl.semaphore_wait(ready.at[0], len(way.all()))
        reduce.first(0)
    complete(5, 6)
    looped(fore(0), fore(1))
    if groups:
        kept.append(keep("fine_head", p.wide_out, 11))
        kept[1].start()
        reduce.second(0)

    adjoint(p.low, p.wide_out - p.low, True)
    looped(back(5, lambda lanes: -dot(w_ref[:, head_at : head_at + p.wide_out], big_ref[:, lanes])))
    if groups:
        kept[1].wait()
        for k in (0, 1, 4, 5, 6):
            gather.sent(k)
        signal(ready.at[1], way.all())
    looped(back(4, times("fine_upper", 5)))
    gradient_slice("head_fore", 5, big_ref, p.start("head_fore", section) + p.low, LANES, -1.0)
    square_slice("fine_upper", 5)
    square_slice("fine_middle", 4)
    if groups:
        pl.semaphore_wait(ready.at[1], len(way.all()))
        reduce.first(1)
    looped(back(3, times("fine_middle", 4)))
    gfine_copy.start()
    gradient_slice("fine_entry", g_refs[3], r1_ref, p.start("fine_entry", section) - first_pair * p.pair, 2 * LANES)
    if groups:
        reduce.first(2)
        reduce.second(1)
        reduce.third(0)
        reduce.sent_far(0)
    gknot_ref[p.knot_rows :, :] = jnp.zeros((p.theta_wide - p.knot_rows, windows), BF16)

    def knots_done(source, lanes):
        for r in range(0, p.knot_rows, strip):
            rows = slice(r, r + strip)
            gknot_ref[rows, lanes] = (gtheta_ref[rows, lanes] - source[rows, :]).astype(BF16)

    looped(
        (nothing, lambda lanes: dot(pw_ref[: p.knot_rows, :], g_refs[3][:, lanes]), knots_done, nothing),
        back(2, lambda lanes: dot(w_ref[:, at_head : at_head + p.theta_wide], gknot_ref[:, lanes])),
    )
    gradient_slice("coarse_head", 2, gknot_ref, p.start("coarse_head", section))
    square_slice("coarse_upper", 2)
    if groups:
        reduce.first(3)
        reduce.second(2)
    looped(back(1, times("coarse_upper", 2)))
    if groups:
        reduce.third(1)
        reduce.second(3)
    square_slice("coarse_middle", 1)
    looped(back(0, times("coarse_middle", 1)))
    gradient_slice("coarse_entry", g_refs[0], pooled_ref, p.start("coarse_entry", section))
    if groups:
        reduce.first(4)
        reduce_bias.to_partner().start()
        reduce.second(4)
        reduce_bias.second()

    def pool_gradient(source, lanes):
        for r in range(0, p.pool_wide, strip):
            pooled_ref[r : r + strip, lanes] = (source[r : r + strip, :] * (1.0 / POOL)).astype(BF16)

    looped(
        (
            lambda: turn_weight(at_entry, p.pool_wide),
            lambda lanes: dot(turned_ref[: p.pool_wide, :], g_refs[0][:, lanes]),
            pool_gradient,
            nothing,
        )
    )
    pool_copy.start()
    if groups:
        reduce.third(2)
        reduce_bias.third()
        reduce.third(3)
        reduce.third(4)
        for k in range(reduce.chunks):
            reduce.complete(k)
            reduce.sent(k)
            if k > 0:
                reduce.sent_far(k)
        reduce_bias.complete()
    else:
        out = load(w_ref.at[:, place : place + p.slice_columns], slice_out, 10)
        out.start()
        out.wait()
    theta_copy.wait()
    h3_copy.wait()
    gfine_copy.wait()
    pool_copy.wait()


ANY = pl.BlockSpec(memory_space=pl.ANY)
VMEM = pl.BlockSpec(memory_space=pltpu.VMEM)


def core(plan, per, groups, history, cotangent, targets, horizon, coarse_bias, fine_bias, weights):
    p = plan
    hid, windows = p.hidden, p.windows
    flops = 2 * windows * hid * (2 * p.length + 2 * p.wide_out // 3 + 12 * hid + p.slice_columns)
    out_shape = [
        jax.ShapeDtypeStruct((p.knot_rows, windows), F32),
        jax.ShapeDtypeStruct((hid, windows), BF16),
        jax.ShapeDtypeStruct((hid, windows), BF16),
        jax.ShapeDtypeStruct((p.pool_wide, windows), BF16),
        jax.ShapeDtypeStruct((1, p.fine_out), F32),
    ]
    out_specs = [ANY] * 4 + [VMEM]
    scratch = [
        pltpu.VMEM((hid, p.columns), BF16),
        pltpu.VMEM((p.wide_out, windows), BF16),
        *[pltpu.VMEM((hid + ONES, windows), BF16)] * 6,
        *[pltpu.VMEM((hid, windows), BF16)] * 6,
        pltpu.VMEM((p.r1_pairs * p.pair, windows), BF16),
        pltpu.VMEM((p.pool_wide, windows), BF16),
        pltpu.VMEM((2 * p.theta_wide, windows), BF16),
        pltpu.VMEM((p.knot_rows, windows), F32),
        pltpu.VMEM((p.knot_rows, windows), F32),
        pltpu.VMEM((p.theta_wide, windows), BF16),
        pltpu.VMEM((p.theta_wide, hid), BF16),
        pltpu.VMEM((hid, p.theta_wide), BF16),
        pltpu.VMEM((hid, hid), BF16),
        pltpu.VMEM((hid, min(512, windows // 2)), F32),
        pltpu.VMEM((hid, min(512, windows // 2)), F32),
        pltpu.VMEM((hid, LANES), F32),
        pltpu.VMEM(horizon.shape, jnp.int32),
        pltpu.VMEM((1, windows), jnp.int32),
        pltpu.VMEM(coarse_bias.shape, F32),
        pltpu.VMEM(fine_bias.shape, F32),
        pltpu.SemaphoreType.DMA((13,)),
    ]
    params = {}
    if groups:
        bias = (p.bias_rows, LANES)
        out_shape += [
            jax.ShapeDtypeStruct((hid, p.columns), BF16),
            jax.ShapeDtypeStruct((4, per, p.slice_columns), BF16),
            jax.ShapeDtypeStruct((4,) + bias, F32),
        ]
        out_specs += [ANY, ANY, VMEM]
        chunks, reduce_chunks = 7, 5
        scratch += [pltpu.VMEM(piece.shape, F32) for piece in weights]
        scratch += [
            pltpu.SemaphoreType.DMA((len(weights),)),
            pltpu.SemaphoreType.DMA((chunks, groups - 1, 6)),
            pltpu.SemaphoreType.DMA((chunks, groups - 1, 4)),
            pltpu.SemaphoreType.DMA((chunks, groups)),
            pltpu.VMEM(bias, F32),
            pltpu.VMEM(bias, F32),
            pltpu.VMEM((groups,) + bias, F32),
            pltpu.VMEM((per, p.slice_columns), BF16),
            pltpu.SemaphoreType.REGULAR((2,)),
            pltpu.SemaphoreType.DMA((reduce_chunks, max(groups, 3), 3)),
            pltpu.SemaphoreType.DMA((reduce_chunks, max(groups, 3), 3)),
            pltpu.SemaphoreType.DMA((groups + 3,)),
            pltpu.SemaphoreType.DMA((groups + 3,)),
            pltpu.SemaphoreType.DMA((reduce_chunks,)),
        ]
        params = {"collective_id": 0, "has_side_effects": True}
    else:
        out_shape += [jax.ShapeDtypeStruct((hid, p.slice_columns), BF16), jax.ShapeDtypeStruct((p.bias_rows, LANES), F32)]
        out_specs += [ANY, VMEM]
    return pl.pallas_call(
        functools.partial(core_kernel, p, per, groups),
        out_shape=tuple(out_shape),
        in_specs=[ANY] * (6 + len(weights)),
        out_specs=tuple(out_specs),
        scratch_shapes=scratch,
        compiler_params=pltpu.CompilerParams(vmem_limit_bytes=63 * MIB, **params),
        cost_estimate=pl.CostEstimate(flops=flops, bytes_accessed=windows * p.length * 4, transcendentals=0),
    )(history, cotangent, targets, horizon, coarse_bias, fine_bias, *weights)


def outputs_kernel(
    plan,
    block,
    steps,
    packed_ref,
    history_ref,
    cotangent_ref,
    theta_ref,
    h3_ref,
    gfine_ref,
    pool_ref,
    fine_bias_ref,
    slices_ref,
    bias_rows_ref,
    residual_ref,
    history_grad_ref,
    prediction_ref,
    *refs,
):
    grads = refs[:16]
    head_ref, entry_ref, side_ref, pool_grad, fore_ref, *products, turned_head, turned_entry, bias_ref, sems = refs[16:]
    back_refs, fine_refs = products[:2], products[2:]
    p = plan
    step = pl.program_id(0)
    windows = p.windows
    chunk = min(512, windows)
    chunks = windows // chunk
    lanes_of = lambda n: slice(n * chunk, (n + 1) * chunk) if isinstance(n, int) else aligned(n * chunk, chunk, chunk)
    knots = block // KNOT
    pooled = block // POOL
    rest, later = fractions(chunk)

    def fetch(name, out, at, slot, sem):
        first = aligned(p.at[name] + at * block, block, LANES)
        return pltpu.make_async_copy(packed_ref.at[:, first], out.at[slot], sems.at[sem, slot])

    def interpolate(k, count, base, lanes):
        low = jnp.minimum if not isinstance(k, int) else min
        own = theta_ref[pl.ds(base + low(k, count - 1), 1), lanes]
        after = theta_ref[pl.ds(base + low(k + 1, count - 1), 1), lanes]
        return own * rest + after * later

    fore_out = pltpu.make_async_copy(fore_ref, prediction_ref, sems.at[3, 0])
    wide = p.wide_out - p.low
    first_fore = p.at["fine_head"] + p.low
    side = pltpu.make_async_copy(packed_ref.at[:, first_fore : first_fore + wide], side_ref, sems.at[2, 0])

    @pl.when(step == 0)
    def _():
        fetch("fine_head", head_ref, 0, 0, 0).start()
        fetch("fine_entry", entry_ref, 0, 0, 1).start()
        side.start()
        pool_grad[...] = pool_ref[...].astype(F32)

    @pl.when(step == 2)
    def _():
        side.wait()
        turned_fore = side_ref[...].T
        fore_bias = column_of(fine_bias_ref, p.low, wide)

        @pl.loop(0, chunks)
        def _(n):
            lanes = lanes_of(n)
            for part in range(0, p.horizon, block):
                size = min(block, p.horizon - part)
                back_refs[part // block][:size, :] = dot(turned_fore[p.skip + part : p.skip + part + size], h3_ref[:, lanes])
            for k in range(0, p.fore, 2):
                rows = slice(k * KNOT, (k + 2) * KNOT)
                here = slice(k * KNOT % block, k * KNOT % block + 2 * KNOT)
                second = back_refs[k * KNOT // block][here, :] + fore_bias[p.skip + k * KNOT : p.skip + (k + 2) * KNOT]
                first = jnp.concatenate([interpolate(k + j, p.fore, p.back, lanes) for j in range(2)], axis=0)
                fore_ref[rows, lanes] = first.astype(BF16).astype(F32) + second.astype(BF16).astype(F32)

        fore_out.start()

    @pl.when(step == 1)
    def _():
        unpack(p, slices_ref, bias_rows_ref, grads)

    slot = step % 2

    @pl.when(step + 1 < steps)
    def _():
        fetch("fine_head", head_ref, step + 1, 1 - slot, 0).start()
        fetch("fine_entry", entry_ref, step + 1, 1 - slot, 1).start()

    fetch("fine_head", head_ref, step, slot, 0).wait()
    fetch("fine_entry", entry_ref, step, slot, 1).wait()
    turned_head[...] = head_ref[slot].T
    turned_entry[...] = entry_ref[slot].T
    row = jnp.broadcast_to(fine_bias_ref[:, aligned(step * block, block, LANES)], (8, block))
    bias_ref[...] = row.T[:, :1]
    pair = 2 * KNOT

    def make(n, place):
        lanes = lanes_of(n)
        back_refs[place][...] = dot(turned_head[...], h3_ref[:, lanes])
        fine_refs[place][...] = dot(turned_entry[...], gfine_ref[:, lanes])

    def finish(n, place):
        lanes = lanes_of(n)
        for at in range(0, block, pair):
            rows = slice(at, at + pair)
            k = step * knots + at // KNOT
            made = jnp.concatenate([interpolate(k + j, p.back, 0, lanes) for j in range(2)], axis=0)
            back = back_refs[place][rows, :] + bias_ref[rows, :]
            residual_ref[rows, lanes] = (history_ref[rows, lanes].astype(F32) - made - back).astype(BF16)
            first = step * pooled + at // POOL
            spread = jnp.concatenate(
                [jnp.broadcast_to(pool_grad[pl.ds(first + j, 1), lanes], (POOL, chunk)) for j in range(pair // POOL)],
                axis=0,
            )
            fine = fine_refs[place][rows, :] + spread
            history_grad_ref[rows, lanes] = (cotangent_ref[rows, lanes].astype(F32) + fine).astype(BF16)

    for n in range(chunks + 1):
        if n < chunks:
            make(n, n % 2)
        if n > 0:
            finish(n - 1, (n - 1) % 2)

    @pl.when(step == steps - 1)
    def _():
        fore_out.wait()


def outputs(plan, packed, history, cotangent, theta, h3, gfine, pool, fine_bias, slices, bias_rows):
    p = plan
    hid, windows = p.hidden, p.windows
    block = 3 * LANES
    steps = -(-p.length // block)
    rows = pl.BlockSpec((block, windows), lambda i: (i, 0))
    wide = p.wide_out - p.low
    per = slices.shape[1]
    square, vector = (per, hid), (1, per)
    grads = []
    for entry, out in ((p.pooled, p.coarse_out), (p.length, p.fine_out)):
        grads += [(per, entry), vector, square, vector, square, vector, (per, out), (1, out)]
    grads[-1] = (p.fine_out,)
    return pl.pallas_call(
        functools.partial(outputs_kernel, p, block, steps),
        grid=(steps,),
        out_shape=(
            jax.ShapeDtypeStruct((p.length, windows), BF16),
            jax.ShapeDtypeStruct((p.length, windows), BF16),
            jax.ShapeDtypeStruct((p.horizon, windows), F32),
        )
        + tuple(jax.ShapeDtypeStruct(shape, F32) for shape in grads),
        in_specs=[ANY, rows, rows, VMEM, VMEM, VMEM, VMEM, VMEM, VMEM, VMEM],
        out_specs=(rows, rows, ANY) + (VMEM,) * len(grads),
        scratch_shapes=[
            pltpu.VMEM((2, hid, block), BF16),
            pltpu.VMEM((2, hid, block), BF16),
            pltpu.VMEM((hid, wide), BF16),
            pltpu.VMEM((p.pool_wide, windows), F32),
            pltpu.VMEM((p.horizon, windows), F32),
            *[pltpu.VMEM((block, min(512, windows)), F32)] * 4,
            pltpu.VMEM((block, hid), BF16),
            pltpu.VMEM((block, hid), BF16),
            pltpu.VMEM((block, 1), F32),
            pltpu.SemaphoreType.DMA((4, 2)),
        ],
        compiler_params=pltpu.CompilerParams(vmem_limit_bytes=56 * MIB),
        cost_estimate=pl.CostEstimate(
            flops=2 * windows * hid * (2 * p.length + p.horizon), bytes_accessed=windows * p.length * 8, transcendentals=0
        ),
    )(packed, history, cotangent, theta, h3, gfine, pool, fine_bias, slices, bias_rows)


def pack(plan, arrays, biases):
    p = plan
    names = sorted(p.at, key=p.at.get)
    ends = [p.at[name] for name in names[1:]] + [p.columns]
    columns = []
    for name, end in zip(names, ends):
        piece = arrays[name] if name != "bias" else biases
        columns.append(jnp.pad(piece.astype(BF16), ((0, 0), (0, end - p.at[name] - piece.shape[1]))))
    return jnp.concatenate(columns, axis=1)


def unpack(plan, slices_ref, bias_rows_ref, grads):
    p = plan
    hid = p.hidden

    def joined(name, out, source, row=None, base=0, low=0, high=None):
        high, done = out.shape[-1] if high is None else high, low
        for section in range(p.sections):
            first = base + p.start(name, section)
            last = min(first + p.rows(name), high)
            if row is not None:
                for at in range(max(done // LANES * LANES, first), last, LANES):
                    begin, end = max(at, done), min(at + LANES, last)
                    if begin < end:
                        here = source[section, pl.ds(row + (at - first) // LANES, 1), :]
                        here = here[:, begin - at : end - at]
                        if len(out.shape) == 1:
                            out[begin:end] = here.reshape(end - begin)
                        else:
                            out[:, begin:end] = here
            elif done < last:
                at = p.slice_at[name] + done - first
                out[:, done:last] = source[section, :, at : at + last - done].astype(F32)
            done = max(done, last)

    def ones_column(name, row):
        section = p.sections - 1
        at = p.slice_at[name] + row - p.start(name, section)
        block = slices_ref[section, :, at // LANES * LANES : at // LANES * LANES + LANES].astype(F32)
        return block.T[at % LANES : at % LANES + 1]

    def own_part(name, out):
        per = out.shape[1]
        width = min(per, LANES)
        share = p.part[name][0]
        for at in range(0, per, width):
            first = lax.axis_index("dp") * per + at
            block = first // LANES
            row = bias_rows_ref[block // share, pl.ds(p.bias_at[name] + block % share, 1), :]
            wide = jnp.broadcast_to(row, (8, LANES))
            out[:, at : at + width] = pltpu.roll(wide, (LANES - first % LANES) % LANES, 1)[:1, :width]

    for base, block in ((0, "coarse_"), (8, "fine_")):
        entry, head = block + "entry", block + "head"
        joined(entry, grads[base], slices_ref)
        grads[base + 1][...] = ones_column(entry, grads[base].shape[1])
        for i, name in enumerate((block + "middle", block + "upper")):
            joined(name, grads[base + 2 + 2 * i], slices_ref)
            own_part(name, grads[base + 3 + 2 * i])
        for number, source in ((6, slices_ref), (7, bias_rows_ref)):
            row = lambda name: p.bias_at[name] if number == 7 else None
            if base == 0:
                joined(head, grads[number], source, row(head))
            else:
                joined("head_back", grads[8 + number], source, row("head_back"), 0, 0, p.length)
                joined("head_fore", grads[8 + number], source, row("head_fore"), p.low, p.length, p.fine_out)


def body(mesh_shape, history, targets, horizon, cotangent, *params):
    (c_entry, c_entry_b, c_middle, c_middle_b, c_upper, c_upper_b, c_head, c_head_b) = params[:8]
    (f_entry, f_entry_b, f_middle, f_middle_b, f_upper, f_upper_b, f_head, f_head_b) = params[8:]
    sections = mesh_shape["section"]
    length, hidden = f_entry.shape[0], c_middle.shape[1]
    p = Plan(
        length, f_head.shape[1] - length, hidden, c_entry.shape[0], c_head.shape[1], sections, history.shape[0]
    )
    pieces = (c_entry.T, c_middle, c_upper, c_head, f_entry.T, f_middle, f_upper, f_head)
    bias_pieces = (c_entry_b, c_middle_b, c_upper_b, f_entry_b, f_middle_b, f_upper_b)
    dp_count, per = mesh_shape["dp"], c_middle.shape[0]
    rows = (history.T, cotangent.T)
    rest = (targets.T, horizon.reshape(-1, LANES), c_head_b[None, :], f_head_b)
    groups = dp_count // 2
    if sections == 4 and dp_count % 2 == 0 and per % 64 == 0 and groups > 1:
        theta, h3, gfine, pool, fine_bias, packed, slices, bias_rows = core(
            p, per, groups, *rows, *rest, pieces + tuple(b[None, :] for b in bias_pieces)
        )
    else:
        packed = pack(p, dict(zip(NAMES, pieces)), jnp.stack(bias_pieces, axis=1))
        packed = lax.all_gather(packed, "dp", axis=0, tiled=True)
        theta, h3, gfine, pool, fine_bias, part, head_bias = core(p, per, 0, *rows, *rest, (packed,))
        own = lax.psum_scatter(part.astype(F32), "dp", scatter_dimension=0, tiled=True)
        slices = lax.all_gather(own, "section", axis=0)
        bias_rows = lax.all_gather(lax.psum(head_bias, "dp"), "section", axis=0)
    residual, history_grad, prediction, *grads = outputs(
        p, packed, *rows, theta, h3, gfine, pool, fine_bias, slices, bias_rows
    )
    grads = [g.T if i in (0, 8) else g[0] if g.shape[0] == 1 else g for i, g in enumerate(grads)]
    return (prediction.T, residual.T, history_grad.T) + tuple(grads)


def solution(mesh):
    by_row, by_column, by_entry, copied = P("dp", None), P(None, "dp"), P("dp"), P()
    block = (by_column, by_entry, by_row, by_entry, by_row, by_entry, by_row, copied)
    in_specs = (by_row, by_row, by_entry, by_row) + block + block
    out_specs = (by_row, by_row, by_row) + block + block
    return jax.shard_map(
        functools.partial(body, dict(mesh.shape)), mesh=mesh, in_specs=in_specs, out_specs=out_specs, check_vma=False
    )
```

```python
import functools

import jax
import jax.numpy as jnp
from jax import lax
from jax.experimental import pallas as pl
from jax.experimental.pallas import tpu as pltpu
from jax.sharding import PartitionSpec as P

POOL = 8
KNOT = 24
LANES = 128
ONES = 16
GELU_A = 0.7978845608028654
GELU_B = GELU_A * 0.044715
F32 = jnp.float32
BF16 = jnp.bfloat16
MIB = 1 << 20


def up(size, unit):
    return -(-size // unit) * unit


class Plan:
    def __init__(self, length, horizon, hidden, pooled, coarse_out, sections, windows):
        self.length, self.horizon, self.hidden = length, horizon, hidden
        self.pooled, self.coarse_out = pooled, coarse_out
        self.fine_out = length + horizon
        self.sections, self.windows = sections, windows
        self.back, self.fore = length // KNOT, horizon // KNOT
        self.wide_in, self.wide_out = up(length + 1, LANES), up(self.fine_out + 1, LANES)
        self.pool_wide, self.theta_wide = up(pooled + 1, LANES), up(coarse_out + 1, LANES)
        widths = [
            ("coarse_entry", self.pool_wide),
            ("bias", LANES),
            ("coarse_middle", hidden),
            ("coarse_upper", hidden),
            ("coarse_head", self.theta_wide),
            ("fine_entry", self.wide_in),
            ("fine_middle", hidden),
            ("fine_upper", hidden),
            ("fine_head", self.wide_out),
        ]
        self.at, place = {}, 0
        for name, width in widths:
            self.at[name] = place
            place += width
        self.columns = place
        self.low = length // LANES * LANES
        self.skip = length - self.low
        self.square = hidden // sections
        self.slice_at, self.part, place = {}, {}, 0
        for name, width in (
            ("head_back", self.wide_in),
            ("head_fore", self.wide_out - self.low),
            ("fine_upper", hidden),
            ("fine_middle", hidden),
            ("fine_entry", self.wide_in),
            ("coarse_head", self.theta_wide),
            ("coarse_upper", hidden),
            ("coarse_middle", hidden),
            ("coarse_entry", self.pool_wide),
        ):
            self.slice_at[name] = place
            total = width // LANES
            share = -(-total // sections)
            self.part[name] = share, total
            place += share * LANES
        self.slice_columns = place
        self.bias_at, place = {}, 0
        for name in ("head_back", "head_fore", "coarse_head", "coarse_middle", "coarse_upper", "fine_middle", "fine_upper"):
            self.bias_at[name] = place
            place += self.part[name][0]
        self.bias_rows = up(place, 8)
        self.knot_rows = up(coarse_out, ONES)
        self.pair = 2 * KNOT
        self.r1_pairs = -(-(self.rows("fine_entry") + self.pair - ONES) // self.pair)

    def rows(self, name):
        return self.part[name][0] * LANES

    def start(self, name, section):
        low = min if isinstance(section, int) else jnp.minimum
        share, total = self.part[name]
        return low(section * share, total - share) * LANES


def gelu_both(a):
    square = a * a
    v = 0.5 + 0.5 * jnp.tanh(a * (GELU_A + GELU_B * square))
    h = a * v
    return h, v + h * (1.0 - v) * (2.0 * GELU_A + (6.0 * GELU_B) * square)


def dot(a, b):
    return jnp.dot(a, b, preferred_element_type=F32)


def dot_rows(a, b):
    return lax.dot_general(a, b, (((1,), (1,)), ((), ())), preferred_element_type=F32)


def aligned(start, size, unit):
    return pl.ds(pl.multiple_of(start, unit), size)


def column_of(row_ref, first, count):
    size = row_ref.shape[1]
    columns = []
    for at in range(first, first + count, LANES):
        width = max(0, min(LANES, size - at))
        row = jnp.zeros((1, LANES), F32) if width == 0 else row_ref[:, at : at + width]
        if 0 < width < LANES:
            row = jnp.concatenate([row, jnp.zeros((1, LANES - width), F32)], axis=1)
        columns.append(jnp.broadcast_to(row, (LANES, LANES)).T[:, :1])
    return jnp.concatenate(columns, axis=0)


def hat_weights(first, count, plan, turned=False, fore=False):
    p = plan
    shape = (p.knot_rows, count) if turned else (count, p.theta_wide)
    row = lax.broadcasted_iota(jnp.int32, shape, 1 if turned else 0) + first
    knot = lax.broadcasted_iota(jnp.int32, shape, 0 if turned else 1)
    away = row - KNOT * knot
    weight = jnp.maximum(KNOT - jnp.abs(away), 0)
    last = (knot == p.back - 1) | (knot == p.back + p.fore - 1)
    weight = jnp.where(last & (away > 0) & (away < KNOT), KNOT, weight)
    own = (knot >= p.back) & (row >= p.length) if fore else (knot < p.back) & (row < p.length)
    inside = own & (row < p.fine_out) & (knot < p.back + p.fore)
    return jnp.where(inside, weight, 0).astype(F32).astype(BF16)


def fractions(width):
    later = lax.broadcasted_iota(jnp.int32, (KNOT, width), 0).astype(F32) * (1.0 / KNOT)
    return 1.0 - later, later


NAMES = (
    "coarse_entry",
    "coarse_middle",
    "coarse_upper",
    "coarse_head",
    "fine_entry",
    "fine_middle",
    "fine_upper",
    "fine_head",
)
KEPT = ("fine_entry", "fine_head")


def remote(source, target, send_sem, recv_sem, place):
    return pltpu.make_async_remote_copy(
        src_ref=source,
        dst_ref=target,
        send_sem=send_sem,
        recv_sem=recv_sem,
        device_id=place,
        device_id_type=pl.DeviceIdType.MESH,
    )


def signal(semaphore, places):
    for place in places:
        pl.semaphore_signal(semaphore, inc=1, device_id=place, device_id_type=pl.DeviceIdType.MESH)


class Ways:
    def __init__(self, groups):
        self.section, self.dp = lax.axis_index("section"), lax.axis_index("dp")
        self.group, self.core = self.dp // 2, self.dp % 2
        self.groups = groups
        self.partner = (self.section, self.group * 2 + 1 - self.core)
        s = self.section
        self.side = [s + 1 - 2 * (s % 2), (s + 2) % 4]
        self.sides = [(t, self.dp) for t in self.side]
        self.across = 3 - s
        self.corner = (self.across, self.dp)

    def far(self, j):
        group = (self.group + j) % self.groups
        return group, (self.section, group * 2 + self.core)

    def from_far(self, j):
        return (self.group + self.groups - j) % self.groups

    def all(self):
        return [self.partner, self.corner] + self.sides + [self.far(j)[1] for j in range(1, self.groups)]


class Gather:
    def __init__(self, plan, way, per, cuts, w_ref, shards, biases, send, recv, partner_recv):
        self.p, self.way, self.per, self.cuts, self.w_ref = plan, way, per, cuts, w_ref
        self.shards, self.biases = shards, biases
        self.send, self.recv, self.partner_recv = send, recv, partner_recv
        self.near = range(1, way.groups)
        self.chunks, self.ahead = len(cuts) - 1, 3

    def at(self, k, owner, s=None):
        quarter = self.per // 4
        rows = aligned(owner * self.per, self.per, self.per)
        if s is not None:
            rows = aligned(owner * self.per + s * quarter, quarter, quarter)
        return self.w_ref.at[rows, self.cuts[k] : self.cuts[k + 1]]

    def source(self, j):
        return self.way.from_far(j) * 2 + self.way.core

    def copy(self, here, k, j, kind, place):
        return remote(here, here, self.send.at[k, j - 1, kind], self.recv.at[k, j - 1, kind], place)

    def to_far(self, k, j):
        return self.copy(self.at(k, self.way.dp, self.way.section), k, j, 0, self.way.far(j)[1])

    def to_side(self, k, j, i):
        return self.copy(self.at(k, self.source(j), self.way.section), k, j, 1 + i, self.way.sides[i])

    def to_across(self, k, j):
        if k == 0:
            return self.copy(self.at(k, self.source(j), self.way.section), k, j, 3, self.way.corner)
        i = (k + j) % 2
        return self.copy(self.at(k, self.source(j), self.way.side[i]), k, j, 3, self.way.sides[1 - i])

    def to_partner(self, k, j):
        here = self.at(k, self.source(j) if j else self.way.dp)
        return remote(here, here, self.send.at[k, max(j - 1, 0), 4 if j else 5], self.partner_recv.at[k, j], self.way.partner)

    def arrived(self, k, j, kind):
        s = [self.way.section, self.way.side[0], self.way.side[1], self.way.across][kind]
        self.copy(self.at(k, self.source(j), s), k, j, kind, self.way.partner).wait_recv()

    def cast(self, k):
        p, own = self.p, aligned(self.way.dp * self.per, self.per, self.per)
        low, high = self.cuts[k], self.cuts[k + 1]
        for ref, name in zip(self.shards, NAMES):
            at, size = p.at[name], ref.shape[1]
            wide = up(size + 1, LANES) if name.endswith(("entry", "head")) else size
            first, last = max(at, low), min(at + wide, high)
            full = min(last, at + size // LANES * LANES)
            if first < full:
                self.w_ref[own, first:full] = ref[:, first - at : full - at].astype(BF16)
            if first < last and last > full:
                rest = ref[:, full - at : size].astype(BF16)
                pad = jnp.zeros((self.per, last - at - size), BF16)
                self.w_ref[own, full:last] = jnp.concatenate([rest, pad], axis=1)
        at = p.at["bias"]
        if low <= at < high:
            count = len(self.biases)
            rows = jnp.concatenate([ref[...] for ref in self.biases] + [jnp.zeros((8 - count, self.per), F32)], axis=0)
            wide = jnp.concatenate([rows, jnp.zeros((8, LANES - self.per), F32)], axis=1)
            wide = jnp.concatenate([wide, jnp.zeros((LANES - 8, LANES), F32)], axis=0)
            self.w_ref[own, at : at + LANES] = wide.T[: self.per].astype(BF16)

    def first(self, k):
        self.cast(k)
        for j in self.near:
            self.to_far(k, j).start()
        self.to_partner(k, 0).start()

    def second(self, k):
        for j in self.near:
            self.arrived(k, j, 0)
            for i in range(2):
                self.to_side(k, j, i).start()
            if k == 0:
                self.to_across(k, j).start()

    def third(self, k):
        for j in self.near:
            self.arrived(k, j, 1)
            self.arrived(k, j, 2)
            if k > 0:
                self.to_across(k, j).start()

    def fourth(self, k):
        for j in self.near:
            self.arrived(k, j, 3)
            self.to_partner(k, j).start()

    def complete(self, k):
        for j in range(self.way.groups):
            there = (self.way.from_far(j) * 2 + 1 - self.way.core) if j else self.way.partner[1]
            here = self.at(k, there)
            remote(here, here, self.send.at[k, 0, 5], self.partner_recv.at[k, j], self.way.partner).wait_recv()

    def sent(self, k):
        for j in self.near:
            for copy in (self.to_far(k, j), self.to_side(k, j, 0), self.to_side(k, j, 1), self.to_across(k, j)):
                copy.wait_send()
            self.to_partner(k, j).wait_send()
        self.to_partner(k, 0).wait_send()


class Reduce:
    def __init__(self, plan, way, per, cuts, part_ref, core_in, far_in, far_out, stage_ref, out_ref, send, recv, local):
        self.p, self.way, self.per, self.cuts = plan, way, per, cuts
        self.part_ref, self.core_in, self.far_in, self.far_out = part_ref, core_in, far_in, far_out
        self.stage_ref, self.out_ref, self.send, self.recv, self.local = stage_ref, out_ref, send, recv, local
        self.near = range(1, way.groups)
        self.chunks = len(cuts) - 1

    def columns(self, k):
        return slice(self.cuts[k], self.cuts[k + 1])

    def to_partner(self, k, g):
        return remote(
            self.part_ref(g * 2 + 1 - self.way.core, k),
            self.core_in(g, k),
            self.send.at[k, g, 0],
            self.recv.at[k, g, 0],
            self.way.partner,
        )

    def to_far(self, k, j):
        here, there = self.far_out(j - 1, k), self.far_in(j - 1, k)
        return remote(here, there, self.send.at[k, j - 1, 1], self.recv.at[k, j - 1, 1], self.way.far(j)[1])

    def side(self, k, source, i, to):
        here = self.out_ref.at[source, :, self.columns(k)]
        return remote(here, here, self.send.at[k, i, 2], self.recv.at[k, i, 2], to)

    def to_side(self, k, i):
        here = self.stage_ref.at[:, self.columns(k)]
        there = self.out_ref.at[self.way.section, :, self.columns(k)]
        place = (self.way.sides + [self.way.corner])[i]
        return remote(here, there, self.send.at[k, i, 2], self.recv.at[k, i, 2], place)

    def keep(self, k):
        there = self.out_ref.at[self.way.section, :, self.columns(k)]
        return pltpu.make_async_copy(self.stage_ref.at[:, self.columns(k)], there, self.local.at[k])

    def summed(self, k, group):
        own = self.part_ref(group * 2 + self.way.core, k)[...].astype(F32)
        return own + self.core_in(group, k)[...].astype(F32)

    def first(self, k):
        for g in range(self.way.groups):
            self.to_partner(k, g).start()

    def second(self, k):
        for g in range(self.way.groups):
            self.to_partner(k, g).wait_recv()
        for j in self.near:
            self.far_out(j - 1, k)[...] = self.summed(k, self.way.far(j)[0]).astype(BF16)
            self.to_far(k, j).start()

    def third(self, k):
        total = self.summed(k, self.way.group)
        for j in self.near:
            self.to_far(k, j).wait_recv()
            total += self.far_in(j - 1, k)[...].astype(F32)
        self.stage_ref[:, self.columns(k)] = total.astype(BF16)
        for i in range(3):
            self.to_side(k, i).start()
        self.keep(k).start()

    def complete(self, k):
        for i, source in enumerate(self.way.side + [self.way.across]):
            self.side(k, source, i, self.way.partner).wait_recv()

    def sent_far(self, k):
        for j in self.near:
            self.to_far(k, j).wait_send()

    def sent(self, k):
        for g in range(self.way.groups):
            self.to_partner(k, g).wait_send()
        for i in range(3):
            self.to_side(k, i).wait_send()
        self.keep(k).wait()


class ReduceBias:
    def __init__(self, way, own_ref, core_in, far_ref, out_ref, send, recv):
        self.way, self.own_ref, self.core_in, self.far_ref, self.out_ref = way, own_ref, core_in, far_ref, out_ref
        self.send, self.recv = send, recv
        self.near = range(1, way.groups)

    def copy(self, here, there, n, place):
        return remote(here, there, self.send.at[n], self.recv.at[n], place)

    def to_partner(self):
        return self.copy(self.own_ref, self.core_in, 0, self.way.partner)

    def to_far(self, j):
        here = self.far_ref.at[self.way.group]
        return self.copy(here, here, j, self.way.far(j)[1])

    def side(self, source, n, to):
        here = self.out_ref.at[source]
        return self.copy(here, here, self.way.groups + n, to)

    def to_side(self, i):
        return self.side(self.way.section, i, (self.way.sides + [self.way.corner])[i])

    def second(self):
        self.to_partner().wait_recv()
        self.far_ref[self.way.group] = self.own_ref[...] + self.core_in[...]
        for j in self.near:
            self.to_far(j).start()

    def third(self):
        for j in self.near:
            here = self.far_ref.at[self.way.from_far(j)]
            self.copy(here, here, j, self.way.partner).wait_recv()
        total = self.far_ref[0]
        for g in range(1, self.way.groups):
            total += self.far_ref[g]
        self.out_ref[self.way.section] = total
        for i in range(3):
            self.to_side(i).start()

    def complete(self):
        for i, source in enumerate(self.way.side + [self.way.across]):
            self.side(source, i, self.way.partner).wait_recv()
        self.to_partner().wait_send()
        for j in self.near:
            self.to_far(j).wait_send()
        for i in range(3):
            self.to_side(i).wait_send()


def core_kernel(plan, per, groups, *refs):
    p = plan
    refs = list(refs)
    take = lambda count: [refs.pop(0) for _ in range(count)]
    history_ref, cotangent_ref, target_ref, horizon_ref, coarse_bias_ref, fine_bias_ref = take(6)
    if groups:
        shards_in = take(14)
    else:
        (packed_ref,) = take(1)
    theta_out, h3_out, gfine_out, pool_out, row_out = take(5)
    if groups:
        kept_out, slices_out, bias_out = take(3)
    else:
        slice_out, bias_out = take(2)
    w_ref, big_ref = take(2)
    h_refs, g_refs = take(6), take(6)
    r1_ref, pooled_ref, split_ref, theta_ref, gtheta_ref, gknot_ref = take(6)
    pw_ref, pwt_ref, turned_ref, even_ref, odd_ref, bias_ref = take(6)
    horizon_rows, horizon_buf, coarse_bias_buf, fine_bias_buf, sems = take(5)
    if groups:
        shards = take(14)
        shard_sems, send, recv, partner_recv = take(4)
        head_bias_ref, bias_in, bias_far, stage_ref, ready, reduce_send, reduce_recv, bias_send, bias_recv = take(9)
        keep_sems = take(1)[0]
    else:
        head_bias_ref = bias_out
    hid, windows = p.hidden, p.windows
    section = lax.axis_index("section")
    chunk = min(512, windows // 2)
    chunks = windows // chunk
    H = slice(0, hid)
    lanes_of = lambda n: aligned(n * chunk, chunk, chunk)
    place = p.at["fine_entry"]
    head_at = p.at["fine_head"]

    load = lambda source, out, sem: pltpu.make_async_copy(source, out, sems.at[sem])
    history_in = load(history_ref, big_ref.at[: p.length], 1)
    cotangent_in = load(cotangent_ref, big_ref.at[: p.length], 2)
    target_in = load(target_ref, big_ref.at[p.length : p.fine_out], 0)
    rows_in = [
        load(horizon_ref, horizon_rows, 3),
        load(coarse_bias_ref, coarse_bias_buf, 4),
        load(fine_bias_ref, fine_bias_buf, 5),
    ]
    theta_copy = load(theta_ref, theta_out, 6)
    h3_copy = load(h_refs[5].at[H], h3_out, 7)
    gfine_copy = load(g_refs[3], gfine_out, 8)
    pool_copy = load(pooled_ref, pool_out, 9)

    if groups:
        shards_load = [
            pltpu.make_async_copy(source, out, shard_sems.at[n]) for n, (source, out) in enumerate(zip(shards_in, shards))
        ]
        order = [0, 1, 2, 3, 8, 9, 10, 11, 12, 13, 4, 5, 6, 7]
        for n in order:
            shards_load[n].start()
        way = Ways(groups)
        middle = p.at["fine_middle"]
        third = (p.columns - middle) // 3 // LANES * LANES
        entry_cut = place + up((middle - place) // 2, LANES)
        cuts = (0, p.at["coarse_middle"], place, entry_cut, middle, middle + third, middle + 2 * third, p.columns)
        gather = Gather(p, way, per, cuts, w_ref, shards[:8], shards[8:], send, recv, partner_recv)
        cotangent_in.start()
        for copy in rows_in:
            copy.start()
        barrier = pltpu.get_barrier_semaphore()
        signal(barrier, way.all())
        for n in order[:10]:
            shards_load[n].wait()
        pl.semaphore_wait(barrier, len(way.all()))
        gather.first(0)
        for n in order[10:]:
            shards_load[n].wait()
        for k in range(1, gather.ahead):
            gather.first(k)
    else:
        weights_in = load(packed_ref, w_ref, 10)
        weights_in.start()
        cotangent_in.start()
        for copy in rows_in:
            copy.start()

    def move(*steps):
        if groups:
            for stage, k in steps:
                {2: gather.second, 3: gather.third, 4: gather.fourth}[stage](k)
                if stage == 2 and k + gather.ahead < gather.chunks:
                    gather.first(k + gather.ahead)

    def complete(*ks):
        if groups:
            for k in ks:
                gather.complete(k)

    tail = p.wide_out - p.length
    mark = lax.broadcasted_iota(jnp.int32, (tail, windows), 0) < POOL
    big_ref[p.length :, :] = mark.astype(F32).astype(BF16)
    pooled_ref[...] = jnp.zeros_like(pooled_ref)
    for index in range(6):
        h_refs[index][hid:, :] = jnp.ones((ONES, windows), BF16)
    for copy in rows_in:
        copy.wait()
    for at in range(0, p.fine_out, LANES):
        part = slice(at, min(at + LANES, p.fine_out))
        row_out[:, part] = fine_bias_buf[part].reshape(1, part.stop - at)
    for n in range(windows // LANES):
        horizon_buf[:, n * LANES : (n + 1) * LANES] = horizon_rows[n : n + 1, :]
    step = 6 * LANES

    def adjoint(first, count, fore):
        hats = hat_weights(first, count, p, True, fore)

        @pl.loop(0, chunks)
        def _(n):
            lanes = lanes_of(n)
            rows = slice(first, first + count) if isinstance(first, int) else aligned(first, count, ONES)
            gtheta_ref[:, lanes] += dot(hats, big_ref[rows, lanes]) * (-1.0 / KNOT)

    cotangent_in.wait()
    gtheta_ref[...] = jnp.zeros_like(gtheta_ref)
    quarter = p.wide_in // 4
    pl.loop(0, 4)(lambda i: adjoint(i * quarter, quarter, False))
    history_in.start()
    move((2, 0), (2, 1), (3, 0))
    history_in.wait()

    unit = hid
    shape = (unit // POOL, unit)
    member = lax.broadcasted_iota(jnp.int32, shape, 1) - POOL * lax.broadcasted_iota(jnp.int32, shape, 0)
    turned_ref[: unit // POOL, :] = ((member >= 0) & (member < POOL)).astype(F32).astype(BF16)
    firsts = list(range(0, p.wide_in, unit))
    for number, first in enumerate(firsts):
        count = min(unit, p.wide_in - first)
        rows = slice(first // POOL, (first + count) // POOL)

        @pl.loop(0, chunks)
        def _(n):
            lanes = lanes_of(n)
            total = dot(turned_ref[: count // POOL, :count], big_ref[first : first + count, lanes])
            pooled_ref[rows, lanes] = (total * (1.0 / POOL)).astype(BF16)

        if number == len(firsts) // 2:
            move((4, 0))
    move((3, 1), (2, 2))
    complete(0)
    if not groups:
        weights_in.wait()
    fore_parts = [(0, 8 * p.pair), (8 * p.pair, p.horizon)]
    fore_bias = column_of(row_out, p.low, p.wide_out - p.low)
    placed = w_ref[:, p.at["bias"] : p.at["bias"] + LANES].astype(F32)
    lane = lax.broadcasted_iota(jnp.int32, (hid, LANES), 1)
    for number, (low, high) in enumerate(fore_parts):
        column = fore_bias[p.skip + low : p.skip + high]
        column = jnp.concatenate([column, jnp.zeros((hid - high + low, 1), F32)], axis=0)
        placed = jnp.where(lane == 6 + number, column, placed)
    bias_ref[...] = placed

    def pipeline(*layers):
        tile, pending = 0, nothing
        for before, produce, finish, after in layers:
            before()
            for n in range(chunks):
                lanes = slice(n * chunk, (n + 1) * chunk)
                out = (even_ref, odd_ref)[tile % 2]
                value = produce(lanes)
                out[: value.shape[0], :] = value
                pending()
                pending = functools.partial(finish, out, lanes)
                tile += 1
            after()
        pending()

    def nothing():
        pass

    def looped(*layers):
        for before, produce, finish, after in layers:
            before()

            @pl.loop(0, chunks)
            def _(n, produce=produce, finish=finish):
                value = produce(lanes_of(n))
                even_ref[: value.shape[0], :] = value
                finish(even_ref, lanes_of(n))

            after()

    def turn_weight(first, count):
        turned_ref[:count, :] = w_ref[:, first : first + count].T

    strip = ONES

    def activate(index):
        def finish(source, lanes):
            for r in range(0, hid, strip):
                rows = slice(r, r + strip)
                h, slope = gelu_both(source[rows, :] + bias_ref[rows, index : index + 1])
                h_refs[index][rows, lanes] = h.astype(BF16)
                g_refs[index][rows, lanes] = slope.astype(BF16)

        return finish

    def hidden(name, index, after=nothing):
        return (
            lambda: turn_weight(p.at[name], hid),
            lambda lanes: dot(turned_ref[H, :], h_refs[index - 1][H, lanes]),
            activate(index),
            after,
        )

    at_entry = p.at["coarse_entry"]
    at_head = p.at["coarse_head"]
    theta_bias = column_of(coarse_bias_buf, 0, p.theta_wide)

    def keep_theta(source, lanes):
        for r in range(0, p.theta_wide, strip):
            rows = slice(r, r + strip)
            theta = source[rows, :] + theta_bias[rows]
            if r < p.knot_rows:
                theta_ref[rows, lanes] = theta
            knots = jnp.where(lax.broadcasted_iota(jnp.int32, theta.shape, 0) + r < p.back, theta, 0.0)
            high = knots.astype(BF16)
            split_ref[rows, lanes] = high
            split_ref[p.theta_wide + r : p.theta_wide + r + strip, lanes] = (knots - high.astype(F32)).astype(BF16)

    def coarse_rest():
        move((4, 1), (3, 2), (2, 3))
        complete(1)

    forward = pipeline if groups else looped
    forward(
        (
            nothing,
            lambda lanes: dot(w_ref[:, at_entry : at_entry + p.pool_wide], pooled_ref[:, lanes]),
            activate(0),
            coarse_rest,
        ),
        hidden("coarse_middle", 1, lambda: move((4, 2), (2, 4))),
        hidden("coarse_upper", 2, lambda: move((3, 3))),
        (
            lambda: turn_weight(at_head, p.theta_wide),
            lambda lanes: dot(turned_ref[: p.theta_wide, :], h_refs[2][H, lanes]),
            keep_theta,
            nothing,
        ),
    )
    theta_copy.start()

    def keep(name, wide, sem):
        columns = slice(p.at[name], p.at[name] + wide)
        return load(w_ref.at[:, columns], kept_out.at[:, columns], sem)

    first_pair = p.start("fine_entry", section) // p.pair

    def interpolate(base, count, k, rest, later, lanes):
        own = theta_ref[pl.ds(base + jnp.minimum(k, count - 1), 1), lanes]
        after = theta_ref[pl.ds(base + jnp.minimum(k + 1, count - 1), 1), lanes]
        return own * rest + after * later

    everything = slice(0, windows)
    rest, later = fractions(windows)

    @pl.loop(0, p.r1_pairs)
    def _(i):
        pair = first_pair + i
        source = aligned(pair * p.pair, p.pair, ONES)
        made = jnp.concatenate(
            [interpolate(0, p.back, 2 * pair + j, rest, later, everything) for j in range(2)], axis=0
        )
        made = made * (pair < p.back // 2).astype(F32)
        r1_ref[aligned(i * p.pair, p.pair, ONES), :] = (big_ref[source, :].astype(F32) - made).astype(BF16)

    move((4, 3), (2, 5), (3, 4))
    complete(2, 3)
    kept = []
    if groups:
        kept.append(keep("fine_entry", p.wide_in, 10))
        kept[0].start()

    total = jnp.zeros((hid, p.theta_wide), F32)
    for first in range(0, p.wide_in, step):
        count = min(step, p.wide_in - first)
        total += dot(w_ref[:, place + first : place + first + count], hat_weights(first, count, p))
    product = (total * (1.0 / KNOT)).astype(BF16)
    pwt_ref[...] = product
    pw_ref[...] = product.T
    move((4, 4), (2, 6), (3, 5))

    def fine_entry(lanes):
        a = dot(w_ref[:, place : place + p.wide_in], big_ref[: p.wide_in, lanes])
        for part in (0, p.theta_wide):
            a -= dot(pwt_ref[...], split_ref[part : part + p.theta_wide, lanes])
        return a

    def entry_made():
        cotangent_in.start()
        target_in.start()
        big_ref[p.fine_out :, :] = jnp.zeros((p.wide_out - p.fine_out, windows), BF16)
        if groups:
            signal(ready.at[0], way.all())
        move((4, 5), (3, 6))
        complete(4)

    rest_c, later_c = fractions(chunk)

    def fore(number):
        low, high = fore_parts[number]

        def before():
            first = head_at + p.low + low
            turned = w_ref[:, first : first + up(high - low + p.skip, LANES)].T
            turned_ref[: high - low, :] = turned[p.skip : p.skip + high - low]

        def finish(source, lanes):
            for k in range(low // KNOT, high // KNOT, 2):
                here = slice(k * KNOT - low, (k + 2) * KNOT - low)
                second = source[here, :] + bias_ref[here, 6 + number : 7 + number]
                first = jnp.concatenate(
                    [interpolate(p.back, p.fore, k + j, rest_c, later_c, lanes) for j in range(2)], axis=0
                )
                counts = (lax.broadcasted_iota(jnp.int32, (2 * KNOT, chunk), 0) + k * KNOT) < horizon_buf[:, lanes]
                there = slice(p.length + k * KNOT, p.length + (k + 2) * KNOT)
                error = first + second - big_ref[there, lanes].astype(F32)
                big_ref[there, lanes] = jnp.where(counts, -error, 0.0).astype(BF16)

        return before, lambda lanes: dot(turned_ref[: high - low, :], h_refs[5][H, lanes]), finish, nothing

    looped((nothing, fine_entry, activate(3), entry_made))
    forward(hidden("fine_middle", 4, lambda: move((4, 6))), hidden("fine_upper", 5))
    h3_copy.start()
    cotangent_in.wait()
    target_in.wait()

    def gradient_slice(name, left, right_ref, first, step=LANES, sign=1.0):
        left_ref = left if name.endswith("entry") else h_refs[left]

        def part(b):
            value = sign * dot_rows(left_ref[...], right_ref[aligned(first + b * step, step, ONES), :])
            w_ref[:, aligned(place + p.slice_at[name] + b * step, step, LANES)] = value[:hid].astype(BF16)
            if name in p.bias_at:
                for c in range(step // LANES):
                    row = p.bias_at[name] + b * (step // LANES) + c
                    head_bias_ref[pl.ds(row, 1), :] = value[hid : hid + 1, c * LANES : (c + 1) * LANES]

        count = p.rows(name) // step
        if count > 1:
            pl.loop(0, count)(part)
        else:
            part(0)

    def square_slice(name, index):
        gradient_slice(name, index - 1, g_refs[index], p.start(name, section))

    def back(index, product, after=nothing):
        def finish(source, lanes):
            for r in range(0, hid, strip):
                rows = slice(r, r + strip)
                g_refs[index][rows, lanes] = (source[rows, :] * g_refs[index][rows, lanes].astype(F32)).astype(BF16)

        return nothing, product, finish, after

    def times(name, index):
        at = p.at[name]
        return lambda lanes: dot(w_ref[:, at : at + hid], g_refs[index][:, lanes])

    if groups:
        cuts = (0, p.slice_at["head_fore"], p.slice_at["fine_entry"])
        cuts += (p.slice_at["coarse_head"], p.slice_at["coarse_middle"], p.slice_columns)
        width = lambda k: cuts[k + 1] - cuts[k]

        def arrivals(row, k):
            rows = slice(row * per, (row + 1) * per) if isinstance(row, int) else aligned(row * per, per, per)
            if k == 0:
                return split_ref.at[rows, : width(0)]
            first = head_at + cuts[k] - cuts[1]
            return w_ref.at[rows, first : first + width(k)]

        def departures(j, k):
            if k == 0:
                return gknot_ref.at[j * per : (j + 1) * per, : width(0)]
            first = (k * groups + j) * per
            return big_ref.at[first : first + per, : width(k)]

        reduce = Reduce(
            p,
            way,
            per,
            cuts,
            lambda owner, k: w_ref.at[aligned(owner * per, per, per), place + cuts[k] : place + cuts[k + 1]],
            arrivals,
            lambda j, k: arrivals(groups + j, k),
            departures,
            stage_ref,
            slices_out,
            reduce_send,
            reduce_recv,
            keep_sems,
        )
        reduce_bias = ReduceBias(way, head_bias_ref, bias_in, bias_far, bias_out, bias_send, bias_recv)
        kept[0].wait()
        gather.sent(2)
        gather.sent(3)

    gradient_slice("head_back", 5, big_ref, p.start("head_back", section), 2 * LANES, -1.0)
    if groups:
        pl.semaphore_wait(ready.at[0], len(way.all()))
        reduce.first(0)
    complete(5, 6)
    looped(fore(0), fore(1))
    if groups:
        kept.append(keep("fine_head", p.wide_out, 11))
        kept[1].start()
        reduce.second(0)

    adjoint(p.low, p.wide_out - p.low, True)
    looped(back(5, lambda lanes: -dot(w_ref[:, head_at : head_at + p.wide_out], big_ref[:, lanes])))
    if groups:
        kept[1].wait()
        for k in (0, 1, 4, 5, 6):
            gather.sent(k)
        signal(ready.at[1], way.all())
    looped(back(4, times("fine_upper", 5)))
    gradient_slice("head_fore", 5, big_ref, p.start("head_fore", section) + p.low, LANES, -1.0)
    square_slice("fine_upper", 5)
    square_slice("fine_middle", 4)
    if groups:
        pl.semaphore_wait(ready.at[1], len(way.all()))
        reduce.first(1)
    looped(back(3, times("fine_middle", 4)))
    gfine_copy.start()
    gradient_slice("fine_entry", g_refs[3], r1_ref, p.start("fine_entry", section) - first_pair * p.pair, 2 * LANES)
    if groups:
        reduce.first(2)
        reduce.second(1)
        reduce.third(0)
        reduce.sent_far(0)
    gknot_ref[p.knot_rows :, :] = jnp.zeros((p.theta_wide - p.knot_rows, windows), BF16)

    def knots_done(source, lanes):
        for r in range(0, p.knot_rows, strip):
            rows = slice(r, r + strip)
            gknot_ref[rows, lanes] = (gtheta_ref[rows, lanes] - source[rows, :]).astype(BF16)

    looped(
        (nothing, lambda lanes: dot(pw_ref[: p.knot_rows, :], g_refs[3][:, lanes]), knots_done, nothing),
        back(2, lambda lanes: dot(w_ref[:, at_head : at_head + p.theta_wide], gknot_ref[:, lanes])),
    )
    gradient_slice("coarse_head", 2, gknot_ref, p.start("coarse_head", section))
    square_slice("coarse_upper", 2)
    if groups:
        reduce.first(3)
        reduce.second(2)
    looped(back(1, times("coarse_upper", 2)))
    if groups:
        reduce.third(1)
        reduce.second(3)
    square_slice("coarse_middle", 1)
    looped(back(0, times("coarse_middle", 1)))
    gradient_slice("coarse_entry", g_refs[0], pooled_ref, p.start("coarse_entry", section))
    if groups:
        reduce.first(4)
        reduce_bias.to_partner().start()
        reduce.second(4)
        reduce_bias.second()

    def pool_gradient(source, lanes):
        for r in range(0, p.pool_wide, strip):
            pooled_ref[r : r + strip, lanes] = (source[r : r + strip, :] * (1.0 / POOL)).astype(BF16)

    looped(
        (
            lambda: turn_weight(at_entry, p.pool_wide),
            lambda lanes: dot(turned_ref[: p.pool_wide, :], g_refs[0][:, lanes]),
            pool_gradient,
            nothing,
        )
    )
    pool_copy.start()
    if groups:
        reduce.third(2)
        reduce_bias.third()
        reduce.third(3)
        reduce.third(4)
        for k in range(reduce.chunks):
            reduce.complete(k)
            reduce.sent(k)
            if k > 0:
                reduce.sent_far(k)
        reduce_bias.complete()
    else:
        out = load(w_ref.at[:, place : place + p.slice_columns], slice_out, 10)
        out.start()
        out.wait()
    theta_copy.wait()
    h3_copy.wait()
    gfine_copy.wait()
    pool_copy.wait()


ANY = pl.BlockSpec(memory_space=pl.ANY)
VMEM = pl.BlockSpec(memory_space=pltpu.VMEM)


def core(plan, per, groups, history, cotangent, targets, horizon, coarse_bias, fine_bias, weights):
    p = plan
    hid, windows = p.hidden, p.windows
    flops = 2 * windows * hid * (2 * p.length + 2 * p.wide_out // 3 + 12 * hid + p.slice_columns)
    out_shape = [
        jax.ShapeDtypeStruct((p.knot_rows, windows), F32),
        jax.ShapeDtypeStruct((hid, windows), BF16),
        jax.ShapeDtypeStruct((hid, windows), BF16),
        jax.ShapeDtypeStruct((p.pool_wide, windows), BF16),
        jax.ShapeDtypeStruct((1, p.fine_out), F32),
    ]
    out_specs = [ANY] * 4 + [VMEM]
    scratch = [
        pltpu.VMEM((hid, p.columns), BF16),
        pltpu.VMEM((p.wide_out, windows), BF16),
        *[pltpu.VMEM((hid + ONES, windows), BF16)] * 6,
        *[pltpu.VMEM((hid, windows), BF16)] * 6,
        pltpu.VMEM((p.r1_pairs * p.pair, windows), BF16),
        pltpu.VMEM((p.pool_wide, windows), BF16),
        pltpu.VMEM((2 * p.theta_wide, windows), BF16),
        pltpu.VMEM((p.knot_rows, windows), F32),
        pltpu.VMEM((p.knot_rows, windows), F32),
        pltpu.VMEM((p.theta_wide, windows), BF16),
        pltpu.VMEM((p.theta_wide, hid), BF16),
        pltpu.VMEM((hid, p.theta_wide), BF16),
        pltpu.VMEM((hid, hid), BF16),
        pltpu.VMEM((hid, min(512, windows // 2)), F32),
        pltpu.VMEM((hid, min(512, windows // 2)), F32),
        pltpu.VMEM((hid, LANES), F32),
        pltpu.VMEM(horizon.shape, jnp.int32),
        pltpu.VMEM((1, windows), jnp.int32),
        pltpu.VMEM(coarse_bias.shape, F32),
        pltpu.VMEM(fine_bias.shape, F32),
        pltpu.SemaphoreType.DMA((13,)),
    ]
    params = {}
    if groups:
        bias = (p.bias_rows, LANES)
        out_shape += [
            jax.ShapeDtypeStruct((hid, p.columns), BF16),
            jax.ShapeDtypeStruct((4, per, p.slice_columns), BF16),
            jax.ShapeDtypeStruct((4,) + bias, F32),
        ]
        out_specs += [ANY, ANY, VMEM]
        chunks, reduce_chunks = 7, 5
        scratch += [pltpu.VMEM(piece.shape, F32) for piece in weights]
        scratch += [
            pltpu.SemaphoreType.DMA((len(weights),)),
            pltpu.SemaphoreType.DMA((chunks, groups - 1, 6)),
            pltpu.SemaphoreType.DMA((chunks, groups - 1, 4)),
            pltpu.SemaphoreType.DMA((chunks, groups)),
            pltpu.VMEM(bias, F32),
            pltpu.VMEM(bias, F32),
            pltpu.VMEM((groups,) + bias, F32),
            pltpu.VMEM((per, p.slice_columns), BF16),
            pltpu.SemaphoreType.REGULAR((2,)),
            pltpu.SemaphoreType.DMA((reduce_chunks, max(groups, 3), 3)),
            pltpu.SemaphoreType.DMA((reduce_chunks, max(groups, 3), 3)),
            pltpu.SemaphoreType.DMA((groups + 3,)),
            pltpu.SemaphoreType.DMA((groups + 3,)),
            pltpu.SemaphoreType.DMA((reduce_chunks,)),
        ]
        params = {"collective_id": 0, "has_side_effects": True}
    else:
        out_shape += [jax.ShapeDtypeStruct((hid, p.slice_columns), BF16), jax.ShapeDtypeStruct((p.bias_rows, LANES), F32)]
        out_specs += [ANY, VMEM]
    return pl.pallas_call(
        functools.partial(core_kernel, p, per, groups),
        out_shape=tuple(out_shape),
        in_specs=[ANY] * (6 + len(weights)),
        out_specs=tuple(out_specs),
        scratch_shapes=scratch,
        compiler_params=pltpu.CompilerParams(vmem_limit_bytes=63 * MIB, **params),
        cost_estimate=pl.CostEstimate(flops=flops, bytes_accessed=windows * p.length * 4, transcendentals=0),
    )(history, cotangent, targets, horizon, coarse_bias, fine_bias, *weights)


def outputs_kernel(
    plan,
    block,
    steps,
    packed_ref,
    history_ref,
    cotangent_ref,
    theta_ref,
    h3_ref,
    gfine_ref,
    pool_ref,
    fine_bias_ref,
    slices_ref,
    bias_rows_ref,
    residual_ref,
    history_grad_ref,
    prediction_ref,
    *refs,
):
    grads = refs[:16]
    head_ref, entry_ref, side_ref, pool_in, slices_in, pool_grad, fore_ref, *products, turned_head, turned_entry, bias_ref, sems = refs[16:]
    back_refs, fine_refs = products[:2], products[2:]
    p = plan
    step = pl.program_id(0)
    windows = p.windows
    chunk = min(512, windows)
    chunks = windows // chunk
    lanes_of = lambda n: slice(n * chunk, (n + 1) * chunk) if isinstance(n, int) else aligned(n * chunk, chunk, chunk)
    knots = block // KNOT
    pooled = block // POOL
    rest, later = fractions(chunk)

    def fetch(name, out, at, slot, sem):
        first = aligned(p.at[name] + at * block, block, LANES)
        return pltpu.make_async_copy(packed_ref.at[:, first], out.at[slot], sems.at[sem, slot])

    def interpolate(k, count, base, lanes):
        low = jnp.minimum if not isinstance(k, int) else min
        own = theta_ref[pl.ds(base + low(k, count - 1), 1), lanes]
        after = theta_ref[pl.ds(base + low(k + 1, count - 1), 1), lanes]
        return own * rest + after * later

    fore_out = pltpu.make_async_copy(fore_ref, prediction_ref, sems.at[3, 0])
    wide = p.wide_out - p.low
    first_fore = p.at["fine_head"] + p.low
    side = pltpu.make_async_copy(packed_ref.at[:, first_fore : first_fore + wide], side_ref, sems.at[2, 0])
    pool_copy = pltpu.make_async_copy(pool_ref, pool_in, sems.at[2, 1])
    slices_copy = pltpu.make_async_copy(slices_ref, slices_in, sems.at[3, 1])

    @pl.when(step == 0)
    def _():
        fetch("fine_head", head_ref, 0, 0, 0).start()
        fetch("fine_entry", entry_ref, 0, 0, 1).start()
        pool_copy.start()
        side.start()
        slices_copy.start()

    @pl.when(step == 2)
    def _():
        side.wait()
        turned_fore = side_ref[...].T
        fore_bias = column_of(fine_bias_ref, p.low, wide)

        @pl.loop(0, chunks)
        def _(n):
            lanes = lanes_of(n)
            for part in range(0, p.horizon, block):
                size = min(block, p.horizon - part)
                back_refs[part // block][:size, :] = dot(turned_fore[p.skip + part : p.skip + part + size], h3_ref[:, lanes])
            for k in range(0, p.fore, 2):
                rows = slice(k * KNOT, (k + 2) * KNOT)
                here = slice(k * KNOT % block, k * KNOT % block + 2 * KNOT)
                second = back_refs[k * KNOT // block][here, :] + fore_bias[p.skip + k * KNOT : p.skip + (k + 2) * KNOT]
                first = jnp.concatenate([interpolate(k + j, p.fore, p.back, lanes) for j in range(2)], axis=0)
                fore_ref[rows, lanes] = first.astype(BF16).astype(F32) + second.astype(BF16).astype(F32)

        fore_out.start()

    @pl.when(step == 1)
    def _():
        slices_copy.wait()
        unpack(p, slices_in, bias_rows_ref, grads)

    slot = step % 2

    @pl.when(step + 1 < steps)
    def _():
        fetch("fine_head", head_ref, step + 1, 1 - slot, 0).start()
        fetch("fine_entry", entry_ref, step + 1, 1 - slot, 1).start()

    fetch("fine_head", head_ref, step, slot, 0).wait()
    fetch("fine_entry", entry_ref, step, slot, 1).wait()
    turned_head[...] = head_ref[slot].T
    turned_entry[...] = entry_ref[slot].T

    @pl.when(step == 0)
    def _():
        pool_copy.wait()
        pool_grad[...] = pool_in[...].astype(F32)

    row = jnp.broadcast_to(fine_bias_ref[:, aligned(step * block, block, LANES)], (8, block))
    bias_ref[...] = row.T[:, :1]
    pair = 2 * KNOT

    def make(n, place):
        lanes = lanes_of(n)
        back_refs[place][...] = dot(turned_head[...], h3_ref[:, lanes])
        fine_refs[place][...] = dot(turned_entry[...], gfine_ref[:, lanes])

    def finish(n, place):
        lanes = lanes_of(n)
        for at in range(0, block, pair):
            rows = slice(at, at + pair)
            k = step * knots + at // KNOT
            made = jnp.concatenate([interpolate(k + j, p.back, 0, lanes) for j in range(2)], axis=0)
            back = back_refs[place][rows, :] + bias_ref[rows, :]
            residual_ref[rows, lanes] = (history_ref[rows, lanes].astype(F32) - made - back).astype(BF16)
            first = step * pooled + at // POOL
            spread = jnp.concatenate(
                [jnp.broadcast_to(pool_grad[pl.ds(first + j, 1), lanes], (POOL, chunk)) for j in range(pair // POOL)],
                axis=0,
            )
            fine = fine_refs[place][rows, :] + spread
            history_grad_ref[rows, lanes] = (cotangent_ref[rows, lanes].astype(F32) + fine).astype(BF16)

    for n in range(chunks + 1):
        if n < chunks:
            make(n, n % 2)
        if n > 0:
            finish(n - 1, (n - 1) % 2)

    @pl.when(step == steps - 1)
    def _():
        fore_out.wait()


def outputs(plan, packed, history, cotangent, theta, h3, gfine, pool, fine_bias, slices, bias_rows):
    p = plan
    hid, windows = p.hidden, p.windows
    block = 6 * LANES
    steps = -(-p.length // block)
    rows = pl.BlockSpec((block, windows), lambda i: (i, 0))
    wide = p.wide_out - p.low
    per = slices.shape[1]
    square, vector = (per, hid), (1, per)
    grads = []
    for entry, out in ((p.pooled, p.coarse_out), (p.length, p.fine_out)):
        grads += [(per, entry), vector, square, vector, square, vector, (per, out), (1, out)]
    grads[-1] = (p.fine_out,)
    return pl.pallas_call(
        functools.partial(outputs_kernel, p, block, steps),
        grid=(steps,),
        out_shape=(
            jax.ShapeDtypeStruct((p.length, windows), BF16),
            jax.ShapeDtypeStruct((p.length, windows), BF16),
            jax.ShapeDtypeStruct((p.horizon, windows), F32),
        )
        + tuple(jax.ShapeDtypeStruct(shape, F32) for shape in grads),
        in_specs=[ANY, rows, rows, VMEM, VMEM, VMEM, ANY, VMEM, ANY, VMEM],
        out_specs=(rows, rows, ANY) + (VMEM,) * len(grads),
        scratch_shapes=[
            pltpu.VMEM((2, hid, block), BF16),
            pltpu.VMEM((2, hid, block), BF16),
            pltpu.VMEM((hid, wide), BF16),
            pltpu.VMEM(pool.shape, BF16),
            pltpu.VMEM(slices.shape, slices.dtype),
            pltpu.VMEM((p.pool_wide, windows), F32),
            pltpu.VMEM((p.horizon, windows), F32),
            *[pltpu.VMEM((block, min(512, windows)), F32)] * 4,
            pltpu.VMEM((block, hid), BF16),
            pltpu.VMEM((block, hid), BF16),
            pltpu.VMEM((block, 1), F32),
            pltpu.SemaphoreType.DMA((4, 2)),
        ],
        compiler_params=pltpu.CompilerParams(vmem_limit_bytes=56 * MIB),
        cost_estimate=pl.CostEstimate(
            flops=2 * windows * hid * (2 * p.length + p.horizon), bytes_accessed=windows * p.length * 8, transcendentals=0
        ),
    )(packed, history, cotangent, theta, h3, gfine, pool, fine_bias, slices, bias_rows)


def pack(plan, arrays, biases):
    p = plan
    names = sorted(p.at, key=p.at.get)
    ends = [p.at[name] for name in names[1:]] + [p.columns]
    columns = []
    for name, end in zip(names, ends):
        piece = arrays[name] if name != "bias" else biases
        columns.append(jnp.pad(piece.astype(BF16), ((0, 0), (0, end - p.at[name] - piece.shape[1]))))
    return jnp.concatenate(columns, axis=1)


def unpack(plan, slices_ref, bias_rows_ref, grads):
    p = plan
    hid = p.hidden

    def joined(name, out, source, row=None, base=0, low=0, high=None):
        high, done = out.shape[-1] if high is None else high, low
        for section in range(p.sections):
            first = base + p.start(name, section)
            last = min(first + p.rows(name), high)
            if row is not None:
                for at in range(max(done // LANES * LANES, first), last, LANES):
                    begin, end = max(at, done), min(at + LANES, last)
                    if begin < end:
                        here = source[section, pl.ds(row + (at - first) // LANES, 1), :]
                        here = here[:, begin - at : end - at]
                        if len(out.shape) == 1:
                            out[begin:end] = here.reshape(end - begin)
                        else:
                            out[:, begin:end] = here
            elif done < last:
                at = p.slice_at[name] + done - first
                out[:, done:last] = source[section, :, at : at + last - done].astype(F32)
            done = max(done, last)

    def ones_column(name, row):
        section = p.sections - 1
        at = p.slice_at[name] + row - p.start(name, section)
        block = slices_ref[section, :, at // LANES * LANES : at // LANES * LANES + LANES].astype(F32)
        return block.T[at % LANES : at % LANES + 1]

    def own_part(name, out):
        per = out.shape[1]
        width = min(per, LANES)
        share = p.part[name][0]
        for at in range(0, per, width):
            first = lax.axis_index("dp") * per + at
            block = first // LANES
            row = bias_rows_ref[block // share, pl.ds(p.bias_at[name] + block % share, 1), :]
            wide = jnp.broadcast_to(row, (8, LANES))
            out[:, at : at + width] = pltpu.roll(wide, (LANES - first % LANES) % LANES, 1)[:1, :width]

    for base, block in ((0, "coarse_"), (8, "fine_")):
        entry, head = block + "entry", block + "head"
        joined(entry, grads[base], slices_ref)
        grads[base + 1][...] = ones_column(entry, grads[base].shape[1])
        for i, name in enumerate((block + "middle", block + "upper")):
            joined(name, grads[base + 2 + 2 * i], slices_ref)
            own_part(name, grads[base + 3 + 2 * i])
        for number, source in ((6, slices_ref), (7, bias_rows_ref)):
            row = lambda name: p.bias_at[name] if number == 7 else None
            if base == 0:
                joined(head, grads[number], source, row(head))
            else:
                joined("head_back", grads[8 + number], source, row("head_back"), 0, 0, p.length)
                joined("head_fore", grads[8 + number], source, row("head_fore"), p.low, p.length, p.fine_out)


def body(mesh_shape, history, targets, horizon, cotangent, *params):
    (c_entry, c_entry_b, c_middle, c_middle_b, c_upper, c_upper_b, c_head, c_head_b) = params[:8]
    (f_entry, f_entry_b, f_middle, f_middle_b, f_upper, f_upper_b, f_head, f_head_b) = params[8:]
    sections = mesh_shape["section"]
    length, hidden = f_entry.shape[0], c_middle.shape[1]
    p = Plan(
        length, f_head.shape[1] - length, hidden, c_entry.shape[0], c_head.shape[1], sections, history.shape[0]
    )
    pieces = (c_entry.T, c_middle, c_upper, c_head, f_entry.T, f_middle, f_upper, f_head)
    bias_pieces = (c_entry_b, c_middle_b, c_upper_b, f_entry_b, f_middle_b, f_upper_b)
    dp_count, per = mesh_shape["dp"], c_middle.shape[0]
    rows = (history.T, cotangent.T)
    rest = (targets.T, horizon.reshape(-1, LANES), c_head_b[None, :], f_head_b)
    groups = dp_count // 2
    if sections == 4 and dp_count % 2 == 0 and per % 64 == 0 and groups > 1:
        theta, h3, gfine, pool, fine_bias, packed, slices, bias_rows = core(
            p, per, groups, *rows, *rest, pieces + tuple(b[None, :] for b in bias_pieces)
        )
    else:
        packed = pack(p, dict(zip(NAMES, pieces)), jnp.stack(bias_pieces, axis=1))
        packed = lax.all_gather(packed, "dp", axis=0, tiled=True)
        theta, h3, gfine, pool, fine_bias, part, head_bias = core(p, per, 0, *rows, *rest, (packed,))
        own = lax.psum_scatter(part.astype(F32), "dp", scatter_dimension=0, tiled=True)
        slices = lax.all_gather(own, "section", axis=0)
        bias_rows = lax.all_gather(lax.psum(head_bias, "dp"), "section", axis=0)
    residual, history_grad, prediction, *grads = outputs(
        p, packed, *rows, theta, h3, gfine, pool, fine_bias, slices, bias_rows
    )
    grads = [g.T if i in (0, 8) else g[0] if g.shape[0] == 1 else g for i, g in enumerate(grads)]
    return (prediction.T, residual.T, history_grad.T) + tuple(grads)


def solution(mesh):
    by_row, by_column, by_entry, copied = P("dp", None), P(None, "dp"), P("dp"), P()
    block = (by_column, by_entry, by_row, by_entry, by_row, by_entry, by_row, copied)
    in_specs = (by_row, by_row, by_entry, by_row) + block + block
    out_specs = (by_row, by_row, by_row) + block + block
    return jax.shard_map(
        functools.partial(body, dict(mesh.shape)), mesh=mesh, in_specs=in_specs, out_specs=out_specs, check_vma=False
    )
```
